32 devices in a mesh: stream: 2 (over core), dp: 16 (over z, y, x).
Axes of the slice: x: 2, y: 2, z: 4, core: 2. Of those that a mesh axis runs over, the one named last changes fastest.
Arguments:
- embedded: bfloat16 [2, 16384, 768], P('stream', 'dp'), may hold values from -6 to 6
- seq_cotangent: bfloat16 [2, 16384, 768], P('stream', 'dp'), may hold values from -6 to 6
- pair_ids: int32 [256], replicated, may hold values from 0 to 108
- w_qkv: bfloat16 [768, 2304], replicated, may hold values from -0.21875 to 0.21875
- b_qv: float32 [1536], replicated, may hold values from -3 to 3
- w_out: bfloat16 [768, 768], replicated, may hold values from -1.75 to 1.75
- b_out: float32 [768], replicated, may hold values from -1.75 to 1.75
- ln1_gain: float32 [768], replicated, may hold values from 0.5 to 1.5
- ln1_bias: float32 [768], replicated, may hold values from -1.75 to 1.75
- w_in: bfloat16 [768, 3072], replicated, may hold values from -0.21875 to 0.21875
- b_in: float32 [3072], replicated, may hold values from -3 to 3
- w_down: bfloat16 [3072, 768], replicated, may hold values from -0.109375 to 0.109375
- b_down: float32 [768], replicated, may hold values from -1.75 to 1.75
- ln2_gain: float32 [768], replicated, may hold values from 0.5 to 1.5
- ln2_bias: float32 [768], replicated, may hold values from -1.75 to 1.75
- w_pool: bfloat16 [768, 768], replicated, may hold values from -0.21875 to 0.21875
- b_pool: float32 [768], replicated, may hold values from -3 to 3
Outputs:
- encoded: bfloat16 [2, 16384, 768], P('stream', 'dp')
- input_grad: bfloat16 [2, 16384, 768], P('stream', 'dp')
- grad_w_qkv: float32 [768, 2304], replicated
- grad_b_qv: float32 [1536], replicated
- grad_w_out: float32 [768, 768], replicated
- grad_b_out: float32 [768], replicated
- grad_ln1_gain: float32 [768], replicated
- grad_ln1_bias: float32 [768], replicated
- grad_w_in: float32 [768, 3072], replicated
- grad_b_in: float32 [3072], replicated
- grad_w_down: float32 [3072, 768], replicated
- grad_b_down: float32 [768], replicated
- grad_ln2_gain: float32 [768], replicated
- grad_ln2_bias: float32 [768], replicated
- grad_w_pool: float32 [768, 768], replicated
- grad_b_pool: float32 [768], replicated
The draws below stay inside these ranges and needn't reach their ends.
All inputs are finite; a program needn't handle non-finite values.
Results may differ from the reference program's by a relative error of at most 0.029.
Values may be sent and summed in bfloat16 or wider, within the bound.
No kernel may reach another device: no remote copies, remote signals or barrier semaphores. Data moves between devices by JAX's collectives and lax.ppermute only.
A program may use at most 256 MiB of HBM per device.

```python
import math
from functools import partial
import jax
import jax.numpy as jnp
import numpy as np
from jax import lax

D = 768
HEADS = 12
HEAD_DIM = 64
FF = 3072
SEQ = 64
PAIRS = 109
SENT = 256
TOKENS = 16384


def plant(result, own_key, least, top_value):
    spot = [jax.random.randint(jax.random.fold_in(own_key, axis), (), 0, length) for axis, length in enumerate(result.shape)]
    longest = result.shape.index(max(result.shape))
    neighbour = spot[:longest] + [(spot[longest] + 1) % result.shape[longest]] + spot[longest + 1:]
    return result.at[tuple(spot)].set(least).at[tuple(neighbour)].set(top_value)


def levels(rng, extent, pieces, smallest, largest):
    gain, own = 1.0, jax.random.fold_in(rng, 6)
    for dim, blocks in pieces:
        steps = jnp.exp(jax.random.uniform(jax.random.fold_in(own, dim), (blocks,), jnp.float32, smallest / len(pieces), largest / len(pieces)))
        gain = gain * jnp.repeat(steps, extent[dim] // blocks).reshape([-1 if axis == dim else 1 for axis in range(len(extent))])
    return gain


def rank_bounds(count, skew):
    portions = [(1 << 20) // math.isqrt(rank ** skew) + 1 for rank in range(1, count + 1)]
    deviation = 1 + sum(portions) // (1 << 30)
    return np.cumsum(np.array([max(1, weight // deviation) for weight in portions]))


def skewed_ids(stream_key, extent, number_of, slope):
    listing = rank_bounds(number_of, slope)
    ticket = jax.random.randint(jax.random.fold_in(stream_key, 1), extent, 0, int(listing[number_of - 1]))
    rank = jnp.searchsorted(jnp.asarray(listing, jnp.int32), ticket, side="right")
    return jax.random.permutation(jax.random.fold_in(stream_key, 2), number_of)[rank].astype(jnp.int32)


def centred(key, extent, spread, limit, cuts=(), kind=jnp.bfloat16):
    result = jax.random.normal(key, extent, jnp.float32) * spread
    if len(cuts) > 0:
        result = levels(key, extent, cuts, -0.22, 0.18) * result
    return jnp.clip(result, min=-limit, max=limit).astype(kind)


def setup_inputs(seed: int = 0) -> dict:
    key_of = jax.random.split(jax.random.key(seed), 18)
    return {
        "embedded": centred(key_of[0], (2, TOKENS, D), 1.0, 6.0, ((0, 2), (1, 16))),
        "seq_cotangent": centred(key_of[1], (2, TOKENS, D), 1.0, 6.0, ((0, 2), (1, 16))),
        "pair_ids": plant(skewed_ids(key_of[2], (SENT,), PAIRS, 2), jax.random.fold_in(key_of[2], 3), 0, PAIRS - 1).astype(jnp.int32),
        "w_qkv": centred(key_of[3], (D, 3 * D), D ** -0.5, 0.21875),
        "b_qv": centred(key_of[4], (2 * D,), 0.5, 3.0, (), jnp.float32),
        "w_out": centred(key_of[5], (D, D), (D // SEQ) ** -0.5, 1.75),
        "b_out": centred(key_of[6], (D,), 0.3, 1.75, (), jnp.float32),
        "ln1_gain": jnp.clip(1.0 + 0.1 * jax.random.normal(key_of[7], (D,), jnp.float32), 0.5, 1.5),
        "ln1_bias": centred(key_of[8], (D,), 0.3, 1.75, (), jnp.float32),
        "w_in": centred(key_of[9], (D, FF), D ** -0.5, 0.21875),
        "b_in": centred(key_of[10], (FF,), 0.5, 3.0, (), jnp.float32),
        "w_down": centred(key_of[11], (FF, D), FF ** -0.5, 0.109375),
        "b_down": centred(key_of[12], (D,), 0.3, 1.75, (), jnp.float32),
        "ln2_gain": jnp.clip(1.0 + 0.1 * jax.random.normal(key_of[13], (D,), jnp.float32), 0.5, 1.5),
        "ln2_bias": centred(key_of[14], (D,), 0.3, 1.75, (), jnp.float32),
        "w_pool": centred(key_of[15], (D, D), D ** -0.5, 0.21875),
        "b_pool": centred(key_of[16], (D,), 0.5, 3.0, (), jnp.float32),
    }


epsilon = 1e-06
score_scale = 10.0
margin_shift = score_scale * 0.3

@jax.custom_vjp
def low(v):
    return lax.optimization_barrier(v.astype(jnp.bfloat16)).astype(jnp.float32)

@jax.custom_vjp
def low_back(v):
    return v

def low_keep(v):
    return (low(v), None)

def low_pass(kept, grad):
    return (grad,)

def back_keep(v):
    return (v, None)

def back_low(kept, grad):
    return (low(grad),)
low.defvjp(low_keep, low_pass)
low_back.defvjp(back_keep, back_low)

def matmul(inputs, matrix):
    return jnp.dot(inputs, matrix, precision=lax.Precision.HIGHEST, preferred_element_type=jnp.float32)

def layer_norm(hidden, gain_row, bias_row):
    center = hidden - lax.optimization_barrier(jnp.mean(hidden, axis=-1, keepdims=True))
    variance = lax.optimization_barrier(jnp.mean(center * center, axis=-1, keepdims=True))
    return center * lax.rsqrt(variance + epsilon) * gain_row + bias_row

def encode_group(params, sent_block):
    w_qkv, b_qv, w_out, b_out, ln1_gain, ln1_bias, w_in, b_in, w_down, b_down, ln2_gain, ln2_bias, w_pool, b_pool = params
    sent_count = sent_block.shape[0]
    head_scale = 1.0 / math.sqrt(HEAD_DIM)
    tokens = sent_block.reshape(sent_count * SEQ, D)
    qkv_bias = jnp.concatenate([b_qv[:D], jnp.zeros((D,), jnp.float32), b_qv[D:]])
    projected = low(low_back(matmul(tokens, w_qkv)) + qkv_bias)
    head_view = projected.reshape(sent_count, SEQ, 3, HEADS, HEAD_DIM)
    queries = head_view[:, :, 0]
    key_rows = head_view[:, :, 1]
    value_rows = head_view[:, :, 2]
    scores = low_back(jnp.einsum('slhd,smhd->shlm', queries, key_rows, precision=lax.Precision.HIGHEST) * head_scale)
    probs = jax.nn.softmax(scores, axis=-1)
    context = low_back(low(jnp.einsum('shlm,smhd->slhd', low(probs), value_rows, precision=lax.Precision.HIGHEST)))
    context = context.reshape(sent_count * SEQ, D)
    attn_out = low_back(matmul(context, w_out)) + b_out
    hidden = layer_norm(tokens + attn_out, ln1_gain, ln1_bias)
    gate_in = low_back(matmul(low(hidden), w_in)) + b_in
    activated = jax.nn.gelu(gate_in, approximate=False)
    ffn_out = low_back(matmul(low(activated), w_down)) + b_down
    block_out = layer_norm(hidden + ffn_out, ln2_gain, ln2_bias)
    first_rows = block_out.reshape(sent_count, SEQ, D)[:, 0]
    pooled = jnp.tanh(low_back(matmul(low(first_rows), w_pool)) + b_pool)
    normed = pooled * lax.rsqrt(lax.optimization_barrier(jnp.sum(pooled * pooled, axis=-1, keepdims=True)) + epsilon)
    return (block_out.reshape(sent_count, SEQ, D), low(normed))

def reference(embedded, seq_cotangent, pair_ids, w_qkv, b_qv, w_out, b_out, ln1_gain, ln1_bias, w_in, b_in, w_down, b_down, ln2_gain, ln2_bias, w_pool, b_pool):
    params = tuple((member.astype(jnp.float32) for member in (w_qkv, b_qv, w_out, b_out, ln1_gain, ln1_bias, w_in, b_in, w_down, b_down, ln2_gain, ln2_bias, w_pool, b_pool)))
    inputs = embedded.astype(jnp.float32)
    cotangent = seq_cotangent.astype(jnp.float32)
    same_pair = pair_ids[:, None] == pair_ids[None, :]
    diagonal = jnp.eye(SENT, dtype=jnp.float32)
    group_size = math.gcd(2 * SENT, max(1, 4096 // SEQ))

    def objective_of(source, weights):
        sentences = source.reshape(2 * SENT // group_size, group_size, SEQ, D)
        block_out, embeds = lax.map(jax.checkpoint(partial(encode_group, weights)), sentences)
        block_out = block_out.reshape(2, TOKENS, D)
        embeds = embeds.reshape(2, SENT, D)
        loss_sum = jnp.zeros((), jnp.float32)
        for half_index in range(2):
            cosine = low_back(matmul(embeds[half_index], embeds[1 - half_index].T))
            logits = score_scale * cosine - margin_shift * diagonal
            masked = jnp.where(same_pair, logits, -jnp.inf)
            loss_sum = loss_sum + jnp.sum(jax.nn.logsumexp(masked, axis=-1) - lax.optimization_barrier(jnp.sum(logits * diagonal, axis=-1)))
        return (loss_sum + jnp.sum(block_out * cotangent), block_out)
    objective, pullback, block_out = jax.vjp(objective_of, inputs, params, has_aux=True)
    input_grad, param_grads = pullback(jnp.ones((), jnp.float32))
    return (block_out.astype(jnp.bfloat16), input_grad.astype(jnp.bfloat16), param_grads[0], param_grads[1], param_grads[2], param_grads[3], param_grads[4], param_grads[5], param_grads[6], param_grads[7], param_grads[8], param_grads[9], param_grads[10], param_grads[11], param_grads[12], param_grads[13])
```

```python
import functools
import math

import jax
import jax.numpy as jnp
from jax import lax
from jax.experimental import pallas as pl
from jax.experimental.pallas import tpu as pltpu
from jax.sharding import PartitionSpec as P

HEADS = 12
HEAD_DIM = 64
SEQ = 64
GROUP = 16

epsilon = 1e-06
score_scale = 10.0
margin_shift = score_scale * 0.3
root_half = 0.7071067811865476
gauss_norm = 0.3989422804014327

low = jnp.bfloat16
wide = jnp.float32


def struct(shape, dtype):
    return jax.ShapeDtypeStruct(shape, dtype)


def whole(shape):
    return pl.BlockSpec(shape, lambda *_: (0,) * len(shape))


def call(body, grid, in_specs, out_specs, out_shape, flops=0, scratch=(), aliases=None, limit=48):
    return pl.pallas_call(
        body,
        grid=grid,
        in_specs=in_specs,
        out_specs=out_specs,
        out_shape=out_shape,
        scratch_shapes=list(scratch),
        input_output_aliases=aliases or {},
        cost_estimate=pl.CostEstimate(flops=int(flops), bytes_accessed=int(flops / 400), transcendentals=0),
        compiler_params=pltpu.CompilerParams(vmem_limit_bytes=limit << 20),
    )


def mat_mul(a, b):
    return jnp.dot(a, b, preferred_element_type=wide)


def trans_left(a, b):
    return lax.dot_general(a, b, (((0,), (0,)), ((), ())), preferred_element_type=wide)


def trans_right(a, b):
    return lax.dot_general(a, b, (((1,), (1,)), ((), ())), preferred_element_type=wide)


def normalize(h):
    center = h - jnp.mean(h, axis=-1, keepdims=True)
    inv = lax.rsqrt(jnp.mean(center * center, axis=-1, keepdims=True) + epsilon)
    return center * inv, inv


def norm_input_grad(grad, normed, inv):
    return inv * (
        grad
        - jnp.mean(grad, axis=-1, keepdims=True)
        - normed * jnp.mean(grad * normed, axis=-1, keepdims=True)
    )


def split_heads(pair, first):
    zero = jnp.zeros_like(pair)
    return jnp.concatenate([jnp.where(first, pair, zero), jnp.where(first, zero, pair)], axis=0)


def join_heads(rows, first):
    return jnp.where(first, rows[:SEQ], rows[SEQ:])


def attention_forward(x, w_qkv, qkv_bias, w_out, b_out, gain, bias):
    tokens, width = x.shape
    rows = 4 * SEQ
    pairs = width // (2 * HEAD_DIM)
    scale = 1.0 / math.sqrt(HEAD_DIM)

    def body(x_ref, wq_ref, bq_ref, wo_ref, bo_ref, g_ref, b_ref, proj_ref, prob_ref, ctx_ref, hid_ref, low_ref, inv_ref):
        x_in = x_ref[...]
        for part in range(3):
            cols = slice(part * width, (part + 1) * width)
            proj_ref[:, cols] = (mat_mul(x_in, wq_ref[:, cols]) + bq_ref[:, cols]).astype(low)
        first = lax.broadcasted_iota(jnp.int32, (SEQ, 128), 1) < HEAD_DIM
        for sent in range(4):
            r = slice(sent * SEQ, (sent + 1) * SEQ)
            for pair in range(pairs):
                c = pair * 128
                q = proj_ref[r, c : c + 128]
                k = proj_ref[r, width + c : width + c + 128]
                v = proj_ref[r, 2 * width + c : 2 * width + c + 128]
                scores = trans_right(k, split_heads(q, first)) * scale
                e = jnp.exp(scores - jnp.max(scores, axis=0, keepdims=True))
                probs = (e * (1.0 / jnp.sum(e, axis=0, keepdims=True))).astype(low)
                prob_ref[sent, pair] = probs
                ctx_ref[r, c : c + 128] = join_heads(trans_left(probs, v), first).astype(low)
        h = x_in.astype(wide) + mat_mul(ctx_ref[...], wo_ref[...]) + bo_ref[...]
        normed, inv = normalize(h)
        hidden = normed * g_ref[...] + b_ref[...]
        hid_ref[...] = hidden
        low_ref[...] = hidden.astype(low)
        inv_ref[...] = inv

    row = lambda cols: pl.BlockSpec((rows, cols), lambda i: (i, 0))
    prob_shape = (tokens // SEQ, pairs, SEQ, 128)
    return call(
        body,
        (tokens // rows,),
        [row(width), whole(w_qkv.shape), whole(qkv_bias.shape), whole(w_out.shape)] + [whole((1, width))] * 3,
        [row(3 * width), pl.BlockSpec((4,) + prob_shape[1:], lambda i: (i, 0, 0, 0)), row(width), row(width), row(width), row(1)],
        [
            struct((tokens, 3 * width), low),
            struct(prob_shape, low),
            struct((tokens, width), low),
            struct((tokens, width), wide),
            struct((tokens, width), low),
            struct((tokens, 1), wide),
        ],
        flops=2 * tokens * width * (4 * width + 4 * SEQ),
    )(x, w_qkv, qkv_bias, w_out, b_out, gain, bias)


CHUNK = 512


def ffn_forward_rows(hidden, wi_ref, bi_ref, wd_ref, bd_ref, store_act, store_slope):
    h_low = hidden.astype(low)
    ffn = wi_ref.shape[1]
    total = hidden + bd_ref[...]
    for c in range(0, ffn, CHUNK):
        u = mat_mul(h_low, wi_ref[:, c : c + CHUNK]) + bi_ref[:, c : c + CHUNK]
        phi = 0.5 + 0.5 * lax.erf(u * root_half)
        act = (u * phi).astype(low)
        store_act(c, act)
        store_slope(c, (phi + u * jnp.exp(-0.5 * u * u) * gauss_norm).astype(low))
        total = total + mat_mul(act, wd_ref[c : c + CHUNK, :])
    return normalize(total)


def ffn_backward_rows(grad_block, normed, inv, gain_ref, wd_ref, slope_of, store_gate, small_ref, bin_ref):
    grad_two = norm_input_grad(grad_block * gain_ref[...], normed, inv)
    small_ref[0:1, :] += jnp.sum(grad_block * normed, axis=0, keepdims=True)
    small_ref[1:2, :] += jnp.sum(grad_block, axis=0, keepdims=True)
    small_ref[2:3, :] += jnp.sum(grad_two, axis=0, keepdims=True)
    grad_low = grad_two.astype(low)
    for c in range(0, wd_ref.shape[0], CHUNK):
        gate = trans_right(grad_low, wd_ref[c : c + CHUNK, :]) * slope_of(c).astype(wide)
        bin_ref[:, c : c + CHUNK] += jnp.sum(gate, axis=0, keepdims=True)
        store_gate(c, gate.astype(low))
    return grad_low


def group_spec(sents, cols, index):
    return pl.BlockSpec((sents, GROUP, cols), lambda i: (0, index(i), 0))


def ffn_first(hidden, w_in, b_in, w_down, b_down, gain, bias):
    sents, _, width = hidden.shape
    ffn = w_in.shape[1]
    rows = sents * GROUP

    def body(h_ref, wi_ref, bi_ref, wd_ref, bd_ref, g_ref, b_ref, enc_ref, act_ref, slope_ref, n_ref, inv_ref, first_ref):
        def store_act(c, v):
            act_ref[:, :, c : c + CHUNK] = v.reshape(sents, GROUP, CHUNK)

        def store_slope(c, v):
            slope_ref[:, c : c + CHUNK] = v

        normed, inv = ffn_forward_rows(h_ref[...].reshape(rows, width), wi_ref, bi_ref, wd_ref, bd_ref, store_act, store_slope)
        n_ref[...] = normed
        inv_ref[...] = inv
        block = (normed * g_ref[...] + b_ref[...]).reshape(sents, GROUP, width)
        enc_ref[...] = block.astype(low)
        first_ref[...] = block[:, 0, :].astype(low)

    zero = lambda i: 0
    return call(
        body,
        (1,),
        [group_spec(sents, width, zero), whole(w_in.shape), whole((1, ffn)), whole(w_down.shape)] + [whole((1, width))] * 3,
        [
            group_spec(sents, width, zero),
            group_spec(sents, ffn, zero),
            whole((rows, ffn)),
            whole((rows, width)),
            whole((rows, 1)),
            whole((sents, width)),
        ],
        [
            struct((sents, SEQ, width), low),
            struct((sents, SEQ, ffn), low),
            struct((rows, ffn), low),
            struct((rows, width), wide),
            struct((rows, 1), wide),
            struct((sents, width), low),
        ],
        flops=4 * rows * width * ffn,
    )(hidden, w_in, b_in, w_down, b_down, gain, bias)


def ffn_rest(hidden, cot, w_in, b_in, w_down, b_down, gain, bias, encoded, act):
    sents, _, width = hidden.shape
    ffn = w_in.shape[1]
    rows = sents * GROUP
    groups = SEQ // GROUP

    def body(h_ref, cot_ref, wi_ref, bi_ref, wd_ref, bd_ref, g_ref, b_ref, _e, _a, enc_ref, act_ref, gate_ref, two_ref, small_ref, bin_ref, slope_ref):
        @pl.when(pl.program_id(0) == 0)
        def _():
            small_ref[...] = jnp.zeros_like(small_ref)
            bin_ref[...] = jnp.zeros_like(bin_ref)

        def store_act(c, v):
            act_ref[:, :, c : c + CHUNK] = v.reshape(sents, GROUP, CHUNK)

        def store_slope(c, v):
            slope_ref[:, c : c + CHUNK] = v

        def store_gate(c, v):
            gate_ref[:, :, c : c + CHUNK] = v.reshape(sents, GROUP, CHUNK)

        normed, inv = ffn_forward_rows(h_ref[...].reshape(rows, width), wi_ref, bi_ref, wd_ref, bd_ref, store_act, store_slope)
        enc_ref[...] = (normed * g_ref[...] + b_ref[...]).astype(low).reshape(sents, GROUP, width)
        grad_block = cot_ref[...].reshape(rows, width).astype(wide)
        two = ffn_backward_rows(
            grad_block, normed, inv, g_ref, wd_ref, lambda c: slope_ref[:, c : c + CHUNK], store_gate, small_ref, bin_ref
        )
        two_ref[...] = two.reshape(sents, GROUP, width)

    nxt = lambda i: i + 1
    anyspec = pl.BlockSpec(memory_space=pl.ANY)
    return call(
        body,
        (groups - 1,),
        [group_spec(sents, width, nxt)] * 2
        + [whole(w_in.shape), whole((1, ffn)), whole(w_down.shape)]
        + [whole((1, width))] * 3
        + [anyspec] * 2,
        [
            group_spec(sents, width, nxt),
            group_spec(sents, ffn, nxt),
            group_spec(sents, ffn, nxt),
            group_spec(sents, width, nxt),
            whole((8, width)),
            whole((1, ffn)),
        ],
        [
            struct((sents, SEQ, width), low),
            struct((sents, SEQ, ffn), low),
            struct((sents, SEQ, ffn), low),
            struct((sents, SEQ, width), low),
            struct((8, width), wide),
            struct((1, ffn), wide),
        ],
        flops=6 * (groups - 1) * rows * width * ffn,
        scratch=[pltpu.VMEM((rows, ffn), low)],
        aliases={8: 0, 9: 1},
    )(hidden, cot, w_in, b_in, w_down, b_down, gain, bias, encoded, act)


def ffn_first_back(cot, grad_first, normed, inv, slope, gain, w_down, gate, two, small, bin_sum):
    sents, _, width = cot.shape
    ffn = w_down.shape[0]
    rows = sents * GROUP

    def body(cot_ref, first_ref, n_ref, inv_ref, slope_ref, g_ref, wd_ref, sin_ref, bin_in_ref, _g, _t, gate_ref, two_ref, small_ref, bin_ref):
        small_ref[...] = sin_ref[...]
        bin_ref[...] = bin_in_ref[...]
        position = lax.broadcasted_iota(jnp.int32, (sents, GROUP, width), 1)
        at_first = jnp.broadcast_to(first_ref[...][:, None, :], (sents, GROUP, width))
        grad_block = cot_ref[...].astype(wide) + jnp.where(position == 0, at_first, 0.0)

        def store_gate(c, v):
            gate_ref[:, :, c : c + CHUNK] = v.reshape(sents, GROUP, CHUNK)

        got = ffn_backward_rows(
            grad_block.reshape(rows, width),
            n_ref[...],
            inv_ref[...],
            g_ref,
            wd_ref,
            lambda c: slope_ref[:, c : c + CHUNK],
            store_gate,
            small_ref,
            bin_ref,
        )
        two_ref[...] = got.reshape(sents, GROUP, width)

    zero = lambda i: 0
    anyspec = pl.BlockSpec(memory_space=pl.ANY)
    return call(
        body,
        (1,),
        [
            group_spec(sents, width, zero),
            whole((sents, width)),
            whole((rows, width)),
            whole((rows, 1)),
            whole((rows, ffn)),
            whole((1, width)),
            whole(w_down.shape),
            whole((8, width)),
            whole((1, ffn)),
            anyspec,
            anyspec,
        ],
        [group_spec(sents, ffn, zero), group_spec(sents, width, zero), whole((8, width)), whole((1, ffn))],
        [
            struct((sents, SEQ, ffn), low),
            struct((sents, SEQ, width), low),
            struct((8, width), wide),
            struct((1, ffn), wide),
        ],
        flops=2 * rows * width * ffn,
        aliases={9: 0, 10: 1},
    )(cot, grad_first, normed, inv, slope, gain, w_down, small, bin_sum, gate, two)


def lower_backward(two, gate, hidden, inv, proj, probs, w_in, w_out, gain, bias):
    tokens, width = hidden.shape
    ffn = w_in.shape[1]
    rows = 4 * SEQ
    pairs = width // (2 * HEAD_DIM)
    scale = 1.0 / math.sqrt(HEAD_DIM)

    def body(two_ref, gate_ref, hid_ref, inv_ref, proj_ref, prob_ref, wi_ref, wo_ref, g_ref, b_ref, one_ref, gp_ref, small_ref, bqv_ref, ctx_ref):
        @pl.when(pl.program_id(0) == 0)
        def _():
            small_ref[...] = jnp.zeros_like(small_ref)
            bqv_ref[...] = jnp.zeros_like(bqv_ref)

        grad_hidden = two_ref[...].astype(wide) + trans_right(gate_ref[...], wi_ref[...])
        normed = (hid_ref[...] - b_ref[...]) * (1.0 / g_ref[...])
        small_ref[0:1, :] += jnp.sum(grad_hidden * normed, axis=0, keepdims=True)
        small_ref[1:2, :] += jnp.sum(grad_hidden, axis=0, keepdims=True)
        grad_one = norm_input_grad(grad_hidden * g_ref[...], normed, inv_ref[...])
        small_ref[2:3, :] += jnp.sum(grad_one, axis=0, keepdims=True)
        one_low = grad_one.astype(low)
        one_ref[...] = one_low
        ctx_ref[...] = trans_right(one_low, wo_ref[...]).astype(low)
        first = lax.broadcasted_iota(jnp.int32, (SEQ, 128), 1) < HEAD_DIM
        for pair in range(pairs):
            c = pair * 128
            sum_q = jnp.zeros((1, 128), wide)
            sum_v = jnp.zeros((1, 128), wide)
            for sent in range(4):
                r = slice(sent * SEQ, (sent + 1) * SEQ)
                q = split_heads(proj_ref[r, c : c + 128], first)
                k = proj_ref[r, width + c : width + c + 128]
                v = proj_ref[r, 2 * width + c : 2 * width + c + 128]
                d = split_heads(ctx_ref[r, c : c + 128], first)
                p_low = prob_ref[sent, pair]
                p = p_low.astype(wide)
                grad_p = trans_right(v, d)
                grad_v = mat_mul(p_low, d)
                grad_s = (p * (grad_p - jnp.sum(grad_p * p, axis=0, keepdims=True))).astype(low)
                grad_k = mat_mul(grad_s, q) * scale
                grad_q = join_heads(trans_left(grad_s, k), first) * scale
                sum_q += jnp.sum(grad_q, axis=0, keepdims=True)
                sum_v += jnp.sum(grad_v, axis=0, keepdims=True)
                gp_ref[r, c : c + 128] = grad_q.astype(low)
                gp_ref[r, width + c : width + c + 128] = grad_k.astype(low)
                gp_ref[r, 2 * width + c : 2 * width + c + 128] = grad_v.astype(low)
            bqv_ref[0:1, c : c + 128] += sum_q
            bqv_ref[1:2, c : c + 128] += sum_v

    row = lambda cols: pl.BlockSpec((rows, cols), lambda i: (i, 0))
    return call(
        body,
        (tokens // rows,),
        [
            row(width),
            row(ffn),
            row(width),
            row(1),
            row(3 * width),
            pl.BlockSpec((4,) + probs.shape[1:], lambda i: (i, 0, 0, 0)),
            whole(w_in.shape),
            whole(w_out.shape),
            whole((1, width)),
            whole((1, width)),
        ],
        [row(width), row(3 * width), whole((8, width)), whole((8, width))],
        [struct((tokens, width), low), struct((tokens, 3 * width), low), struct((8, width), wide), struct((8, width), wide)],
        flops=2 * tokens * width * (ffn + width + 8 * SEQ),
        scratch=[pltpu.VMEM((rows, width), low)],
    )(two, gate, hidden, inv, proj, probs, w_in, w_out, gain, bias)


def input_gradient(grad_proj, w_qkv, grad_one):
    tokens, width = grad_one.shape
    rows = 4 * SEQ

    def body(gp_ref, w_ref, one_ref, out_ref):
        out_ref[...] = (one_ref[...].astype(wide) + trans_right(gp_ref[...], w_ref[...])).astype(low)

    row = lambda cols: pl.BlockSpec((rows, cols), lambda i: (i, 0))
    return call(
        body,
        (tokens // rows,),
        [row(3 * width), whole(w_qkv.shape), row(width)],
        row(width),
        struct((tokens, width), low),
        flops=6 * tokens * width * width,
    )(grad_proj, w_qkv, grad_one)


def weight_gradient(a, g, block):
    tokens, m = a.shape
    n = g.shape[1]

    def body(a_ref, g_ref, o_ref):
        o_ref[...] = trans_left(a_ref[...], g_ref[...]).astype(low)

    return call(
        body,
        (m // block,),
        [pl.BlockSpec((tokens, block), lambda i: (0, i)), whole(g.shape)],
        pl.BlockSpec((block, n), lambda i: (i, 0)),
        struct((m, n), low),
        flops=2 * tokens * m * n,
    )(a, g)


def contrastive(first, ids, w_pool, b_pool):
    total = first.shape[1]
    flat = first.reshape(2 * total, -1)
    pooled = jnp.tanh(mat_mul(flat, w_pool) + b_pool)
    inv_len = lax.rsqrt(jnp.sum(pooled * pooled, axis=-1, keepdims=True) + epsilon)
    unit = pooled * inv_len
    embed = unit.astype(low)
    zero, one = embed[:total], embed[total:]
    same = ids[:, None] == ids[None, :]
    eye = (jnp.arange(total)[:, None] == jnp.arange(total)[None, :]).astype(wide)
    logits = score_scale * trans_right(zero, one) - margin_shift * eye
    masked = jnp.where(same, logits, -jnp.inf)

    def soft(axis):
        e = jnp.exp(masked - jnp.max(masked, axis=axis, keepdims=True))
        return (score_scale * (e / jnp.sum(e, axis=axis, keepdims=True) - eye)).astype(low)

    by_row, by_col = soft(1), soft(0)
    grad_embed = jnp.concatenate(
        [mat_mul(by_row, one) + mat_mul(by_col, one), trans_left(by_row, zero) + trans_left(by_col, zero)]
    )
    grad_pre = (
        inv_len * (grad_embed - unit * jnp.sum(unit * grad_embed, axis=-1, keepdims=True)) * (1.0 - pooled * pooled)
    )
    pre_low = grad_pre.astype(low)
    return pre_low, trans_left(flat, pre_low), jnp.sum(grad_pre, axis=0)


def exchange(a, axis, mask):
    size = lax.axis_size(axis)
    return lax.ppermute(a, axis, [(i, i ^ mask) for i in range(size)])


def gather_ordered(a, axis, mask):
    got = exchange(a, axis, mask)
    bit = (lax.axis_index(axis) // mask) % 2
    n = a.shape[0]
    return lax.dynamic_slice_in_dim(jnp.concatenate([got, a, got]), (1 - bit) * n, 2 * n, 0)


def take_half(a, which, n):
    return lax.dynamic_slice_in_dim(a, which * n, n, 0)


def reduce_parts(terms, axis, mask):
    n = terms[0].shape[0] // 2
    bit = (lax.axis_index(axis) // mask) % 2
    send = sum(take_half(t, 1 - bit, n).astype(wide) for t in terms).astype(low)
    return [take_half(t, bit, n) for t in terms] + [exchange(send, axis, mask)]


def sum_all(part, steps):
    terms = [part]
    for axis, mask in steps:
        terms = reduce_parts(terms, axis, mask)
    total = sum(t.astype(wide) for t in terms).astype(low)
    return total


def spread(total, steps):
    for axis, mask in reversed(steps):
        total = gather_ordered(total, axis, mask)
    return total


def shards(
    embedded, seq_cotangent, pair_ids, w_qkv, b_qv, w_out, b_out, ln1_gain, ln1_bias, w_in, b_in, w_down, b_down,
    ln2_gain, ln2_bias, w_pool, b_pool,
):
    x = embedded[0]
    tokens, width = x.shape
    sents = tokens // SEQ
    ffn = w_in.shape[1]
    dp = lax.axis_size("dp")
    stream = lax.axis_index("stream")
    row = lambda v: v.reshape(1, -1)
    qkv_bias = row(jnp.concatenate([b_qv[:width], jnp.zeros((width,), wide), b_qv[width:]]))
    proj, probs, context, hidden, hidden_low, inv_one = attention_forward(
        x, w_qkv, qkv_bias, w_out, row(b_out), row(ln1_gain), row(ln1_bias)
    )
    hid3 = hidden.reshape(sents, SEQ, width)
    cot3 = seq_cotangent[0].reshape(sents, SEQ, width)
    upper = (w_in, row(b_in), w_down, row(b_down), row(ln2_gain), row(ln2_bias))
    enc, act, slope, normed_two, inv_two, first_low = ffn_first(hid3, *upper)
    gathered = first_low
    mask = 1
    while mask < dp:
        gathered = gather_ordered(gathered, "dp", mask)
        mask *= 2
    gathered = gather_ordered(gathered, "stream", 1)
    enc, act, gate, two, small_up, bin_sum = ffn_rest(hid3, cot3, *upper, enc, act)
    total = sents * dp
    pre_low, grad_w_pool, grad_b_pool = contrastive(gathered.reshape(2, total, width), pair_ids, w_pool, row(b_pool))
    own_pre = lax.dynamic_slice_in_dim(pre_low, stream * total + lax.axis_index("dp") * sents, sents)
    grad_first = trans_right(own_pre, w_pool)
    gate, two, small_up, bin_sum = ffn_first_back(
        cot3, grad_first, normed_two, inv_two, slope, row(ln2_gain), w_down, gate, two, small_up, bin_sum
    )
    act, gate, two = (v.reshape(tokens, -1) for v in (act, gate, two))
    grad_w_down = weight_gradient(act, two, 768)
    grad_w_in = weight_gradient(hidden_low, gate, 256)
    grad_one, grad_proj, small_low, bqv = lower_backward(
        two, gate, hidden, inv_one, proj, probs, w_in, w_out, row(ln1_gain), row(ln1_bias)
    )
    grad_w_qkv = weight_gradient(x, grad_proj, 256)
    grad_w_out = weight_gradient(context, grad_one, 256)
    grad_input = input_gradient(grad_proj, w_qkv, grad_one)

    bits = [1 << i for i in range(4)]
    tail = [1 << i for i in range(4, dp.bit_length() - 1)]
    order_a = [("stream", 1)] + [("dp", m) for m in bits]
    order_b = [("stream", 1)] + [("dp", m) for m in [bits[1], bits[0]] + bits[2:]]

    def reduce(part, order):
        s = sum_all(part, order)
        for m in tail:
            s = (s.astype(wide) + exchange(s, "dp", m).astype(wide)).astype(low)
        return spread(s, order)

    half = ffn // 2
    out_down = jnp.concatenate([reduce(grad_w_down[:half], order_a), reduce(grad_w_down[half:], order_b)], 0)
    out_in = jnp.concatenate([reduce(grad_w_in[:, :half], order_a), reduce(grad_w_in[:, half:], order_b)], 1)
    lower_rest = jnp.concatenate([grad_w_qkv[:, half:], grad_w_out], 1)
    out_qkv_a = reduce(grad_w_qkv[:, :half], order_a)
    out_rest = reduce(lower_rest, order_b)
    out_qkv = jnp.concatenate([out_qkv_a, out_rest[:, : 3 * width - half]], 1)
    out_out = out_rest[:, 3 * width - half :]
    small = jnp.concatenate([small_up[:3], bin_sum.reshape(-1, width), small_low[:3], bqv[:2]], 0)
    for axis, m in [("stream", 1)] + [("dp", m) for m in bits + tail]:
        small = small + exchange(small, axis, m)
    f32 = lambda v: v.astype(wide)
    n_in = ffn // width
    return (
        enc.reshape(1, tokens, width),
        grad_input[None],
        f32(out_qkv),
        small[6 + n_in : 8 + n_in].reshape(-1),
        f32(out_out),
        small[5 + n_in],
        small[3 + n_in],
        small[4 + n_in],
        f32(out_in),
        small[3 : 3 + n_in].reshape(-1),
        f32(out_down),
        small[2],
        small[0],
        small[1],
        grad_w_pool,
        grad_b_pool,
    )


def solution(mesh):
    sharded = P("stream", "dp", None)
    return jax.shard_map(
        shards,
        mesh=mesh,
        in_specs=(sharded, sharded) + (P(),) * 15,
        out_specs=(sharded, sharded) + (P(),) * 14,
        check_vma=False,
    )
```

```python
import math

import jax
import jax.numpy as jnp
from jax import lax
from jax.experimental import pallas as pl
from jax.experimental.pallas import tpu as pltpu
from jax.sharding import PartitionSpec as P

HEAD_DIM = 64
SEQ = 64
GROUP = 16
CHUNK = 512

epsilon = 1e-06
score_scale = 10.0
margin_shift = score_scale * 0.3
root_half = 0.7071067811865476
gauss_norm = 0.3989422804014327

low = jnp.bfloat16
wide = jnp.float32
ANY = pl.BlockSpec(memory_space=pl.ANY)


def struct(shape, dtype):
    return jax.ShapeDtypeStruct(shape, dtype)


def whole(shape):
    return pl.BlockSpec(shape, lambda *_: (0,) * len(shape))


def call(body, grid, ins, outs, bits=None, scratch=(), aliases=None, after=(), limit=60):
    n_in, n_bits = len(ins), 0 if bits is None else 1

    def wrapped(*refs):
        body(*refs[: n_bits + n_in], *refs[n_bits + n_in + len(after) :])

    return pl.pallas_call(
        wrapped,
        grid_spec=pltpu.PrefetchScalarGridSpec(
            num_scalar_prefetch=n_bits,
            grid=grid,
            in_specs=[s for s, _ in ins] + [ANY] * len(after),
            out_specs=[s for s, _ in outs],
            scratch_shapes=list(scratch),
        ),
        out_shape=[s for _, s in outs],
        input_output_aliases={n_bits + k: v for k, v in (aliases or {}).items()},
        cost_estimate=pl.CostEstimate(flops=0, bytes_accessed=0, transcendentals=0),
        compiler_params=pltpu.CompilerParams(vmem_limit_bytes=limit << 20),
    )(*([] if bits is None else [bits]), *[a for _, a in ins], *after)


def mat_mul(a, b):
    return jnp.dot(a, b, preferred_element_type=wide)


def trans_left(a, b):
    return lax.dot_general(a, b, (((0,), (0,)), ((), ())), preferred_element_type=wide)


def trans_right(a, b):
    return lax.dot_general(a, b, (((1,), (1,)), ((), ())), preferred_element_type=wide)


def normalize(h):
    center = h - jnp.mean(h, axis=-1, keepdims=True)
    inv = lax.rsqrt(jnp.mean(center * center, axis=-1, keepdims=True) + epsilon)
    return center * inv, inv


def norm_input_grad(grad, normed, inv):
    return inv * (
        grad
        - jnp.mean(grad, axis=-1, keepdims=True)
        - normed * jnp.mean(grad * normed, axis=-1, keepdims=True)
    )


def split_heads(pair, first):
    zero = jnp.zeros_like(pair)
    return jnp.concatenate([jnp.where(first, pair, zero), jnp.where(first, zero, pair)], axis=0)


def join_heads(rows, first):
    return jnp.where(first, rows[:SEQ], rows[SEQ:])


class Rows:
    def __init__(self, width, ffn):
        self.at, start = {}, 0
        for name, size in (
            ("qkv", 3 * width), ("out", width), ("gain1", width), ("bias1", width), ("in", ffn),
            ("down", width), ("gain2", width), ("bias2", width), ("pool", width),
        ):
            self.at[name] = (start, size)
            start += size
        self.size = start

    def read(self, ref, name, start=0, size=None):
        base, full = self.at[name]
        return ref[:, base + start : base + start + (full if size is None else size)]


def attention_forward(x, w_qkv, w_out, pack, rows_of):
    tokens, width = x.shape
    rows = 4 * SEQ
    pairs = width // (2 * HEAD_DIM)
    scale = 1.0 / math.sqrt(HEAD_DIM)

    def body(x_ref, wq_ref, wo_ref, pack_ref, proj_ref, prob_ref, ctx_ref, hid_ref, low_ref, inv_ref):
        x_in = x_ref[...]
        for part in range(3):
            c = slice(part * width, (part + 1) * width)
            proj_ref[:, c] = (mat_mul(x_in, wq_ref[:, c]) + rows_of.read(pack_ref, "qkv", part * width, width)).astype(low)
        first = lax.broadcasted_iota(jnp.int32, (SEQ, 128), 1) < HEAD_DIM
        cols = [slice(p * 128, (p + 1) * 128) for p in range(pairs)]
        for sent in range(4):
            r = slice(sent * SEQ, (sent + 1) * SEQ)
            q = proj_ref[r, :width]
            k = proj_ref[r, width : 2 * width]
            v = proj_ref[r, 2 * width :]
            scores = jnp.concatenate([trans_right(k[:, c], split_heads(q[:, c], first)) for c in cols], axis=1) * scale
            e = jnp.exp(scores - jnp.max(scores, axis=0, keepdims=True))
            probs = (e * (1.0 / jnp.sum(e, axis=0, keepdims=True))).astype(low)
            prob_ref[r, :] = probs
            ctx_ref[r, :] = jnp.concatenate(
                [join_heads(trans_left(probs[:, c], v[:, c]), first) for c in cols], axis=1
            ).astype(low)
        h = x_in.astype(wide) + mat_mul(ctx_ref[...], wo_ref[...]) + rows_of.read(pack_ref, "out")
        normed, inv = normalize(h)
        hidden = normed * rows_of.read(pack_ref, "gain1") + rows_of.read(pack_ref, "bias1")
        hid_ref[...] = hidden
        low_ref[...] = hidden.astype(low)
        inv_ref[...] = inv

    row = lambda cols: pl.BlockSpec((rows, cols), lambda i, *_: (i, 0))
    return call(
        body,
        (tokens // rows,),
        [(row(width), x), (whole(w_qkv.shape), w_qkv), (whole(w_out.shape), w_out), (whole(pack.shape), pack)],
        [
            (row(3 * width), struct((tokens, 3 * width), low)),
            (row(width), struct((tokens, width), low)),
            (row(width), struct((tokens, width), low)),
            (row(width), struct((tokens, width), wide)),
            (row(width), struct((tokens, width), low)),
            (row(1), struct((tokens, 1), wide)),
        ],
    )


class Streamed:
    def __init__(self, source, target, sems, axis):
        self.copies = []
        for n in range(source.shape[axis] // CHUNK):
            at = (slice(None),) * axis + (pl.ds(n * CHUNK, CHUNK),)
            self.copies.append(pltpu.make_async_copy(source.at[at], target.at[at], sems.at[n]))

    def start(self, n):
        self.copies[n].start()

    def wait(self, n):
        self.copies[n].wait()


def ffn_forward_rows(hidden, wi_ref, wd_ref, pack_ref, rows_of, wait, store_act, store_slope):
    h_low = hidden.astype(low)
    total = hidden + rows_of.read(pack_ref, "down")
    for n in range(wi_ref.shape[1] // CHUNK):
        c = n * CHUNK
        wait(n)
        u = mat_mul(h_low, wi_ref[:, c : c + CHUNK]) + rows_of.read(pack_ref, "in", c, CHUNK)
        phi = 0.5 + 0.5 * lax.erf(u * root_half)
        act = (u * phi).astype(low)
        store_act(c, act)
        store_slope(c, (phi + u * jnp.exp(-0.5 * u * u) * gauss_norm).astype(low))
        total = total + mat_mul(act, wd_ref[c : c + CHUNK, :])
    return normalize(total)


def ffn_backward_rows(grad_block, normed, inv, gain, wd_ref, wait, slope_of, store_gate, small_ref, bin_ref):
    grad_two = norm_input_grad(grad_block * gain, normed, inv)
    small_ref[0:1, :] += jnp.sum(grad_block * normed, axis=0, keepdims=True)
    small_ref[1:2, :] += jnp.sum(grad_block, axis=0, keepdims=True)
    small_ref[2:3, :] += jnp.sum(grad_two, axis=0, keepdims=True)
    grad_low = grad_two.astype(low)
    for n in range(wd_ref.shape[0] // CHUNK):
        c = n * CHUNK
        wait(n)
        gate = trans_right(grad_low, wd_ref[c : c + CHUNK, :]) * slope_of(c).astype(wide)
        bin_ref[:, c : c + CHUNK] += jnp.sum(gate, axis=0, keepdims=True)
        store_gate(c, gate.astype(low))
    return grad_low


def group_spec(sents, cols, index):
    return pl.BlockSpec((sents, GROUP, cols), lambda i, *_: (0, index, 0))


def ffn_scratch(width, ffn):
    parts = ffn // CHUNK
    return [
        pltpu.VMEM((width, ffn), low),
        pltpu.VMEM((ffn, width), low),
        pltpu.SemaphoreType.DMA((parts,)),
        pltpu.SemaphoreType.DMA((parts,)),
    ]


def start_ffn_weights(wi_hbm, wd_hbm, wi_ref, wd_ref, sem_i, sem_d):
    stream_i = Streamed(wi_hbm, wi_ref, sem_i, 1)
    stream_d = Streamed(wd_hbm, wd_ref, sem_d, 0)
    for n in range(len(stream_i.copies)):
        stream_i.start(n)
        stream_d.start(n)

    def wait(n):
        stream_i.wait(n)
        stream_d.wait(n)

    return wait


def ffn_first(hidden, w_in, w_down, pack, rows_of):
    sents, _, width = hidden.shape
    ffn = w_in.shape[1]
    rows = sents * GROUP

    def body(h_ref, wi_hbm, wd_hbm, pack_ref, enc_ref, act_ref, slope_ref, n_ref, inv_ref, first_ref, wi_ref, wd_ref, sem_i, sem_d):
        wait = start_ffn_weights(wi_hbm, wd_hbm, wi_ref, wd_ref, sem_i, sem_d)

        def store_act(c, v):
            act_ref[:, :, c : c + CHUNK] = v.reshape(sents, GROUP, CHUNK)

        def store_slope(c, v):
            slope_ref[:, c : c + CHUNK] = v

        normed, inv = ffn_forward_rows(
            h_ref[...].reshape(rows, width), wi_ref, wd_ref, pack_ref, rows_of, wait, store_act, store_slope
        )
        n_ref[...] = normed
        inv_ref[...] = inv
        block = (normed * rows_of.read(pack_ref, "gain2") + rows_of.read(pack_ref, "bias2")).reshape(sents, GROUP, width)
        enc_ref[...] = block.astype(low)
        first_ref[...] = block[:, 0, :].astype(low)

    return call(
        body,
        (1,),
        [(group_spec(sents, width, 0), hidden), (ANY, w_in), (ANY, w_down), (whole(pack.shape), pack)],
        [
            (group_spec(sents, width, 0), struct((sents, SEQ, width), low)),
            (group_spec(sents, ffn, 0), struct((sents, SEQ, ffn), low)),
            (whole((rows, ffn)), struct((rows, ffn), low)),
            (whole((rows, width)), struct((rows, width), wide)),
            (whole((rows, 1)), struct((rows, 1), wide)),
            (whole((sents, width)), struct((sents, width), low)),
        ],
        scratch=ffn_scratch(width, ffn),
    )


def ffn_group(index, hidden, cot, w_in, w_down, pack, rows_of, encoded, act, gate, two, small, bin_sum, after=()):
    sents, _, width = hidden.shape
    ffn = w_in.shape[1]
    rows = sents * GROUP
    fresh = gate is None

    def body(h_ref, cot_ref, wi_hbm, wd_hbm, pack_ref, *refs):
        refs = refs[2 if fresh else 4 :]
        if not fresh:
            sin_ref, bin_in_ref = refs[:2]
            refs = refs[2:]
        enc_ref, act_ref, gate_ref, two_ref, small_ref, bin_ref, slope_ref, wi_ref, wd_ref, sem_i, sem_d = refs
        wait = start_ffn_weights(wi_hbm, wd_hbm, wi_ref, wd_ref, sem_i, sem_d)
        small_ref[...] = jnp.zeros_like(small_ref) if fresh else sin_ref[...]
        bin_ref[...] = jnp.zeros_like(bin_ref) if fresh else bin_in_ref[...]

        def store_act(c, v):
            act_ref[:, :, c : c + CHUNK] = v.reshape(sents, GROUP, CHUNK)

        def store_slope(c, v):
            slope_ref[:, c : c + CHUNK] = v

        def store_gate(c, v):
            gate_ref[:, :, c : c + CHUNK] = v.reshape(sents, GROUP, CHUNK)

        normed, inv = ffn_forward_rows(
            h_ref[...].reshape(rows, width), wi_ref, wd_ref, pack_ref, rows_of, wait, store_act, store_slope
        )
        gain = rows_of.read(pack_ref, "gain2")
        enc_ref[...] = (normed * gain + rows_of.read(pack_ref, "bias2")).astype(low).reshape(sents, GROUP, width)
        grad_block = cot_ref[...].reshape(rows, width).astype(wide)
        got = ffn_backward_rows(
            grad_block, normed, inv, gain, wd_ref, lambda n: None, lambda c: slope_ref[:, c : c + CHUNK], store_gate,
            small_ref, bin_ref,
        )
        two_ref[...] = got.reshape(sents, GROUP, width)

    spec = lambda cols: group_spec(sents, cols, index)
    kept = [(ANY, encoded), (ANY, act)]
    aliases = {5: 0, 6: 1}
    if not fresh:
        kept += [(ANY, gate), (ANY, two), (whole(small.shape), small), (whole(bin_sum.shape), bin_sum)]
        aliases.update({7: 2, 8: 3})
    return call(
        body,
        (1,),
        [(spec(width), hidden), (spec(width), cot), (ANY, w_in), (ANY, w_down), (whole(pack.shape), pack)] + kept,
        [
            (spec(width), struct((sents, SEQ, width), low)),
            (spec(ffn), struct((sents, SEQ, ffn), low)),
            (spec(ffn), struct((sents, SEQ, ffn), low)),
            (spec(width), struct((sents, SEQ, width), low)),
            (whole((8, width)), struct((8, width), wide)),
            (whole((1, ffn)), struct((1, ffn), wide)),
        ],
        scratch=[pltpu.VMEM((rows, ffn), low)] + ffn_scratch(width, ffn),
        aliases=aliases,
        after=after,
    )


def ffn_first_back(cot, grad_first, normed, inv, slope, w_down, pack, rows_of, gate, two, small, bin_sum, after=()):
    sents, _, width = cot.shape
    ffn = w_down.shape[0]
    rows = sents * GROUP

    def body(cot_ref, first_ref, n_ref, inv_ref, slope_ref, wd_hbm, pack_ref, sin_ref, bin_in_ref, _g, _t, gate_ref, two_ref, small_ref, bin_ref, wd_ref, sem):
        stream = Streamed(wd_hbm, wd_ref, sem, 0)
        for n in range(ffn // CHUNK):
            stream.start(n)
        small_ref[...] = sin_ref[...]
        bin_ref[...] = bin_in_ref[...]
        position = lax.broadcasted_iota(jnp.int32, (sents, GROUP, width), 1)
        at_first = jnp.broadcast_to(first_ref[...][:, None, :], (sents, GROUP, width))
        grad_block = cot_ref[...].astype(wide) + jnp.where(position == 0, at_first, 0.0)

        def store_gate(c, v):
            gate_ref[:, :, c : c + CHUNK] = v.reshape(sents, GROUP, CHUNK)

        got = ffn_backward_rows(
            grad_block.reshape(rows, width), n_ref[...], inv_ref[...], rows_of.read(pack_ref, "gain2"), wd_ref, stream.wait,
            lambda c: slope_ref[:, c : c + CHUNK], store_gate, small_ref, bin_ref,
        )
        two_ref[...] = got.reshape(sents, GROUP, width)

    return call(
        body,
        (1,),
        [
            (group_spec(sents, width, 0), cot),
            (whole((sents, width)), grad_first),
            (whole((rows, width)), normed),
            (whole((rows, 1)), inv),
            (whole((rows, ffn)), slope),
            (ANY, w_down),
            (whole(pack.shape), pack),
            (whole(small.shape), small),
            (whole(bin_sum.shape), bin_sum),
            (ANY, gate),
            (ANY, two),
        ],
        [
            (group_spec(sents, ffn, 0), struct((sents, SEQ, ffn), low)),
            (group_spec(sents, width, 0), struct((sents, SEQ, width), low)),
            (whole((8, width)), struct((8, width), wide)),
            (whole((1, ffn)), struct((1, ffn), wide)),
        ],
        scratch=[pltpu.VMEM((ffn, width), low), pltpu.SemaphoreType.DMA((ffn // CHUNK,))],
        aliases={9: 0, 10: 1},
        after=after,
    )


def lower_backward(part, parts, two, gate, hidden, inv, proj, probs, w_in, w_out, pack, rows_of, before=None, after=()):
    tokens, width = hidden.shape
    ffn = w_in.shape[1]
    rows = 4 * SEQ
    steps = tokens // rows // parts
    pairs = width // (2 * HEAD_DIM)
    scale = 1.0 / math.sqrt(HEAD_DIM)
    fresh = before is None

    def body(two_ref, gate_ref, hid_ref, inv_ref, proj_ref, prob_ref, wi_hbm, wo_ref, pack_ref, *refs):
        if not fresh:
            sin_ref, bin_ref = refs[2:4]
            refs = refs[4:]
        one_ref, gp_ref, small_ref, bqv_ref, ctx_ref, wi_ref, sem = refs
        stream = Streamed(wi_hbm, wi_ref, sem, 1)

        @pl.when(pl.program_id(0) == 0)
        def _():
            for n in range(ffn // CHUNK):
                stream.start(n)
            small_ref[...] = jnp.zeros_like(small_ref) if fresh else sin_ref[...]
            bqv_ref[...] = jnp.zeros_like(bqv_ref) if fresh else bin_ref[...]
            for n in range(ffn // CHUNK):
                stream.wait(n)

        gain = rows_of.read(pack_ref, "gain1")
        grad_hidden = two_ref[...].astype(wide) + trans_right(gate_ref[...], wi_ref[...])
        normed = (hid_ref[...] - rows_of.read(pack_ref, "bias1")) * (1.0 / gain)
        small_ref[0:1, :] += jnp.sum(grad_hidden * normed, axis=0, keepdims=True)
        small_ref[1:2, :] += jnp.sum(grad_hidden, axis=0, keepdims=True)
        grad_one = norm_input_grad(grad_hidden * gain, normed, inv_ref[...])
        small_ref[2:3, :] += jnp.sum(grad_one, axis=0, keepdims=True)
        one_low = grad_one.astype(low)
        one_ref[...] = one_low
        ctx_ref[...] = trans_right(one_low, wo_ref[...]).astype(low)
        first = lax.broadcasted_iota(jnp.int32, (SEQ, 128), 1) < HEAD_DIM
        sum_q = jnp.zeros((1, width), wide)
        sum_v = jnp.zeros((1, width), wide)
        cols = [slice(p * 128, (p + 1) * 128) for p in range(pairs)]
        for sent in range(4):
            r = slice(sent * SEQ, (sent + 1) * SEQ)
            q_all = proj_ref[r, :width]
            k = proj_ref[r, width : 2 * width]
            v = proj_ref[r, 2 * width :]
            d_all = ctx_ref[r, :]
            p_low = prob_ref[r, :]
            q = [split_heads(q_all[:, c], first) for c in cols]
            d = [split_heads(d_all[:, c], first) for c in cols]
            p = p_low.astype(wide)
            grad_p = jnp.concatenate([trans_right(v[:, c], dd) for c, dd in zip(cols, d)], axis=1)
            grad_v = jnp.concatenate([mat_mul(p_low[:, c], dd) for c, dd in zip(cols, d)], axis=1)
            gp = grad_p * p
            grad_s = (gp - p * jnp.sum(gp, axis=0, keepdims=True)).astype(low)
            grad_k = jnp.concatenate([mat_mul(grad_s[:, c], qq) for c, qq in zip(cols, q)], axis=1) * scale
            grad_q = (
                jnp.concatenate([join_heads(trans_left(grad_s[:, c], k[:, c]), first) for c in cols], axis=1) * scale
            )
            sum_q += jnp.sum(grad_q, axis=0, keepdims=True)
            sum_v += jnp.sum(grad_v, axis=0, keepdims=True)
            gp_ref[r, :width] = grad_q.astype(low)
            gp_ref[r, width : 2 * width] = grad_k.astype(low)
            gp_ref[r, 2 * width :] = grad_v.astype(low)
        bqv_ref[0:1, :] += sum_q
        bqv_ref[1:2, :] += sum_v

    row = lambda cols: pl.BlockSpec((rows, cols), lambda i, *_: (i + part * steps, 0))
    ins = [
        (row(width), two),
        (row(ffn), gate),
        (row(width), hidden),
        (row(1), inv),
        (row(3 * width), proj),
        (row(width), probs),
        (ANY, w_in),
        (whole(w_out.shape), w_out),
        (whole(pack.shape), pack),
    ]
    if not fresh:
        ins += [(ANY, before[0]), (ANY, before[1]), (whole((8, width)), before[2]), (whole((8, width)), before[3])]
    return call(
        body,
        (steps,),
        ins,
        [
            (row(width), struct((tokens, width), low)),
            (row(3 * width), struct((tokens, 3 * width), low)),
            (whole((8, width)), struct((8, width), wide)),
            (whole((8, width)), struct((8, width), wide)),
        ],
        scratch=[pltpu.VMEM((rows, width), low), pltpu.VMEM((width, ffn), low), pltpu.SemaphoreType.DMA((ffn // CHUNK,))],
        aliases=None if fresh else {9: 0, 10: 1},
        after=after,
    )


def input_gradient(grad_proj, w_qkv, grad_one, after=()):
    tokens, width = grad_one.shape
    rows = 4 * SEQ

    def body(gp_ref, w_ref, one_ref, out_ref):
        out_ref[...] = (one_ref[...].astype(wide) + trans_right(gp_ref[...], w_ref[...])).astype(low)

    row = lambda cols: pl.BlockSpec((rows, cols), lambda i, *_: (i, 0))
    return call(
        body,
        (tokens // rows,),
        [(row(3 * width), grad_proj), (whole(w_qkv.shape), w_qkv), (row(width), grad_one)],
        [(row(width), struct((tokens, width), low))],
        after=after,
    )[0]


def contrastive(first, ids, w_pool, b_pool):
    total = first.shape[1]
    flat = first.reshape(2 * total, -1)
    pooled = jnp.tanh(mat_mul(flat, w_pool) + b_pool)
    inv_len = lax.rsqrt(jnp.sum(pooled * pooled, axis=-1, keepdims=True) + epsilon)
    unit = pooled * inv_len
    embed = unit.astype(low)
    zero, one = embed[:total], embed[total:]
    same = ids[:, None] == ids[None, :]
    eye = (jnp.arange(total)[:, None] == jnp.arange(total)[None, :]).astype(wide)
    logits = score_scale * trans_right(zero, one) - margin_shift * eye
    masked = jnp.where(same, logits, -jnp.inf)

    def soft(axis):
        e = jnp.exp(masked - jnp.max(masked, axis=axis, keepdims=True))
        return (score_scale * (e / jnp.sum(e, axis=axis, keepdims=True) - eye)).astype(low)

    by_row, by_col = soft(1), soft(0)
    grad_embed = jnp.concatenate(
        [mat_mul(by_row, one) + mat_mul(by_col, one), trans_left(by_row, zero) + trans_left(by_col, zero)]
    )
    grad_pre = (
        inv_len * (grad_embed - unit * jnp.sum(unit * grad_embed, axis=-1, keepdims=True)) * (1.0 - pooled * pooled)
    )
    pre_low = grad_pre.astype(low)
    return pre_low, trans_left(flat, pre_low), jnp.sum(grad_pre, axis=0)


CORE, BIT0, BIT1, BIT2 = range(4)


def exchange(a, axis, mask):
    size = lax.axis_size(axis)
    return lax.ppermute(a, axis, [(i, i ^ mask) for i in range(size)])


class Sources:
    def __init__(self, pairs):
        self.pairs = pairs
        self.m = pairs[0][0].shape[1]
        self.n = sum(g.shape[1] for _, g in pairs)
        self.tokens = pairs[0][0].shape[0]


def gradient_rows(src, bits, recv, after=()):
    m, n, tokens = src.m, src.n, src.tokens
    keep = recv is not None
    by_rows = m > n
    half = m // 2
    tile = (half // 4, n) if by_rows else (half, n // 4)
    count = len(src.pairs)
    starts = []
    at = 0
    for _, g in src.pairs:
        starts.append(at)
        at += g.shape[1] // tile[1]
    starts.append(at)

    def row_block(core, i):
        mine = core if keep else 1 - core
        return mine * (half // tile[0]) + (i if by_rows else 0)

    ins = []
    for p, (a, g) in enumerate(src.pairs):
        ins.append((pl.BlockSpec((tokens, tile[0]), lambda i, b: (0, row_block(b[CORE], i))), a))
        lo, hi = starts[p], starts[p + 1]
        ins.append(
            (
                pl.BlockSpec(
                    (tokens, tile[1]), lambda i, b, lo=lo, hi=hi: (0, 0 if by_rows else jnp.clip(i - lo, 0, hi - lo - 1))
                ),
                g,
            )
        )
    tiled = pl.BlockSpec(tile, lambda i, b: (i, 0) if by_rows else (0, i))
    if not keep:

        def body(b, *refs):
            out = refs[2 * count]
            for p in range(count):

                def run(p=p):
                    out[...] = trans_left(refs[2 * p][...], refs[2 * p + 1][...]).astype(low)

                if count == 1:
                    run()
                else:
                    pl.when((pl.program_id(0) >= starts[p]) & (pl.program_id(0) < starts[p + 1]))(run)

        return call(body, (4,), ins, [(tiled, struct((half, n), low))], bits=bits, after=after)[0]

    ins.append((tiled, recv))
    quarter = (half // 2, n // 2)

    def body(b, *refs):
        got = refs[2 * count]
        left_send, left_keep, right_send, right_keep = refs[2 * count + 1 :]
        i = pl.program_id(0)

        def put(send_ref, keep_ref, bit, rows, cols, upper, value):
            @pl.when(b[bit] == upper)
            def _():
                keep_ref[rows, cols] = value.astype(low)

            @pl.when(b[bit] != upper)
            def _():
                send_ref[rows, cols] = value.astype(low)

        for p in range(count):

            def run(p=p):
                value = trans_left(refs[2 * p][...], refs[2 * p + 1][...]) + got[...].astype(wide)
                if by_rows:
                    rows = pl.ds(pl.multiple_of((i % 2) * tile[0], tile[0]), tile[0])
                    put(left_send, left_keep, BIT0, rows, slice(None), i // 2, value[:, : n // 2])
                    put(right_send, right_keep, BIT1, rows, slice(None), i // 2, value[:, n // 2 :])
                else:
                    cols = pl.ds(pl.multiple_of((i % 2) * tile[1], tile[1]), tile[1])

                    @pl.when(i < 2)
                    def _():
                        put(left_send, left_keep, BIT0, slice(None), cols, 0, value[: half // 2])
                        put(left_send, left_keep, BIT0, slice(None), cols, 1, value[half // 2 :])

                    @pl.when(i >= 2)
                    def _():
                        put(right_send, right_keep, BIT1, slice(None), cols, 0, value[: half // 2])
                        put(right_send, right_keep, BIT1, slice(None), cols, 1, value[half // 2 :])

            if count == 1:
                run()
            else:
                pl.when((i >= starts[p]) & (i < starts[p + 1]))(run)

    return call(body, (4,), ins, [(whole(quarter), struct(quarter, low))] * 4, bits=bits, after=after)


def part_rows(ref, bit, rows):
    return ref[pl.ds(pl.multiple_of(bit * rows, rows), rows), :].astype(wide)


def whole_call(body, arrays, shapes, bits, after=()):
    return call(
        body, (1,), [(whole(a.shape), a) for a in arrays], [(whole(s), struct(s, low)) for s in shapes], bits=bits, after=after
    )


def halve_sides(left, left_got, right, right_got, bits, after=()):
    rows, cols = left.shape[0] // 2, left.shape[1]

    def body(b, l, lg, r, rg, ls, lk, rs, rk):
        for mine, got, bit, send, keep in ((l, lg, BIT1, ls, lk), (r, rg, BIT0, rs, rk)):
            send[...] = (part_rows(mine, 1 - b[bit], rows) + part_rows(got, 1 - b[bit], rows)).astype(low)
            keep[...] = (part_rows(mine, b[bit], rows) + part_rows(got, b[bit], rows)).astype(low)

    return whole_call(body, [left, left_got, right, right_got], [(rows, cols)] * 4, bits, after)


def halve_both(left, left_got, right, right_got, bits, after=()):
    rows, cols = left.shape[0] // 2, left.shape[1]

    def body(b, l, lg, r, rg, send, keep):
        for mine, got, c in ((l, lg, slice(0, cols)), (r, rg, slice(cols, 2 * cols))):
            send[:, c] = (part_rows(mine, 1 - b[BIT2], rows) + part_rows(got, 1 - b[BIT2], rows)).astype(low)
            keep[:, c] = (part_rows(mine, b[BIT2], rows) + part_rows(got, b[BIT2], rows)).astype(low)

    return whole_call(body, [left, left_got, right, right_got], [(rows, 2 * cols)] * 2, bits, after)


def add_up(mine, got, bits, after=()):
    def body(b, m, g, out):
        out[...] = (m[...].astype(wide) + g[...].astype(wide)).astype(low)

    return whole_call(body, [mine, got], [mine.shape], bits, after)[0]


def place(out, mine, got, bit, cols=slice(None)):
    rows = mine.shape[0]
    out[pl.ds(pl.multiple_of(bit * rows, rows), rows), :] = mine[:, cols]
    out[pl.ds(pl.multiple_of((1 - bit) * rows, rows), rows), :] = got[:, cols]


def join_both(mine, got, bits, after=()):
    rows, cols = mine.shape[0], mine.shape[1] // 2

    def body(b, m, g, left, right):
        place(left, m, g, b[BIT2], slice(0, cols))
        place(right, m, g, b[BIT2], slice(cols, 2 * cols))

    return whole_call(body, [mine, got], [(2 * rows, cols)] * 2, bits, after)


def join_sides(left, left_got, right, right_got, bits, after=()):
    rows, cols = left.shape

    def body(b, l, lg, r, rg, lo, ro):
        place(lo, l, lg, b[BIT1])
        place(ro, r, rg, b[BIT0])

    return whole_call(body, [left, left_got, right, right_got], [(2 * rows, cols)] * 2, bits, after)


def join_half(left, left_got, right, right_got, bits, after=()):
    rows, cols = left.shape

    def body(b, l, lg, r, rg, out):
        place(out.at[:, pl.ds(0, cols)], l, lg, b[BIT0])
        place(out.at[:, pl.ds(cols, cols)], r, rg, b[BIT1])

    return whole_call(body, [left, left_got, right, right_got], [(2 * rows, 2 * cols)], bits, after)[0]


def widen(mine, got, widths, bits, after=()):
    half, n = mine.shape
    tile = half // 4

    def body(b, m, g, *outs):
        mine_now = (pl.program_id(0) // 4) == b[CORE]
        value = jnp.where(mine_now, m[...], g[...]).astype(wide)
        at = 0
        for out, w in zip(outs, widths):
            out[...] = value[:, at : at + w]
            at += w

    def index(core_of):
        return lambda i, b: (jnp.clip(i - 4 * core_of(b), 0, 3), 0)

    return call(
        body,
        (8,),
        [(pl.BlockSpec((tile, n), index(lambda b: b[CORE])), mine), (pl.BlockSpec((tile, n), index(lambda b: 1 - b[CORE])), got)],
        [(pl.BlockSpec((tile, w), lambda i, b: (i, 0)), struct((2 * half, w), wide)) for w in widths],
        bits=bits,
        after=after,
    )


class Reduction:
    def __init__(self, src, widths, bits, clock, tail):
        self.src, self.widths, self.bits, self.clock, self.tail = src, widths, bits, clock, tail

    def step(self, fn, *args):
        out = fn(*args, after=self.clock.now())
        self.clock.set(out[0] if isinstance(out, (list, tuple)) else out)
        return out

    def core_send(self):
        send = self.step(gradient_rows, self.src, self.bits, None)
        self.got = exchange(send, "stream", 1)

    def core_sum(self):
        ls, self.l, rs, self.r = self.step(gradient_rows, self.src, self.bits, self.got)
        self.gl, self.gr = exchange(ls, "dp", 1), exchange(rs, "dp", 2)

    def first_sum(self):
        ls, self.l, rs, self.r = self.step(halve_sides, self.l, self.gl, self.r, self.gr, self.bits)
        self.gl, self.gr = exchange(ls, "dp", 2), exchange(rs, "dp", 1)

    def second_sum(self):
        send, self.v = self.step(halve_both, self.l, self.gl, self.r, self.gr, self.bits)
        self.got = exchange(send, "dp", 4)

    def third_sum(self):
        self.v = self.step(add_up, self.v, self.got, self.bits)
        self.got = exchange(self.v, "dp", self.tail[0])

    def last_sum(self):
        for mask in self.tail[1:]:
            self.v = self.step(add_up, self.v, self.got, self.bits)
            self.got = exchange(self.v, "dp", mask)
        self.v = self.step(add_up, self.v, self.got, self.bits)
        self.got = exchange(self.v, "dp", 4)

    def third_back(self):
        self.l, self.r = self.step(join_both, self.v, self.got, self.bits)
        self.gl, self.gr = exchange(self.l, "dp", 2), exchange(self.r, "dp", 1)

    def second_back(self):
        self.l, self.r = self.step(join_sides, self.l, self.gl, self.r, self.gr, self.bits)
        self.gl, self.gr = exchange(self.l, "dp", 1), exchange(self.r, "dp", 2)

    def first_back(self):
        self.v = self.step(join_half, self.l, self.gl, self.r, self.gr, self.bits)
        self.got = exchange(self.v, "stream", 1)

    def finish(self):
        return self.step(widen, self.v, self.got, self.widths, self.bits)


class Clock:
    def __init__(self, start):
        self.last = start

    def now(self):
        return (self.last,)

    def set(self, value):
        self.last = value


def gather_ordered(a, axis, mask):
    got = exchange(a, axis, mask)
    bit = (lax.axis_index(axis) // mask) % 2
    n = a.shape[0]
    return lax.dynamic_slice_in_dim(jnp.concatenate([got, a, got]), (1 - bit) * n, 2 * n, 0)


def shards(
    embedded, seq_cotangent, pair_ids, w_qkv, b_qv, w_out, b_out, ln1_gain, ln1_bias, w_in, b_in, w_down, b_down,
    ln2_gain, ln2_bias, w_pool, b_pool,
):
    x = embedded[0]
    tokens, width = x.shape
    sents = tokens // SEQ
    ffn = w_in.shape[1]
    dp = lax.axis_size("dp")
    stream, place_dp = lax.axis_index("stream"), lax.axis_index("dp")
    bits = jnp.stack([stream, place_dp % 2, (place_dp // 2) % 2, (place_dp // 4) % 2]).astype(jnp.int32)
    rows_of = Rows(width, ffn)
    pack = jnp.concatenate(
        [b_qv[:width], jnp.zeros((width,), wide), b_qv[width:], b_out, ln1_gain, ln1_bias, b_in, b_down, ln2_gain, ln2_bias, b_pool]
    ).reshape(1, -1)
    proj, probs, context, hidden, hidden_low, inv_one = attention_forward(x, w_qkv, w_out, pack, rows_of)
    hid3 = hidden.reshape(sents, SEQ, width)
    cot3 = seq_cotangent[0].reshape(sents, SEQ, width)
    enc, act, slope, normed_two, inv_two, first_low = ffn_first(hid3, w_in, w_down, pack, rows_of)
    gathered = first_low
    gate = two = small_up = bin_sum = None
    masks = [1 << i for i in range(dp.bit_length() - 1)]
    for index in range(1, SEQ // GROUP):
        enc, act, gate, two, small_up, bin_sum = ffn_group(
            index, hid3, cot3, w_in, w_down, pack, rows_of, enc, act, gate, two, small_up, bin_sum
        )
    for mask in masks:
        gathered = gather_ordered(gathered, "dp", mask)
    gathered = gather_ordered(gathered, "stream", 1)
    total = sents * dp
    pre_low, grad_w_pool, grad_b_pool = contrastive(gathered.reshape(2, total, width), pair_ids, w_pool, b_pool)
    own_pre = lax.dynamic_slice_in_dim(pre_low, stream * total + place_dp * sents, sents)
    grad_first = trans_right(own_pre, w_pool)
    gate, two, small_up, bin_sum = ffn_first_back(
        cot3, grad_first, normed_two, inv_two, slope, w_down, pack, rows_of, gate, two, small_up, bin_sum
    )
    clock = Clock(small_up)
    act, gate, two = (v.reshape(tokens, -1) for v in (act, gate, two))
    tail = masks[3:]
    down = Reduction(Sources([(act, two)]), [width], bits, clock, tail)
    into = Reduction(Sources([(hidden_low, gate)]), [ffn], bits, clock, tail)
    down.core_send()
    into.core_send()
    down.core_sum()
    state = lower_backward(0, 2, two, gate, hidden, inv_one, proj, probs, w_in, w_out, pack, rows_of, after=clock.now())
    clock.set(state[0])
    into.core_sum()
    down.first_sum()
    state = lower_backward(
        1, 2, two, gate, hidden, inv_one, proj, probs, w_in, w_out, pack, rows_of, before=state, after=clock.now()
    )
    grad_one, grad_proj, small_low, bqv = state
    clock.set(grad_one)
    down.second_sum()
    low_part = Reduction(Sources([(x, grad_proj), (context, grad_one)]), [3 * width, width], bits, clock, tail)
    low_part.core_send()
    into.first_sum()
    down.third_sum()
    small = jnp.concatenate([small_up[:3], bin_sum.reshape(-1, width), small_low[:3], bqv[:2]], 0)
    low_part.core_sum()
    down.last_sum()
    into.second_sum()
    grad_input = input_gradient(grad_proj, w_qkv, grad_one, after=clock.now())
    clock.set(grad_input)
    for axis, mask in [("stream", 1)] + [("dp", m) for m in masks]:
        small = small + exchange(small, axis, mask)
    down.third_back()
    low_part.first_sum()
    into.third_sum()
    down.second_back()
    low_part.second_sum()
    into.last_sum()
    low_part.third_sum()
    into.third_back()
    down.first_back()
    into.second_back()
    low_part.last_sum()
    (out_down,) = down.finish()
    low_part.third_back()
    into.first_back()
    low_part.second_back()
    (out_in,) = into.finish()
    low_part.first_back()
    out_qkv, out_out = low_part.finish()
    n_in = ffn // width
    return (
        enc.reshape(1, tokens, width),
        grad_input[None],
        out_qkv,
        small[6 + n_in : 8 + n_in].reshape(-1),
        out_out,
        small[5 + n_in],
        small[3 + n_in],
        small[4 + n_in],
        out_in,
        small[3 : 3 + n_in].reshape(-1),
        out_down,
        small[2],
        small[0],
        small[1],
        grad_w_pool,
        grad_b_pool,
    )


def solution(mesh):
    sharded = P("stream", "dp", None)
    return jax.shard_map(
        shards,
        mesh=mesh,
        in_specs=(sharded, sharded) + (P(),) * 15,
        out_specs=(sharded, sharded) + (P(),) * 14,
        check_vma=False,
    )
```

```python
import functools
import math

import jax
import jax.numpy as jnp
from jax import lax
from jax.experimental import pallas as pl
from jax.experimental.pallas import tpu as pltpu
from jax.sharding import PartitionSpec as P

HEAD_DIM = 64
SEQ = 64
GROUP = 16
CHUNK = 512

epsilon = 1e-06
score_scale = 10.0
margin_shift = score_scale * 0.3
root_half = 0.7071067811865476
gauss_norm = 0.3989422804014327

low = jnp.bfloat16
wide = jnp.float32
ANY = pl.BlockSpec(memory_space=pl.ANY)
VMEM = pl.BlockSpec(memory_space=pltpu.VMEM)
SMEM = pl.BlockSpec(memory_space=pltpu.SMEM)
HBM = pl.BlockSpec(memory_space=pltpu.HBM)
MIB = 1 << 20


def struct(shape, dtype):
    return jax.ShapeDtypeStruct(shape, dtype)


def call(body, ins, outs, bits=None, scratch=(), aliases=None, after=(), limit=10, far=(), far_out=(), hand_out=(), cost=460):
    first = 0 if bits is None else 1
    ins = [pltpu.with_memory_space_constraint(a, pltpu.HBM) if i in far else a for i, a in enumerate(ins)]

    def wrapped(*refs):
        body(*refs[: first + len(ins)], *refs[first + len(ins) + len(after) :])

    return pl.pallas_call(
        wrapped,
        in_specs=[SMEM] * first + [HBM if i in far else VMEM for i in range(len(ins))] + [ANY] * len(after),
        out_specs=[HBM if i in hand_out else VMEM for i in range(len(outs))],
        out_shape=[(pltpu.HBM if i in far_out or i in hand_out else pltpu.VMEM)(o.shape, o.dtype) for i, o in enumerate(outs)],
        scratch_shapes=list(scratch),
        input_output_aliases={first + k: v for k, v in (aliases or {}).items()},
        cost_estimate=pl.CostEstimate(flops=cost * 2 * 10**8, bytes_accessed=0, transcendentals=0),
        compiler_params=pltpu.CompilerParams(vmem_limit_bytes=limit * MIB),
    )(*([] if bits is None else [bits]), *ins, *after)


def row_of(ref, start=0, size=None):
    return ref[pl.ds(start, ref.shape[0] if size is None else size)].reshape(1, -1)


def mat_mul(a, b):
    return jnp.dot(a, b, preferred_element_type=wide)


def trans_left(a, b):
    return lax.dot_general(a, b, (((0,), (0,)), ((), ())), preferred_element_type=wide)


def trans_right(a, b):
    return lax.dot_general(a, b, (((1,), (1,)), ((), ())), preferred_element_type=wide)


def normalize(h):
    center = h - jnp.mean(h, axis=-1, keepdims=True)
    inv = lax.rsqrt(jnp.mean(center * center, axis=-1, keepdims=True) + epsilon)
    return center * inv, inv


def norm_input_grad(grad, normed, inv):
    return inv * (
        grad
        - jnp.mean(grad, axis=-1, keepdims=True)
        - normed * jnp.mean(grad * normed, axis=-1, keepdims=True)
    )


def split_heads(pair, first):
    zero = jnp.zeros_like(pair)
    return jnp.concatenate([jnp.where(first, pair, zero), jnp.where(first, zero, pair)], axis=0)


def join_heads(rows, first):
    return jnp.where(first, rows[:SEQ], rows[SEQ:])


def attention_forward(bits, x, w_qkv, b_qv, w_out, b_out, gain, bias, later):
    tokens, width = x.shape
    rows = 4 * SEQ
    pairs = width // (2 * HEAD_DIM)
    scale = 1.0 / math.sqrt(HEAD_DIM)

    def body(_bits, *refs):
        n = len(later)
        far, far_later, outs, near_later, near, sems = (
            refs[:7], refs[7 : 7 + n], refs[7 + n : 13 + n], refs[13 + n : 13 + 2 * n], refs[13 + 2 * n : -1], refs[-1]
        )
        proj_ref, prob_ref, ctx_ref, hid_ref, low_ref, inv_ref = outs
        x_ref, wq_ref, bqv_ref, wo_ref, bo_ref, g_ref, b_ref = near
        pairs_of = zip(far + far_later, near + near_later)
        copies = [pltpu.make_async_copy(f, near_f, sems.at[i]) for i, (f, near_f) in enumerate(pairs_of)]
        for copy in copies:
            copy.start()
        for copy in copies[:3]:
            copy.wait()
        first = lax.broadcasted_iota(jnp.int32, (SEQ, 128), 1) < HEAD_DIM
        cols = [slice(p * 128, (p + 1) * 128) for p in range(pairs)]

        @pl.loop(0, tokens // rows)
        def _(step):
            base = pl.multiple_of(step * rows, rows)
            block = pl.ds(base, rows)
            x_in = x_ref[block, :]
            for part in range(3):
                c = slice(part * width, (part + 1) * width)
                value = mat_mul(x_in, wq_ref[:, c])
                if part != 1:
                    value = value + row_of(bqv_ref, (part // 2) * width, width)
                proj_ref[block, c] = value.astype(low)
            for sent in range(4):
                r = pl.ds(pl.multiple_of(base + sent * SEQ, SEQ), SEQ)
                q = proj_ref[r, :width]
                k = proj_ref[r, width : 2 * width]
                v = proj_ref[r, 2 * width :]
                scores = (
                    jnp.concatenate([trans_right(k[:, c], split_heads(q[:, c], first)) for c in cols], axis=1) * scale
                )
                e = jnp.exp(scores - jnp.max(scores, axis=0, keepdims=True))
                probs = (e * (1.0 / jnp.sum(e, axis=0, keepdims=True))).astype(low)
                prob_ref[r, :] = probs
                ctx_ref[r, :] = jnp.concatenate(
                    [join_heads(trans_left(probs[:, c], v[:, c]), first) for c in cols], axis=1
                ).astype(low)

            @pl.when(step == 0)
            def _():
                for copy in copies[3:7]:
                    copy.wait()

            h = x_in.astype(wide) + mat_mul(ctx_ref[block, :], wo_ref[...]) + row_of(bo_ref)
            normed, inv = normalize(h)
            hidden = normed * row_of(g_ref) + row_of(b_ref)
            hid_ref[block, :] = hidden
            low_ref[block, :] = hidden.astype(low)
            inv_ref[block, :] = inv

        for copy in copies[7:]:
            copy.wait()

    return call(
        body,
        [x, w_qkv, b_qv, w_out, b_out, gain, bias] + later,
        [
            struct((tokens, 3 * width), low),
            struct((tokens, width), low),
            struct((tokens, width), low),
            struct((tokens, width), wide),
            struct((tokens, width), low),
            struct((tokens, 1), wide),
        ]
        + [struct(v.shape, v.dtype) for v in later],
        scratch=[pltpu.VMEM(v.shape, v.dtype) for v in (x, w_qkv, b_qv, w_out, b_out, gain, bias)]
        + [pltpu.SemaphoreType.DMA((7 + len(later),))],
        bits=bits,
        far=range(7 + len(later)),
        limit=14,
    )


def ffn_forward_rows(hidden, wi_ref, bi_ref, wd_ref, bd_ref, store_act, store_slope):
    h_low = hidden.astype(low)
    total = hidden + row_of(bd_ref)
    for c in range(0, wi_ref.shape[1], CHUNK):
        u = mat_mul(h_low, wi_ref[:, c : c + CHUNK]) + row_of(bi_ref, c, CHUNK)
        phi = 0.5 + 0.5 * lax.erf(u * root_half)
        act = (u * phi).astype(low)
        store_act(c, act)
        store_slope(c, (phi + u * jnp.exp(-0.5 * u * u) * gauss_norm).astype(low))
        total = total + mat_mul(act, wd_ref[c : c + CHUNK, :])
    return normalize(total)


def ffn_backward_rows(grad_block, normed, inv, gain, wd_ref, slope_of, store_gate, small_ref, bin_ref):
    grad_two = norm_input_grad(grad_block * gain, normed, inv)
    small_ref[0:1, :] += jnp.sum(grad_block * normed, axis=0, keepdims=True)
    small_ref[1:2, :] += jnp.sum(grad_block, axis=0, keepdims=True)
    small_ref[2:3, :] += jnp.sum(grad_two, axis=0, keepdims=True)
    grad_low = grad_two.astype(low)
    for c in range(0, wd_ref.shape[0], CHUNK):
        gate = trans_right(grad_low, wd_ref[c : c + CHUNK, :]) * slope_of(c).astype(wide)
        bin_ref[:, c : c + CHUNK] += jnp.sum(gate, axis=0, keepdims=True)
        store_gate(c, gate.astype(low))
    return grad_low


def ffn_group(index, hidden, cot, upper, state, after=()):
    w_in, b_in, w_down, b_down, gain, bias = upper
    sents, _, width = hidden.shape
    ffn = w_in.shape[1]
    rows = sents * GROUP
    at = slice(index * GROUP, (index + 1) * GROUP)
    first = index == 0
    second = index == 1

    def stores(act_ref, slope_ref):
        def store_act(c, v):
            act_ref[:, at, c : c + CHUNK] = v.reshape(sents, GROUP, CHUNK)

        def store_slope(c, v):
            slope_ref[:, c : c + CHUNK] = v

        return store_act, store_slope

    def forward(h_ref, wi_ref, bi_ref, wd_ref, bd_ref, act_ref, slope_ref):
        return ffn_forward_rows(
            h_ref[:, at, :].reshape(rows, width), wi_ref, bi_ref, wd_ref, bd_ref, *stores(act_ref, slope_ref)
        )

    def body_first(h_ref, wi_ref, bi_ref, wd_ref, bd_ref, g_ref, b_ref, enc_hbm, act_ref, slope_ref, n_ref, inv_ref, first_ref, enc_ref, sem):
        normed, inv = forward(h_ref, wi_ref, bi_ref, wd_ref, bd_ref, act_ref, slope_ref)
        n_ref[...] = normed
        inv_ref[...] = inv
        block = (normed * row_of(g_ref) + row_of(b_ref)).reshape(sents, GROUP, width)
        enc_ref[...] = block.astype(low)
        copy = pltpu.make_async_copy(enc_ref, enc_hbm.at[:, pl.ds(index * GROUP, GROUP), :], sem)
        copy.start()
        first_ref[...] = block[:, 0, :].astype(low)
        copy.wait()

    enc_shape = struct((sents, SEQ, width), low)
    enc_scratch = [pltpu.VMEM((sents, GROUP, width), low), pltpu.SemaphoreType.DMA]
    act_shape = struct((sents, SEQ, ffn), low)
    if first:
        return call(
            body_first,
            [hidden, w_in, b_in, w_down, b_down, gain, bias],
            [
                enc_shape,
                act_shape,
                struct((rows, ffn), low),
                struct((rows, width), wide),
                struct((rows, 1), wide),
                struct((sents, width), low),
            ],
            scratch=enc_scratch,
            hand_out=[0],
        )

    def body(h_ref, cot_ref, wi_ref, bi_ref, wd_ref, bd_ref, g_ref, b_ref, *refs):
        refs = refs[2 if second else 4 :]
        if not second:
            sin_ref, bin_in_ref = refs[:2]
            refs = refs[2:]
        enc_hbm, act_ref, gate_ref, two_ref, small_ref, bin_ref, slope_ref, enc_ref, sem = refs
        small_ref[...] = jnp.zeros_like(small_ref) if second else sin_ref[...]
        bin_ref[...] = jnp.zeros_like(bin_ref) if second else bin_in_ref[...]

        def store_gate(c, v):
            gate_ref[:, at, c : c + CHUNK] = v.reshape(sents, GROUP, CHUNK)

        normed, inv = forward(h_ref, wi_ref, bi_ref, wd_ref, bd_ref, act_ref, slope_ref)
        gain_row = row_of(g_ref)
        enc_ref[...] = (normed * gain_row + row_of(b_ref)).astype(low).reshape(sents, GROUP, width)
        copy = pltpu.make_async_copy(enc_ref, enc_hbm.at[:, pl.ds(index * GROUP, GROUP), :], sem)
        copy.start()
        grad_block = cot_ref[:, at, :].reshape(rows, width).astype(wide)
        got = ffn_backward_rows(
            grad_block, normed, inv, gain_row, wd_ref, lambda c: slope_ref[:, c : c + CHUNK], store_gate, small_ref, bin_ref
        )
        two_ref[:, at, :] = got.reshape(sents, GROUP, width)
        copy.wait()

    aliases = {8: 0, 9: 1}
    if not second:
        aliases.update({10: 2, 11: 3})
    return call(
        body,
        [hidden, cot, w_in, b_in, w_down, b_down, gain, bias] + list(state),
        [enc_shape, act_shape, act_shape, enc_shape, struct((8, width), wide), struct((1, ffn), wide)],
        scratch=[pltpu.VMEM((rows, ffn), low)] + enc_scratch,
        aliases=aliases,
        after=after,
        far=[8],
        hand_out=[0],
    )


def ffn_first_back(cot, grad_first, normed, inv, slope, gain, w_down, gate, two, small, bin_sum):
    sents, _, width = cot.shape
    ffn = w_down.shape[0]
    rows = sents * GROUP
    at = slice(0, GROUP)

    def body(cot_ref, first_ref, n_ref, inv_ref, slope_ref, g_ref, wd_ref, sin_ref, bin_in_ref, _g, _t, gate_ref, two_ref, small_ref, bin_ref):
        small_ref[...] = sin_ref[...]
        bin_ref[...] = bin_in_ref[...]
        position = lax.broadcasted_iota(jnp.int32, (sents, GROUP, width), 1)
        at_first = jnp.broadcast_to(first_ref[...][:, None, :], (sents, GROUP, width))
        grad_block = cot_ref[:, at, :].astype(wide) + jnp.where(position == 0, at_first, 0.0)

        def store_gate(c, v):
            gate_ref[:, at, c : c + CHUNK] = v.reshape(sents, GROUP, CHUNK)

        got = ffn_backward_rows(
            grad_block.reshape(rows, width), n_ref[...], inv_ref[...], row_of(g_ref), wd_ref,
            lambda c: slope_ref[:, c : c + CHUNK], store_gate, small_ref, bin_ref,
        )
        two_ref[:, at, :] = got.reshape(sents, GROUP, width)

    return call(
        body,
        [cot, grad_first, normed, inv, slope, gain, w_down, small, bin_sum, gate, two],
        [struct((sents, SEQ, ffn), low), struct((sents, SEQ, width), low), struct((8, width), wide), struct((1, ffn), wide)],
        aliases={9: 0, 10: 1},
    )


def lower_backward(part, parts, two, gate, hidden, inv, proj, probs, w_in, w_out, gain, bias, before=None, after=()):
    tokens, width = hidden.shape
    ffn = w_in.shape[1]
    rows = 4 * SEQ
    steps = tokens // rows // parts
    pairs = width // (2 * HEAD_DIM)
    scale = 1.0 / math.sqrt(HEAD_DIM)
    fresh = before is None

    def body(two_ref, gate_ref, hid_ref, inv_ref, proj_ref, prob_ref, wi_ref, wo_ref, g_ref, b_ref, *refs):
        if not fresh:
            sin_ref, bin_ref = refs[2:4]
            refs = refs[4:]
        one_ref, gp_ref, small_ref, bqv_ref, ctx_ref = refs
        small_ref[...] = jnp.zeros_like(small_ref) if fresh else sin_ref[...]
        bqv_ref[...] = jnp.zeros_like(bqv_ref) if fresh else bin_ref[...]
        first = lax.broadcasted_iota(jnp.int32, (SEQ, 128), 1) < HEAD_DIM
        cols = [slice(p * 128, (p + 1) * 128) for p in range(pairs)]

        @pl.loop(0, steps)
        def _(step):
            base = pl.multiple_of((step + part * steps) * rows, rows)
            block = pl.ds(base, rows)
            gain_row = row_of(g_ref)
            grad_hidden = two_ref[block, :].astype(wide) + trans_right(gate_ref[block, :], wi_ref[...])
            normed = (hid_ref[block, :] - row_of(b_ref)) * (1.0 / gain_row)
            small_ref[0:1, :] += jnp.sum(grad_hidden * normed, axis=0, keepdims=True)
            small_ref[1:2, :] += jnp.sum(grad_hidden, axis=0, keepdims=True)
            grad_one = norm_input_grad(grad_hidden * gain_row, normed, inv_ref[block, :])
            small_ref[2:3, :] += jnp.sum(grad_one, axis=0, keepdims=True)
            one_low = grad_one.astype(low)
            one_ref[block, :] = one_low
            ctx_ref[...] = trans_right(one_low, wo_ref[...]).astype(low)
            sum_q = jnp.zeros((1, width), wide)
            sum_v = jnp.zeros((1, width), wide)
            for sent in range(4):
                r = pl.ds(pl.multiple_of(base + sent * SEQ, SEQ), SEQ)
                q_all = proj_ref[r, :width]
                k = proj_ref[r, width : 2 * width]
                v = proj_ref[r, 2 * width :]
                d_all = ctx_ref[sent * SEQ : (sent + 1) * SEQ, :]
                p_low = prob_ref[r, :]
                q = [split_heads(q_all[:, c], first) for c in cols]
                d = [split_heads(d_all[:, c], first) for c in cols]
                p = p_low.astype(wide)
                grad_p = jnp.concatenate([trans_right(v[:, c], dd) for c, dd in zip(cols, d)], axis=1)
                grad_v = jnp.concatenate([mat_mul(p_low[:, c], dd) for c, dd in zip(cols, d)], axis=1)
                gp = grad_p * p
                grad_s = (gp - p * jnp.sum(gp, axis=0, keepdims=True)).astype(low)
                grad_k = jnp.concatenate([mat_mul(grad_s[:, c], qq) for c, qq in zip(cols, q)], axis=1) * scale
                grad_q = (
                    jnp.concatenate([join_heads(trans_left(grad_s[:, c], k[:, c]), first) for c in cols], axis=1) * scale
                )
                sum_q += jnp.sum(grad_q, axis=0, keepdims=True)
                sum_v += jnp.sum(grad_v, axis=0, keepdims=True)
                gp_ref[r, :width] = grad_q.astype(low)
                gp_ref[r, width : 2 * width] = grad_k.astype(low)
                gp_ref[r, 2 * width :] = grad_v.astype(low)
            bqv_ref[0:1, :] += sum_q
            bqv_ref[1:2, :] += sum_v

    return call(
        body,
        [two, gate, hidden, inv, proj, probs, w_in, w_out, gain, bias] + ([] if fresh else list(before)),
        [struct((tokens, width), low), struct((tokens, 3 * width), low), struct((8, width), wide), struct((8, width), wide)],
        scratch=[pltpu.VMEM((rows, width), low)],
        aliases=None if fresh else {10: 0, 11: 1},
        after=after,
    )


def input_gradient(grad_proj, w_qkv, grad_one, after=()):
    tokens, width = grad_one.shape
    rows = 4 * SEQ

    def body(gp_ref, w_ref, one_ref, out_ref, token):
        token[...] = jnp.zeros_like(token)

        @pl.loop(0, tokens // rows)
        def _(step):
            block = pl.ds(pl.multiple_of(step * rows, rows), rows)
            out_ref[block, :] = (one_ref[block, :].astype(wide) + trans_right(gp_ref[block, :], w_ref[...])).astype(low)

    return call(
        body, [grad_proj, w_qkv, grad_one], [struct((tokens, width), low), struct((8, 128), wide)], after=after, far_out=[0]
    )


def pooler_gradients(flat, id_column, id_row, w_pool, b_pool):
    total = flat.shape[0] // 2
    pooled = jnp.tanh(mat_mul(flat, w_pool) + b_pool)
    inv_len = lax.rsqrt(jnp.sum(pooled * pooled, axis=-1, keepdims=True) + epsilon)
    unit = pooled * inv_len
    embed = unit.astype(low)
    zero, one = embed[:total], embed[total:]
    square = (total, total)
    eye = (lax.broadcasted_iota(jnp.int32, square, 0) == lax.broadcasted_iota(jnp.int32, square, 1)).astype(wide)
    logits = score_scale * trans_right(zero, one) - margin_shift * eye
    masked = jnp.where(id_column == id_row, logits, -jnp.inf)

    def soft(axis):
        e = jnp.exp(masked - jnp.max(masked, axis=axis, keepdims=True))
        return (score_scale * (e / jnp.sum(e, axis=axis, keepdims=True) - eye)).astype(low)

    by_row, by_col = soft(1), soft(0)
    grad_embed = jnp.concatenate(
        [mat_mul(by_row, one) + mat_mul(by_col, one), trans_left(by_row, zero) + trans_left(by_col, zero)], axis=0
    )
    grad_pre = (
        inv_len * (grad_embed - unit * jnp.sum(unit * grad_embed, axis=-1, keepdims=True)) * (1.0 - pooled * pooled)
    )
    pre_low = grad_pre.astype(low)
    return pre_low, trans_left(flat, pre_low), jnp.sum(grad_pre, axis=0, keepdims=True)


def contrastive(own, got, bits, sents, id_column, id_row, w_pool, b_pool, after):
    total, width = own.shape
    if total > 512:
        start = bits[CORE] * total + bits[PLACE] * sents
        flat = jnp.where(bits[CORE] == 0, jnp.concatenate([own, got]), jnp.concatenate([got, own]))
        pre_low, grad_w, grad_b = pooler_gradients(flat, id_column, id_row, w_pool, b_pool.reshape(1, -1))
        return trans_right(lax.dynamic_slice_in_dim(pre_low, start, sents), w_pool), grad_w, grad_b.reshape(-1)

    def body(b, own_ref, got_ref, col_ref, row_ref, w_ref, b_ref, first_ref, gw_ref, gb_ref, flat_ref, pre_ref):
        flat_ref[pl.ds(pl.multiple_of(b[CORE] * total, total), total), :] = own_ref[...]
        flat_ref[pl.ds(pl.multiple_of((1 - b[CORE]) * total, total), total), :] = got_ref[...]
        pre_low, grad_w, grad_b = pooler_gradients(flat_ref[...], col_ref[...], row_ref[...], w_ref[...], row_of(b_ref))
        pre_ref[...] = pre_low
        gw_ref[...] = grad_w
        gb_ref[...] = grad_b.reshape(-1)
        first_ref[...] = trans_right(pre_ref[pl.ds(pl.multiple_of(b[CORE] * total + b[PLACE] * sents, sents), sents), :], w_ref[...])

    return call(
        body,
        [own, got, id_column, id_row, w_pool, b_pool],
        [struct((sents, width), wide), struct((width, width), wide), struct((width,), wide)],
        bits=bits,
        scratch=[pltpu.VMEM((2 * total, width), low)] * 2,
        after=after,
        far_out=[1, 2],
    )


def put_in_order(blocks, bits, low_bit, after):
    rows, width = blocks[0].shape

    def body(b, *refs):
        me = (b[PLACE] >> low_bit) & (len(blocks) - 1)
        for i, ref in enumerate(refs[:-1]):
            at = pl.multiple_of((me ^ i) * rows, rows)
            refs[-1][pl.ds(at, rows), :] = ref[...]

    return call(
        body, blocks, [struct((rows * len(blocks), width), low)], bits=bits, after=after, limit=8, cost=115
    )[0]


CORE, BIT0, BIT1, BIT2, PLACE = range(5)
SMALL = 16


def exchange(a, axis, mask):
    size = lax.axis_size(axis)
    return lax.ppermute(a, axis, [(i, i ^ mask) for i in range(size)])


class Sources:
    def __init__(self, pairs, small=None):
        self.pairs = pairs
        self.small = small
        self.m = pairs[0][0].shape[1]
        self.n = sum(g.shape[1] for _, g in pairs)
        self.flat = [a for pair in pairs for a in pair]


def gradient_rows(src, bits, recv, after=()):
    m, n = src.m, src.n
    half, quarter = m // 2, m // 4
    count = len(src.flat)
    edge = n // 2

    small = src.small or []
    extra = SMALL if small else 0

    if recv is None:

        def body(b, *refs):
            out = refs[count + len(small)]
            rows = pl.ds(pl.multiple_of((1 - b[CORE]) * half, 128), half)
            at = 0
            for a, g in zip(refs[:count:2], refs[1:count:2]):
                out[:half, at : at + g.shape[1]] = trans_left(a[:, rows], g[...]).astype(low)
                at += g.shape[1]
            if small:
                up, bin_sum, down, bqv = refs[count : count + 4]
                kept = refs[-1]
                width = up.shape[1]
                parts = [up[:3]] + [bin_sum[:, c : c + width] for c in range(0, bin_sum.shape[1], width)] + [down[:3], bqv[:2]]
                parts.append(jnp.zeros((SMALL - sum(p.shape[0] for p in parts), width), wide))
                kept[...] = jnp.concatenate(parts, axis=0).astype(low)
                out[half:, :] = jnp.zeros((SMALL, n), low)
                out[half:, :width] = kept[...]

        shapes = [struct((half + extra, n), low)] + ([struct((SMALL, small[0].shape[1]), low)] if small else [])
        return call(body, src.flat + small, shapes, bits=bits, after=after)

    def body(b, *refs):
        got, left_send, left_keep, right_send, right_keep = refs[-5:]
        rows = pl.ds(pl.multiple_of(b[CORE] * half, 128), half)
        if extra:
            total = (refs[count][...].astype(wide) + got[half:, : refs[count].shape[1]].astype(wide)).astype(low)
            for ref in (left_send, left_keep):
                ref[quarter:, :] = jnp.zeros((SMALL, edge), low)
                ref[quarter:, : total.shape[1]] = total
        for side, bit, send, keep in ((0, BIT0, left_send, left_keep), (1, BIT1, right_send, right_keep)):
            at = 0
            for a, g in zip(refs[:count:2], refs[1:count:2]):
                lo, hi = max(at, side * edge), min(at + g.shape[1], (side + 1) * edge)
                if lo < hi:
                    c = slice(lo - side * edge, hi - side * edge)
                    value = (trans_left(a[:, rows], g[:, lo - at : hi - at]) + got[:half, lo:hi].astype(wide)).astype(low)

                    def put(kept, c=c, value=value, send=send, keep=keep):
                        keep[:quarter, c] = value[kept * quarter : (kept + 1) * quarter]
                        send[:quarter, c] = value[(1 - kept) * quarter : (2 - kept) * quarter]

                    pl.when(b[bit] == 0)(functools.partial(put, 0))
                    pl.when(b[bit] != 0)(functools.partial(put, 1))
                at += g.shape[1]

    shapes = [struct((quarter + e, edge), low) for e in (extra, extra, 0, 0)]
    return call(body, src.flat + ([src.kept] if small else []) + [recv], shapes, bits=bits, after=after)


def part_rows(ref, bit, rows):
    return ref[pl.ds(pl.multiple_of(bit * rows, rows), rows), :].astype(wide)


def whole_call(body, arrays, shapes, bits, after=()):
    return call(body, arrays, [struct(s, low) for s in shapes], bits=bits, after=after, limit=8, cost=115)


def halve_sides(left, left_got, right, right_got, bits, after=()):
    rows, cols = right.shape[0] // 2, right.shape[1]
    extra = left.shape[0] - right.shape[0]

    def body(b, l, lg, r, rg, ls, lk, rs, rk):
        for mine, got, bit, send, keep in ((l, lg, BIT1, ls, lk), (r, rg, BIT0, rs, rk)):
            send[:rows, :] = (part_rows(mine, 1 - b[bit], rows) + part_rows(got, 1 - b[bit], rows)).astype(low)
            keep[:rows, :] = (part_rows(mine, b[bit], rows) + part_rows(got, b[bit], rows)).astype(low)
        if extra:
            total = (l[2 * rows :, :].astype(wide) + lg[2 * rows :, :].astype(wide)).astype(low)
            ls[rows:, :] = total
            lk[rows:, :] = total

    shapes = [(rows + e, cols) for e in (extra, extra, 0, 0)]
    return whole_call(body, [left, left_got, right, right_got], shapes, bits, after)


def halve_both(left, left_got, right, right_got, bits, after=()):
    rows, cols = right.shape[0] // 2, right.shape[1]
    extra = left.shape[0] - right.shape[0]

    def body(b, l, lg, r, rg, send, keep):
        for mine, got, c in ((l, lg, slice(0, cols)), (r, rg, slice(cols, 2 * cols))):
            send[:rows, c] = (part_rows(mine, 1 - b[BIT2], rows) + part_rows(got, 1 - b[BIT2], rows)).astype(low)
            keep[:rows, c] = (part_rows(mine, b[BIT2], rows) + part_rows(got, b[BIT2], rows)).astype(low)
        if extra:
            total = (l[2 * rows :, :].astype(wide) + lg[2 * rows :, :].astype(wide)).astype(low)
            for ref in (send, keep):
                ref[rows:, :cols] = total
                ref[rows:, cols:] = jnp.zeros_like(total)

    return whole_call(body, [left, left_got, right, right_got], [(rows + extra, 2 * cols)] * 2, bits, after)


def add_up(mine, got, bits, after=()):
    def body(b, m, g, out):
        out[...] = (m[...].astype(wide) + g[...].astype(wide)).astype(low)

    return whole_call(body, [mine, got], [mine.shape], bits, after)[0]


def place(out, mine, got, bit, cols=slice(None), rows=None):
    rows = mine.shape[0] if rows is None else rows
    out[pl.ds(pl.multiple_of(bit * rows, rows), rows), :] = mine[:rows, cols]
    out[pl.ds(pl.multiple_of((1 - bit) * rows, rows), rows), :] = got[:rows, cols]


def join_both(mine, got, rows, vectors, bits, after=()):
    cols = mine.shape[1] // 2
    width = vectors[1]

    def body(b, m, g, *refs):
        *outs, left, right = refs
        place(left, m, g, b[BIT2], slice(0, cols), rows)
        place(right, m, g, b[BIT2], slice(cols, 2 * cols), rows)
        at = rows
        for out in outs:
            for c in range(0, out.shape[0], width):
                out[pl.ds(c, width)] = m[at : at + 1, :width].astype(wide).reshape(-1)
                at += 1

    shapes = [struct((v,), wide) for v in vectors[0]] + [struct((2 * rows, cols), low)] * 2
    return call(body, [mine, got], shapes, bits=bits, after=after, limit=8, cost=115, far_out=range(len(vectors[0])))


def join_sides(left, left_got, right, right_got, bits, after=()):
    rows, cols = left.shape

    def body(b, l, lg, r, rg, lo, ro):
        place(lo, l, lg, b[BIT1])
        place(ro, r, rg, b[BIT0])

    return whole_call(body, [left, left_got, right, right_got], [(2 * rows, cols)] * 2, bits, after)


def join_half(left, left_got, right, right_got, bits, after=()):
    rows, cols = left.shape

    def body(b, l, lg, r, rg, out):
        place(out.at[:, pl.ds(0, cols)], l, lg, b[BIT0])
        place(out.at[:, pl.ds(cols, cols)], r, rg, b[BIT1])

    return whole_call(body, [left, left_got, right, right_got], [(2 * rows, 2 * cols)], bits, after)[0]


def widen(source, which, before, widths, bits, after=()):
    half, n = source.shape
    parts = 4
    tile = half // parts

    def body(b, src, *refs):
        refs = refs[0 if before is None else len(before) :]
        outs, token, bufs, sems = refs[: len(widths)], refs[len(widths)], refs[len(widths) + 1 : -1], refs[-1]
        token[...] = jnp.zeros_like(token)
        start = (1 - b[CORE] if which else b[CORE]) * half
        copies = []
        for t in range(parts):
            at = 0
            for out, buf, w in zip(outs, bufs, widths):
                buf[t] = src[t * tile : (t + 1) * tile, at : at + w].astype(wide)
                rows = pl.ds(pl.multiple_of(start + t * tile, tile), tile)
                copies.append(pltpu.make_async_copy(buf.at[t], out.at[rows, :], sems.at[len(copies)]))
                copies[-1].start()
                at += w
        for copy in copies:
            copy.wait()

    return call(
        body,
        [source] + list(before or []),
        [struct((2 * half, w), wide) for w in widths] + [struct((8, 128), wide)],
        bits=bits,
        scratch=[pltpu.VMEM((parts, tile, w), wide) for w in widths] + [pltpu.SemaphoreType.DMA((parts * len(widths),))],
        aliases={1 + i: i for i in range(len(widths))} if before else None,
        after=after,
        far=range(1, 1 + len(widths)) if before else (),
        hand_out=range(len(widths)),
        limit=12,
        cost=115,
    )


class Reduction:
    def __init__(self, src, widths, bits, clock, tail, vectors=()):
        self.vectors = vectors
        self.src, self.widths, self.bits, self.clock, self.tail = src, widths, bits, clock, tail

    def step(self, fn, *args):
        out = fn(*args, after=self.clock.now())
        self.clock.set(out[-1] if isinstance(out, (list, tuple)) else out)
        return out

    def core_send(self):
        send, *kept = self.step(gradient_rows, self.src, self.bits, None)
        if kept:
            self.src.kept = kept[0]
        self.got = exchange(send, "stream", 1)

    def core_sum(self):
        ls, self.l, rs, self.r = self.step(gradient_rows, self.src, self.bits, self.got)
        self.gl, self.gr = exchange(ls, "dp", 1), exchange(rs, "dp", 2)

    def first_sum(self):
        ls, self.l, rs, self.r = self.step(halve_sides, self.l, self.gl, self.r, self.gr, self.bits)
        self.gl, self.gr = exchange(ls, "dp", 2), exchange(rs, "dp", 1)

    def second_sum(self):
        send, self.v = self.step(halve_both, self.l, self.gl, self.r, self.gr, self.bits)
        self.got = exchange(send, "dp", 4)

    def third_sum(self):
        self.v = self.step(add_up, self.v, self.got, self.bits)
        self.got = exchange(self.v, "dp", self.tail[0])

    def last_sum(self):
        for mask in self.tail[1:]:
            self.v = self.step(add_up, self.v, self.got, self.bits)
            self.got = exchange(self.v, "dp", mask)
        self.v = self.step(add_up, self.v, self.got, self.bits)
        self.got = exchange(self.v, "dp", 4)

    def third_back(self):
        vectors = self.vectors, self.src.small[0].shape[1] if self.src.small else None
        *self.sums, self.l, self.r = self.step(join_both, self.v, self.got, self.src.m // 16, vectors, self.bits)
        self.gl, self.gr = exchange(self.l, "dp", 2), exchange(self.r, "dp", 1)

    def second_back(self):
        self.l, self.r = self.step(join_sides, self.l, self.gl, self.r, self.gr, self.bits)
        self.gl, self.gr = exchange(self.l, "dp", 1), exchange(self.r, "dp", 2)

    def first_back(self):
        self.v = self.step(join_half, self.l, self.gl, self.r, self.gr, self.bits)
        self.got = exchange(self.v, "stream", 1)

    def finish_own(self):
        self.out = self.step(widen, self.v, 0, None, self.widths, self.bits)[:-1]

    def finish(self):
        return self.step(widen, self.got, 1, self.out, self.widths, self.bits)[:-1]


class Clock:
    def __init__(self, start):
        self.last = start

    def now(self):
        return (self.last,)

    def set(self, value):
        self.last = value


def shards(
    embedded, seq_cotangent, pair_ids, w_qkv, b_qv, w_out, b_out, ln1_gain, ln1_bias, w_in, b_in, w_down, b_down,
    ln2_gain, ln2_bias, w_pool, b_pool,
):
    x = embedded[0]
    tokens, width = x.shape
    sents = tokens // SEQ
    ffn = w_in.shape[1]
    dp = lax.axis_size("dp")
    stream, place_dp = lax.axis_index("stream"), lax.axis_index("dp")
    bits = jnp.stack([stream, place_dp & 1, (place_dp >> 1) & 1, (place_dp >> 2) & 1, place_dp]).astype(jnp.int32)
    later = [
        w_in, w_down, seq_cotangent[0], w_pool, b_in, b_down, ln2_gain, ln2_bias, b_pool, pair_ids[:, None], pair_ids[None, :]
    ]
    proj, probs, context, hidden, hidden_low, inv_one, *later = attention_forward(
        bits, x, w_qkv, b_qv, w_out, b_out, ln1_gain, ln1_bias, later
    )
    w_in, w_down, cotangent, w_pool, b_in, b_down, ln2_gain, ln2_bias, b_pool, id_column, id_row = later
    hid3 = hidden.reshape(sents, SEQ, width)
    cot3 = cotangent.reshape(sents, SEQ, width)
    upper = (w_in, b_in, w_down, b_down, ln2_gain, ln2_bias)
    enc, act, slope, normed_two, inv_two, first_low = ffn_group(0, hid3, cot3, upper, ())
    masks = [1 << i for i in range(dp.bit_length() - 1)]
    state = [enc, act]
    gathered = first_low
    group = 1
    order = [inv_two]
    for low_bit in range(0, len(masks), 2):
        span = 4 if low_bit + 1 < len(masks) else 2
        blocks = [gathered] + [exchange(gathered, "dp", i << low_bit) for i in range(1, span)]
        if group < SEQ // GROUP:
            state = ffn_group(group, hid3, cot3, upper, state, after=order)
            group += 1
            order = [state[-1]]
        gathered = put_in_order(blocks, bits, low_bit, order)
        order = [gathered]
    other = exchange(gathered, "stream", 1)
    while group < SEQ // GROUP:
        state = ffn_group(group, hid3, cot3, upper, state, after=order)
        group += 1
        order = [state[-1]]
    enc, act, gate, two, small_up, bin_sum = state
    grad_first, grad_w_pool, grad_b_pool = contrastive(
        gathered, other, bits, sents, id_column, id_row, w_pool, b_pool, order
    )
    gate, two, small_up, bin_sum = ffn_first_back(
        cot3, grad_first, normed_two, inv_two, slope, ln2_gain, w_down, gate, two, small_up, bin_sum
    )
    clock = Clock(small_up)
    act, gate, two = (v.reshape(tokens, -1) for v in (act, gate, two))
    tail = masks[3:]
    down = Reduction(Sources([(act, two)]), [width], bits, clock, tail)
    into = Reduction(Sources([(hidden_low, gate)]), [ffn], bits, clock, tail)
    down.core_send()
    into.core_send()
    down.core_sum()
    lower = (two, gate, hidden, inv_one, proj, probs, w_in, w_out, ln1_gain, ln1_bias)
    state = lower_backward(0, 2, *lower, after=clock.now())
    clock.set(state[-1])
    state = lower_backward(1, 2, *lower, before=state, after=clock.now())
    grad_one, grad_proj, small_low, bqv = state
    clock.set(bqv)
    down.first_sum()
    into.core_sum()
    low_part = Reduction(
        Sources([(x, grad_proj), (context, grad_one)], [small_up, bin_sum, small_low, bqv]),
        [3 * width, width],
        bits,
        clock,
        tail,
        (width, width, width, ffn, width, width, width, 2 * width),
    )
    down.second_sum()
    low_part.core_send()
    down.third_sum()
    into.first_sum()
    low_part.core_sum()
    into.second_sum()
    down.last_sum()
    grad_input, token = input_gradient(grad_proj, w_qkv, grad_one, after=clock.now())
    clock.set(token)
    low_part.first_sum()
    into.third_sum()
    down.third_back()
    low_part.second_sum()
    down.second_back()
    into.last_sum()
    low_part.third_sum()
    into.third_back()
    down.first_back()
    down.finish_own()
    into.second_back()
    low_part.last_sum()
    (out_down,) = down.finish()
    low_part.third_back()
    into.first_back()
    into.finish_own()
    low_part.second_back()
    (out_in,) = into.finish()
    low_part.first_back()
    low_part.finish_own()
    out_qkv, out_out = low_part.finish()
    g_ln2_gain, g_ln2_bias, g_b_down, g_b_in, g_ln1_gain, g_ln1_bias, g_b_out, g_b_qv = low_part.sums
    return (
        enc.reshape(1, tokens, width),
        grad_input[None],
        out_qkv,
        g_b_qv,
        out_out,
        g_b_out,
        g_ln1_gain,
        g_ln1_bias,
        out_in,
        g_b_in,
        out_down,
        g_b_down,
        g_ln2_gain,
        g_ln2_bias,
        grad_w_pool,
        grad_b_pool,
    )


def solution(mesh):
    sharded = P("stream", "dp", None)
    return jax.shard_map(
        shards,
        mesh=mesh,
        in_specs=(sharded, sharded) + (P(),) * 15,
        out_specs=(sharded, sharded) + (P(),) * 14,
        check_vma=False,
    )
```

```python
import functools
import math

import jax
import jax.numpy as jnp
from jax import lax
from jax.experimental import pallas as pl
from jax.experimental.pallas import tpu as pltpu
from jax.sharding import PartitionSpec as P

HEAD_DIM = 64
SEQ = 64
GROUP = 16
CHUNK = 512

epsilon = 1e-06
score_scale = 10.0
margin_shift = score_scale * 0.3
root_half = 0.7071067811865476
gauss_norm = 0.3989422804014327

low = jnp.bfloat16
wide = jnp.float32
ANY = pl.BlockSpec(memory_space=pl.ANY)
VMEM = pl.BlockSpec(memory_space=pltpu.VMEM)
SMEM = pl.BlockSpec(memory_space=pltpu.SMEM)
HBM = pl.BlockSpec(memory_space=pltpu.HBM)
MIB = 1 << 20


def struct(shape, dtype):
    return jax.ShapeDtypeStruct(shape, dtype)


def call(body, ins, outs, bits=None, scratch=(), aliases=None, after=(), limit=10, far=(), far_out=(), hand_out=(), cost=460):
    first = 0 if bits is None else 1
    ins = [pltpu.with_memory_space_constraint(a, pltpu.HBM) if i in far else a for i, a in enumerate(ins)]

    def wrapped(*refs):
        body(*refs[: first + len(ins)], *refs[first + len(ins) + len(after) :])

    return pl.pallas_call(
        wrapped,
        in_specs=[SMEM] * first + [HBM if i in far else VMEM for i in range(len(ins))] + [ANY] * len(after),
        out_specs=[HBM if i in hand_out else VMEM for i in range(len(outs))],
        out_shape=[(pltpu.HBM if i in far_out or i in hand_out else pltpu.VMEM)(o.shape, o.dtype) for i, o in enumerate(outs)],
        scratch_shapes=list(scratch),
        input_output_aliases={first + k: v for k, v in (aliases or {}).items()},
        cost_estimate=pl.CostEstimate(flops=cost * 10**8, bytes_accessed=0, transcendentals=0),
        compiler_params=pltpu.CompilerParams(vmem_limit_bytes=limit * MIB),
    )(*([] if bits is None else [bits]), *ins, *after)


def row_of(ref, start=0, size=None):
    return ref[pl.ds(start, ref.shape[0] if size is None else size)].reshape(1, -1)


def mat_mul(a, b):
    return jnp.dot(a, b, preferred_element_type=wide)


def trans_left(a, b):
    return lax.dot_general(a, b, (((0,), (0,)), ((), ())), preferred_element_type=wide)


def trans_right(a, b):
    return lax.dot_general(a, b, (((1,), (1,)), ((), ())), preferred_element_type=wide)


def normalize(h):
    center = h - jnp.mean(h, axis=-1, keepdims=True)
    inv = lax.rsqrt(jnp.mean(center * center, axis=-1, keepdims=True) + epsilon)
    return center * inv, inv


def norm_input_grad(grad, normed, inv):
    return inv * (
        grad
        - jnp.mean(grad, axis=-1, keepdims=True)
        - normed * jnp.mean(grad * normed, axis=-1, keepdims=True)
    )


def split_heads(pair, first):
    zero = jnp.zeros_like(pair)
    return jnp.concatenate([jnp.where(first, pair, zero), jnp.where(first, zero, pair)], axis=0)


def join_heads(rows, first):
    return jnp.where(first, rows[:SEQ], rows[SEQ:])


def heads_product(left, right, cols, first):
    zero = jnp.zeros_like(right[0][:, cols[0]])
    out = ([], [])
    for c in cols:
        both = jnp.concatenate([left[0][:, c], left[1][:, c]], axis=0)
        apart = jnp.concatenate(
            [jnp.concatenate([right[0][:, c], zero], axis=1), jnp.concatenate([zero, right[1][:, c]], axis=1)], axis=0
        )
        rows = trans_left(both, apart)
        for i in range(2):
            out[i].append(join_heads(rows[:, i * 128 : (i + 1) * 128], first))
    return [jnp.concatenate(o, axis=1) for o in out]


def attention_forward(bits, x, w_qkv, b_qv, w_out, b_out, gain, bias, later):
    tokens, width = x.shape
    rows = 4 * SEQ
    pairs = width // (2 * HEAD_DIM)
    scale = 1.0 / math.sqrt(HEAD_DIM)

    def body(_bits, *refs):
        n = len(later)
        far, far_later, outs, near_later, near, sems = (
            refs[:7], refs[7 : 7 + n], refs[7 + n : 13 + n], refs[13 + n : 13 + 2 * n], refs[13 + 2 * n : -1], refs[-1]
        )
        proj_ref, prob_ref, ctx_ref, hid_ref, low_ref, inv_ref = outs
        x_ref, wq_ref, bqv_ref, wo_ref, bo_ref, g_ref, b_ref = near
        pairs_of = zip(far + far_later, near + near_later)
        copies = [pltpu.make_async_copy(f, near_f, sems.at[i]) for i, (f, near_f) in enumerate(pairs_of)]
        for copy in copies[:3]:
            copy.start()
        for copy in copies[:3]:
            copy.wait()
        for copy in copies[3:]:
            copy.start()
        first = lax.broadcasted_iota(jnp.int32, (SEQ, 128), 1) < HEAD_DIM
        cols = [slice(p * 128, (p + 1) * 128) for p in range(pairs)]

        for part in range(3):
            c = slice(part * width, (part + 1) * width)
            value = mat_mul(x_ref[...], wq_ref[:, c])
            if part != 1:
                value = value + row_of(bqv_ref, (part // 2) * width, width)
            proj_ref[:, c] = value.astype(low)

        @pl.loop(0, tokens // rows)
        def _(step):
            base = step * rows
            for two in range(2):
                at = [pl.ds(pl.multiple_of(base + (2 * two + i) * SEQ, SEQ), SEQ) for i in range(2)]
                probs = []
                for r in at:
                    q = proj_ref[r, :width]
                    k = proj_ref[r, width : 2 * width]
                    scores = (
                        jnp.concatenate([trans_right(k[:, c], split_heads(q[:, c], first)) for c in cols], axis=1) * scale
                    )
                    e = jnp.exp(scores - jnp.max(scores, axis=0, keepdims=True))
                    probs.append((e * (1.0 / jnp.sum(e, axis=0, keepdims=True))).astype(low))
                    prob_ref[r, :] = probs[-1]
                values = [proj_ref[r, 2 * width :] for r in at]
                for r, context in zip(at, heads_product(probs, values, cols, first)):
                    ctx_ref[r, :] = context.astype(low)

        for copy in copies[3:7]:
            copy.wait()

        for start in range(0, tokens, tokens // 2):
            block = slice(start, start + tokens // 2)
            h = x_ref[block, :].astype(wide) + mat_mul(ctx_ref[block, :], wo_ref[...]) + row_of(bo_ref)
            normed, inv = normalize(h)
            hidden = normed * row_of(g_ref) + row_of(b_ref)
            hid_ref[block, :] = hidden
            low_ref[block, :] = hidden.astype(low)
            inv_ref[block, :] = inv

        for copy in copies[7:]:
            copy.wait()

    return call(
        body,
        [x, w_qkv, b_qv, w_out, b_out, gain, bias] + later,
        [
            struct((tokens, 3 * width), low),
            struct((tokens, width), low),
            struct((tokens, width), low),
            struct((tokens, width), wide),
            struct((tokens, width), low),
            struct((tokens, 1), wide),
        ]
        + [struct(v.shape, v.dtype) for v in later],
        scratch=[pltpu.VMEM(v.shape, v.dtype) for v in (x, w_qkv, b_qv, w_out, b_out, gain, bias)]
        + [pltpu.SemaphoreType.DMA((7 + len(later),))],
        bits=bits,
        far=range(7 + len(later)),
        limit=14,
    )


def ffn_forward_rows(hidden, wi_ref, bi_ref, wd_ref, bd_ref, store_act, store_gate_in):
    h_low = hidden.astype(low)
    total = hidden + row_of(bd_ref)
    for c in range(0, wi_ref.shape[1], CHUNK):
        u = mat_mul(h_low, wi_ref[:, c : c + CHUNK]) + row_of(bi_ref, c, CHUNK)
        phi = 0.5 + 0.5 * lax.erf(u * root_half)
        act = (u * phi).astype(low)
        store_act(c, act)
        store_gate_in(c, u.astype(low), phi.astype(low))
        total = total + mat_mul(act, wd_ref[c : c + CHUNK, :])
    return normalize(total)


def ffn_backward_rows(grad_block, normed, inv, gain, wd_ref, gate_in, store_gate, small_ref, bin_ref):
    grad_two = norm_input_grad(grad_block * gain, normed, inv)
    small_ref[0:1, :] += jnp.sum(grad_block * normed, axis=0, keepdims=True)
    small_ref[1:2, :] += jnp.sum(grad_block, axis=0, keepdims=True)
    small_ref[2:3, :] += jnp.sum(grad_two, axis=0, keepdims=True)
    grad_low = grad_two.astype(low)
    for c in range(0, wd_ref.shape[0], CHUNK):
        u, phi = gate_in(c)
        slope = phi + u * jnp.exp(u * u * low(-0.5)) * low(gauss_norm)
        gate = trans_right(grad_low, wd_ref[c : c + CHUNK, :]) * slope.astype(wide)
        bin_ref[:, c : c + CHUNK] += jnp.sum(gate, axis=0, keepdims=True)
        store_gate(c, gate.astype(low))
    return grad_low


def ffn_group(index, hidden, cot, upper, state, after=()):
    w_in, b_in, w_down, b_down, gain, bias = upper
    sents, _, width = hidden.shape
    ffn = w_in.shape[1]
    rows = sents * GROUP
    at = slice(index * GROUP, (index + 1) * GROUP)
    first = index == 0
    second = index == 1

    def stores(act_ref, u_ref, phi_ref):
        def store_act(c, v):
            act_ref[:, at, c : c + CHUNK] = v.reshape(sents, GROUP, CHUNK)

        def store_gate_in(c, u, phi):
            u_ref[:, c : c + CHUNK] = u
            phi_ref[:, c : c + CHUNK] = phi

        return store_act, store_gate_in

    def forward(h_ref, wi_ref, bi_ref, wd_ref, bd_ref, act_ref, u_ref, phi_ref):
        return ffn_forward_rows(
            h_ref[:, at, :].reshape(rows, width), wi_ref, bi_ref, wd_ref, bd_ref, *stores(act_ref, u_ref, phi_ref)
        )

    def body_first(h_ref, wi_ref, bi_ref, wd_ref, bd_ref, g_ref, b_ref, enc_hbm, act_ref, u_ref, phi_ref, n_ref, inv_ref, first_ref, enc_ref, sem):
        normed, inv = forward(h_ref, wi_ref, bi_ref, wd_ref, bd_ref, act_ref, u_ref, phi_ref)
        n_ref[...] = normed
        inv_ref[...] = inv
        block = (normed * row_of(g_ref) + row_of(b_ref)).reshape(sents, GROUP, width)
        enc_ref[...] = block.astype(low)
        copy = pltpu.make_async_copy(enc_ref, enc_hbm.at[:, pl.ds(index * GROUP, GROUP), :], sem)
        copy.start()
        first_ref[...] = block[:, 0, :].astype(low)
        copy.wait()

    enc_shape = struct((sents, SEQ, width), low)
    enc_scratch = [pltpu.VMEM((sents, GROUP, width), low), pltpu.SemaphoreType.DMA]
    act_shape = struct((sents, SEQ, ffn), low)
    if first:
        return call(
            body_first,
            [hidden, w_in, b_in, w_down, b_down, gain, bias],
            [
                enc_shape,
                act_shape,
                struct((rows, ffn), low),
                struct((rows, ffn), low),
                struct((rows, width), wide),
                struct((rows, 1), wide),
                struct((sents, width), low),
            ],
            scratch=enc_scratch,
            hand_out=[0],
        )

    def body(h_ref, cot_ref, wi_ref, bi_ref, wd_ref, bd_ref, g_ref, b_ref, *refs):
        refs = refs[2 if second else 4 :]
        if not second:
            sin_ref, bin_in_ref = refs[:2]
            refs = refs[2:]
        enc_hbm, act_ref, gate_ref, two_ref, small_ref, bin_ref, u_ref, phi_ref, enc_ref, sem = refs
        small_ref[...] = jnp.zeros_like(small_ref) if second else sin_ref[...]
        bin_ref[...] = jnp.zeros_like(bin_ref) if second else bin_in_ref[...]

        def store_gate(c, v):
            gate_ref[:, at, c : c + CHUNK] = v.reshape(sents, GROUP, CHUNK)

        normed, inv = forward(h_ref, wi_ref, bi_ref, wd_ref, bd_ref, act_ref, u_ref, phi_ref)
        gain_row = row_of(g_ref)
        enc_ref[...] = (normed * gain_row + row_of(b_ref)).astype(low).reshape(sents, GROUP, width)
        copy = pltpu.make_async_copy(enc_ref, enc_hbm.at[:, pl.ds(index * GROUP, GROUP), :], sem)
        copy.start()
        grad_block = cot_ref[:, at, :].reshape(rows, width).astype(wide)
        got = ffn_backward_rows(
            grad_block, normed, inv, gain_row, wd_ref, lambda c: (u_ref[:, c : c + CHUNK], phi_ref[:, c : c + CHUNK]),
            store_gate, small_ref, bin_ref,
        )
        two_ref[:, at, :] = got.reshape(sents, GROUP, width)
        copy.wait()

    aliases = {8: 0, 9: 1}
    if not second:
        aliases.update({10: 2, 11: 3})
    return call(
        body,
        [hidden, cot, w_in, b_in, w_down, b_down, gain, bias] + list(state),
        [enc_shape, act_shape, act_shape, enc_shape, struct((8, width), wide), struct((1, ffn), wide)],
        scratch=[pltpu.VMEM((rows, ffn), low)] * 2 + enc_scratch,
        aliases=aliases,
        after=after,
        far=[8],
        hand_out=[0],
    )


def ffn_first_back(cot, grad_first, normed, inv, gate_in, phi, gain, w_down, gate, two, small, bin_sum):
    sents, _, width = cot.shape
    ffn = w_down.shape[0]
    rows = sents * GROUP
    at = slice(0, GROUP)

    def body(cot_ref, first_ref, n_ref, inv_ref, u_ref, phi_ref, g_ref, wd_ref, sin_ref, bin_in_ref, _g, _t, gate_ref, two_ref, small_ref, bin_ref):
        small_ref[...] = sin_ref[...]
        bin_ref[...] = bin_in_ref[...]
        position = lax.broadcasted_iota(jnp.int32, (sents, GROUP, width), 1)
        at_first = jnp.broadcast_to(first_ref[...][:, None, :], (sents, GROUP, width))
        grad_block = cot_ref[:, at, :].astype(wide) + jnp.where(position == 0, at_first, 0.0)

        def store_gate(c, v):
            gate_ref[:, at, c : c + CHUNK] = v.reshape(sents, GROUP, CHUNK)

        got = ffn_backward_rows(
            grad_block.reshape(rows, width), n_ref[...], inv_ref[...], row_of(g_ref), wd_ref,
            lambda c: (u_ref[:, c : c + CHUNK], phi_ref[:, c : c + CHUNK]), store_gate, small_ref, bin_ref,
        )
        two_ref[:, at, :] = got.reshape(sents, GROUP, width)

    return call(
        body,
        [cot, grad_first, normed, inv, gate_in, phi, gain, w_down, small, bin_sum, gate, two],
        [struct((sents, SEQ, ffn), low), struct((sents, SEQ, width), low), struct((8, width), wide), struct((1, ffn), wide)],
        aliases={10: 0, 11: 1},
    )


def lower_backward(part, parts, two, gate, hidden, inv, proj, probs, w_in, w_out, gain, bias, before=None, after=()):
    tokens, width = hidden.shape
    ffn = w_in.shape[1]
    rows = 4 * SEQ
    steps = tokens // rows // parts
    pairs = width // (2 * HEAD_DIM)
    scale = 1.0 / math.sqrt(HEAD_DIM)
    fresh = before is None

    def body(two_ref, gate_ref, hid_ref, inv_ref, proj_ref, prob_ref, wi_ref, wo_ref, g_ref, b_ref, *refs):
        if not fresh:
            sin_ref, bin_ref = refs[2:4]
            refs = refs[4:]
        one_ref, gp_ref, small_ref, bqv_ref, ctx_ref = refs
        small_ref[...] = jnp.zeros_like(small_ref) if fresh else sin_ref[...]
        bqv_ref[...] = jnp.zeros_like(bqv_ref) if fresh else bin_ref[...]
        first = lax.broadcasted_iota(jnp.int32, (SEQ, 128), 1) < HEAD_DIM
        cols = [slice(p * 128, (p + 1) * 128) for p in range(pairs)]

        block = slice(part * steps * rows, (part + 1) * steps * rows)
        gain_row = row_of(g_ref)
        grad_hidden = two_ref[block, :].astype(wide) + trans_right(gate_ref[block, :], wi_ref[...])
        normed = (hid_ref[block, :] - row_of(b_ref)) * (1.0 / gain_row)
        small_ref[0:1, :] += jnp.sum(grad_hidden * normed, axis=0, keepdims=True)
        small_ref[1:2, :] += jnp.sum(grad_hidden, axis=0, keepdims=True)
        grad_one = norm_input_grad(grad_hidden * gain_row, normed, inv_ref[block, :])
        small_ref[2:3, :] += jnp.sum(grad_one, axis=0, keepdims=True)
        one_ref[block, :] = grad_one.astype(low)
        ctx_ref[...] = trans_right(one_ref[block, :], wo_ref[...]).astype(low)

        @pl.loop(0, steps)
        def _(step):
            base = step * rows + part * steps * rows
            sum_q = jnp.zeros((1, width), wide)
            sum_v = jnp.zeros((1, width), wide)
            for two in range(2):
                at = [pl.ds(pl.multiple_of(base + (2 * two + i) * SEQ, SEQ), SEQ) for i in range(2)]
                grads = []
                for i, r in enumerate(at):
                    q_all = proj_ref[r, :width]
                    v = proj_ref[r, 2 * width :]
                    d_all = ctx_ref[pl.ds(pl.multiple_of(step * rows + (2 * two + i) * SEQ, SEQ), SEQ), :]
                    p_low = prob_ref[r, :]
                    q = [split_heads(q_all[:, c], first) for c in cols]
                    d = [split_heads(d_all[:, c], first) for c in cols]
                    p = p_low.astype(wide)
                    grad_p = jnp.concatenate([trans_right(v[:, c], dd) for c, dd in zip(cols, d)], axis=1)
                    grad_v = jnp.concatenate([mat_mul(p_low[:, c], dd) for c, dd in zip(cols, d)], axis=1)
                    gp = grad_p * p
                    grad_s = (gp - p * jnp.sum(gp, axis=0, keepdims=True)).astype(low)
                    grad_k = jnp.concatenate([mat_mul(grad_s[:, c], qq) for c, qq in zip(cols, q)], axis=1) * scale
                    sum_v += jnp.sum(grad_v, axis=0, keepdims=True)
                    gp_ref[r, width : 2 * width] = grad_k.astype(low)
                    gp_ref[r, 2 * width :] = grad_v.astype(low)
                    grads.append(grad_s)
                keys = [proj_ref[r, width : 2 * width] for r in at]
                for r, product in zip(at, heads_product(grads, keys, cols, first)):
                    grad_q = product * scale
                    sum_q += jnp.sum(grad_q, axis=0, keepdims=True)
                    gp_ref[r, :width] = grad_q.astype(low)
            bqv_ref[0:1, :] += sum_q
            bqv_ref[1:2, :] += sum_v

    return call(
        body,
        [two, gate, hidden, inv, proj, probs, w_in, w_out, gain, bias] + ([] if fresh else list(before)),
        [struct((tokens, width), low), struct((tokens, 3 * width), low), struct((8, width), wide), struct((8, width), wide)],
        scratch=[pltpu.VMEM((rows * steps, width), low)],
        aliases=None if fresh else {10: 0, 11: 1},
        after=after,
    )


def input_gradient(grad_proj, w_qkv, grad_one, after=()):
    tokens, width = grad_one.shape
    rows = tokens // 2

    def body(gp_ref, w_ref, one_ref, out_ref, token):
        token[...] = jnp.zeros_like(token)

        for start in range(0, tokens, rows):
            block = slice(start, start + rows)
            out_ref[block, :] = (one_ref[block, :].astype(wide) + trans_right(gp_ref[block, :], w_ref[...])).astype(low)

    return call(
        body, [grad_proj, w_qkv, grad_one], [struct((tokens, width), low), struct((8, 128), wide)], after=after, far_out=[0]
    )


def pooler_gradients(flat, id_row, w_pool, b_pool):
    total = flat.shape[0] // 2
    pooled = jnp.tanh(mat_mul(flat, w_pool) + b_pool)
    inv_len = lax.rsqrt(jnp.sum(pooled * pooled, axis=-1, keepdims=True) + epsilon)
    unit = pooled * inv_len
    embed = unit.astype(low)
    zero, one = embed[:total], embed[total:]
    square = (total, total)
    eye = (lax.broadcasted_iota(jnp.int32, square, 0) == lax.broadcasted_iota(jnp.int32, square, 1)).astype(wide)
    logits = score_scale * trans_right(zero, one) - margin_shift * eye
    id_column = jnp.sum(jnp.where(eye > 0, id_row, 0), axis=1, keepdims=True)
    masked = jnp.where(id_column == id_row, logits, -jnp.inf)

    def soft(axis):
        e = jnp.exp(masked - jnp.max(masked, axis=axis, keepdims=True))
        return (score_scale * (e / jnp.sum(e, axis=axis, keepdims=True) - eye)).astype(low)

    by_row, by_col = soft(1), soft(0)
    grad_embed = jnp.concatenate(
        [mat_mul(by_row, one) + mat_mul(by_col, one), trans_left(by_row, zero) + trans_left(by_col, zero)], axis=0
    )
    grad_pre = (
        inv_len * (grad_embed - unit * jnp.sum(unit * grad_embed, axis=-1, keepdims=True)) * (1.0 - pooled * pooled)
    )
    pre_low = grad_pre.astype(low)
    return pre_low, trans_left(flat, pre_low), jnp.sum(grad_pre, axis=0, keepdims=True)


def contrastive(own, got, bits, sents, ids, w_pool, b_pool, after):
    total, width = own.shape
    if total > 512:
        start = bits[CORE] * total + bits[PLACE] * sents
        flat = jnp.where(bits[CORE] == 0, jnp.concatenate([own, got]), jnp.concatenate([got, own]))
        pre_low, grad_w, grad_b = pooler_gradients(flat, ids.reshape(1, -1), w_pool, b_pool.reshape(1, -1))
        return trans_right(lax.dynamic_slice_in_dim(pre_low, start, sents), w_pool), grad_w, grad_b.reshape(-1)

    def body(b, own_ref, got_ref, ids_ref, w_ref, b_ref, first_ref, gw_ref, gb_ref, flat_ref, pre_ref):
        flat_ref[pl.ds(pl.multiple_of(b[CORE] * total, total), total), :] = own_ref[...]
        flat_ref[pl.ds(pl.multiple_of((1 - b[CORE]) * total, total), total), :] = got_ref[...]
        pre_low, grad_w, grad_b = pooler_gradients(flat_ref[...], row_of(ids_ref), w_ref[...], row_of(b_ref))
        pre_ref[...] = pre_low
        gw_ref[...] = grad_w
        gb_ref[...] = grad_b.reshape(-1)
        first_ref[...] = trans_right(pre_ref[pl.ds(pl.multiple_of(b[CORE] * total + b[PLACE] * sents, sents), sents), :], w_ref[...])

    return call(
        body,
        [own, got, ids, w_pool, b_pool],
        [struct((sents, width), wide), struct((width, width), wide), struct((width,), wide)],
        bits=bits,
        scratch=[pltpu.VMEM((2 * total, width), low)] * 2,
        after=after,
        far_out=[1, 2],
    )


def put_in_order(blocks, bits, low_bit, after):
    rows, width = blocks[0].shape

    def body(b, *refs):
        me = (b[PLACE] >> low_bit) & (len(blocks) - 1)
        for i, ref in enumerate(refs[:-1]):
            at = pl.multiple_of((me ^ i) * rows, rows)
            refs[-1][pl.ds(at, rows), :] = ref[...]

    return call(
        body, blocks, [struct((rows * len(blocks), width), low)], bits=bits, after=after, limit=8, cost=115
    )[0]


CORE, BIT0, BIT1, BIT2, PLACE = range(5)
SMALL = 16


def exchange(a, axis, mask):
    size = lax.axis_size(axis)
    return lax.ppermute(a, axis, [(i, i ^ mask) for i in range(size)])


class Sources:
    def __init__(self, pairs, small=None):
        self.pairs = pairs
        self.small = small
        self.m = pairs[0][0].shape[1]
        self.n = sum(g.shape[1] for _, g in pairs)
        self.flat = [a for pair in pairs for a in pair]


def gradient_rows(src, bits, recv, after=()):
    m, n = src.m, src.n
    half, quarter = m // 2, m // 4
    count = len(src.flat)
    edge = n // 2

    small = src.small or []
    extra = SMALL if small else 0

    if recv is None:

        def body(b, *refs):
            out = refs[count + len(small)]
            rows = pl.ds(pl.multiple_of((1 - b[CORE]) * half, 128), half)
            at = 0
            for a, g in zip(refs[:count:2], refs[1:count:2]):
                out[:half, at : at + g.shape[1]] = trans_left(a[:, rows], g[...]).astype(low)
                at += g.shape[1]
            if small:
                up, bin_sum, down, bqv = refs[count : count + 4]
                kept = refs[-1]
                width = up.shape[1]
                parts = [up[:3]] + [bin_sum[:, c : c + width] for c in range(0, bin_sum.shape[1], width)] + [down[:3], bqv[:2]]
                parts.append(jnp.zeros((SMALL - sum(p.shape[0] for p in parts), width), wide))
                kept[...] = jnp.concatenate(parts, axis=0).astype(low)
                out[half:, :] = jnp.zeros((SMALL, n), low)
                out[half:, :width] = kept[...]

        shapes = [struct((half + extra, n), low)] + ([struct((SMALL, small[0].shape[1]), low)] if small else [])
        return call(body, src.flat + small, shapes, bits=bits, after=after)

    def body(b, *refs):
        got, left_send, left_keep, right_send, right_keep = refs[-5:]
        rows = pl.ds(pl.multiple_of(b[CORE] * half, 128), half)
        if extra:
            total = (refs[count][...].astype(wide) + got[half:, : refs[count].shape[1]].astype(wide)).astype(low)
            for ref in (left_send, left_keep):
                ref[quarter:, :] = jnp.zeros((SMALL, edge), low)
                ref[quarter:, : total.shape[1]] = total
        for side, bit, send, keep in ((0, BIT0, left_send, left_keep), (1, BIT1, right_send, right_keep)):
            at = 0
            for a, g in zip(refs[:count:2], refs[1:count:2]):
                lo, hi = max(at, side * edge), min(at + g.shape[1], (side + 1) * edge)
                if lo < hi:
                    c = slice(lo - side * edge, hi - side * edge)
                    value = (trans_left(a[:, rows], g[:, lo - at : hi - at]) + got[:half, lo:hi].astype(wide)).astype(low)

                    def put(kept, c=c, value=value, send=send, keep=keep):
                        keep[:quarter, c] = value[kept * quarter : (kept + 1) * quarter]
                        send[:quarter, c] = value[(1 - kept) * quarter : (2 - kept) * quarter]

                    pl.when(b[bit] == 0)(functools.partial(put, 0))
                    pl.when(b[bit] != 0)(functools.partial(put, 1))
                at += g.shape[1]

    shapes = [struct((quarter + e, edge), low) for e in (extra, extra, 0, 0)]
    return call(body, src.flat + ([src.kept] if small else []) + [recv], shapes, bits=bits, after=after)


def part_rows(ref, bit, rows):
    return ref[pl.ds(pl.multiple_of(bit * rows, rows), rows), :].astype(wide)


def whole_call(body, arrays, shapes, bits, after=()):
    return call(body, arrays, [struct(s, low) for s in shapes], bits=bits, after=after, limit=8, cost=115)


def halve_sides(left, left_got, right, right_got, bits, after=()):
    rows, cols = right.shape[0] // 2, right.shape[1]
    extra = left.shape[0] - right.shape[0]

    def body(b, l, lg, r, rg, ls, lk, rs, rk):
        for mine, got, bit, send, keep in ((l, lg, BIT1, ls, lk), (r, rg, BIT0, rs, rk)):
            send[:rows, :] = (part_rows(mine, 1 - b[bit], rows) + part_rows(got, 1 - b[bit], rows)).astype(low)
            keep[:rows, :] = (part_rows(mine, b[bit], rows) + part_rows(got, b[bit], rows)).astype(low)
        if extra:
            total = (l[2 * rows :, :].astype(wide) + lg[2 * rows :, :].astype(wide)).astype(low)
            ls[rows:, :] = total
            lk[rows:, :] = total

    shapes = [(rows + e, cols) for e in (extra, extra, 0, 0)]
    return whole_call(body, [left, left_got, right, right_got], shapes, bits, after)


def halve_both(left, left_got, right, right_got, bits, after=()):
    rows, cols = right.shape[0] // 2, right.shape[1]
    extra = left.shape[0] - right.shape[0]

    def body(b, l, lg, r, rg, send, keep):
        for mine, got, c in ((l, lg, slice(0, cols)), (r, rg, slice(cols, 2 * cols))):
            send[:rows, c] = (part_rows(mine, 1 - b[BIT2], rows) + part_rows(got, 1 - b[BIT2], rows)).astype(low)
            keep[:rows, c] = (part_rows(mine, b[BIT2], rows) + part_rows(got, b[BIT2], rows)).astype(low)
        if extra:
            total = (l[2 * rows :, :].astype(wide) + lg[2 * rows :, :].astype(wide)).astype(low)
            for ref in (send, keep):
                ref[rows:, :cols] = total
                ref[rows:, cols:] = jnp.zeros_like(total)

    return whole_call(body, [left, left_got, right, right_got], [(rows + extra, 2 * cols)] * 2, bits, after)


def add_up(mine, got, bits, after=()):
    def body(b, m, g, out):
        out[...] = (m[...].astype(wide) + g[...].astype(wide)).astype(low)

    return whole_call(body, [mine, got], [mine.shape], bits, after)[0]


def place(out, mine, got, bit, cols=slice(None), rows=None):
    rows = mine.shape[0] if rows is None else rows
    out[pl.ds(pl.multiple_of(bit * rows, rows), rows), :] = mine[:rows, cols]
    out[pl.ds(pl.multiple_of((1 - bit) * rows, rows), rows), :] = got[:rows, cols]


def join_both(mine, got, rows, vectors, bits, after=()):
    cols = mine.shape[1] // 2
    width = vectors[1]

    def body(b, m, g, *refs):
        *outs, left, right = refs
        place(left, m, g, b[BIT2], slice(0, cols), rows)
        place(right, m, g, b[BIT2], slice(cols, 2 * cols), rows)
        at = rows
        for out in outs:
            for c in range(0, out.shape[0], width):
                out[pl.ds(c, width)] = m[at : at + 1, :width].astype(wide).reshape(-1)
                at += 1

    shapes = [struct((v,), wide) for v in vectors[0]] + [struct((2 * rows, cols), low)] * 2
    return call(body, [mine, got], shapes, bits=bits, after=after, limit=8, cost=115, far_out=range(len(vectors[0])))


def join_sides(left, left_got, right, right_got, bits, after=()):
    rows, cols = left.shape

    def body(b, l, lg, r, rg, lo, ro):
        place(lo, l, lg, b[BIT1])
        place(ro, r, rg, b[BIT0])

    return whole_call(body, [left, left_got, right, right_got], [(2 * rows, cols)] * 2, bits, after)


def join_half(left, left_got, right, right_got, bits, after=()):
    rows, cols = left.shape

    def body(b, l, lg, r, rg, out):
        place(out.at[:, pl.ds(0, cols)], l, lg, b[BIT0])
        place(out.at[:, pl.ds(cols, cols)], r, rg, b[BIT1])

    return whole_call(body, [left, left_got, right, right_got], [(2 * rows, 2 * cols)], bits, after)[0]


def widen(source, which, before, widths, bits, after=()):
    half, n = source.shape
    parts = 4
    tile = half // parts

    def body(b, src, *refs):
        refs = refs[0 if before is None else len(before) :]
        outs, token, bufs, sems = refs[: len(widths)], refs[len(widths)], refs[len(widths) + 1 : -1], refs[-1]
        token[...] = jnp.zeros_like(token)
        start = (1 - b[CORE] if which else b[CORE]) * half
        copies = []
        for t in range(parts):
            at = 0
            for out, buf, w in zip(outs, bufs, widths):
                buf[t] = src[t * tile : (t + 1) * tile, at : at + w].astype(wide)
                rows = pl.ds(pl.multiple_of(start + t * tile, tile), tile)
                copies.append(pltpu.make_async_copy(buf.at[t], out.at[rows, :], sems.at[len(copies)]))
                copies[-1].start()
                at += w
        for copy in copies:
            copy.wait()

    return call(
        body,
        [source] + list(before or []),
        [struct((2 * half, w), wide) for w in widths] + [struct((8, 128), wide)],
        bits=bits,
        scratch=[pltpu.VMEM((parts, tile, w), wide) for w in widths] + [pltpu.SemaphoreType.DMA((parts * len(widths),))],
        aliases={1 + i: i for i in range(len(widths))} if before else None,
        after=after,
        far=range(1, 1 + len(widths)) if before else (),
        hand_out=range(len(widths)),
        limit=12,
        cost=115,
    )


class Reduction:
    def __init__(self, src, widths, bits, clock, tail, vectors=()):
        self.vectors = vectors
        self.src, self.widths, self.bits, self.clock, self.tail = src, widths, bits, clock, tail

    def step(self, fn, *args):
        out = fn(*args, after=self.clock.now())
        self.clock.set(out[-1] if isinstance(out, (list, tuple)) else out)
        return out

    def core_send(self):
        send, *kept = self.step(gradient_rows, self.src, self.bits, None)
        if kept:
            self.src.kept = kept[0]
        self.got = exchange(send, "stream", 1)

    def core_sum(self):
        ls, self.l, rs, self.r = self.step(gradient_rows, self.src, self.bits, self.got)
        self.gl, self.gr = exchange(ls, "dp", 1), exchange(rs, "dp", 2)

    def first_sum(self):
        ls, self.l, rs, self.r = self.step(halve_sides, self.l, self.gl, self.r, self.gr, self.bits)
        self.gl, self.gr = exchange(ls, "dp", 2), exchange(rs, "dp", 1)

    def second_sum(self):
        send, self.v = self.step(halve_both, self.l, self.gl, self.r, self.gr, self.bits)
        self.got = exchange(send, "dp", 4)

    def third_sum(self):
        self.v = self.step(add_up, self.v, self.got, self.bits)
        self.got = exchange(self.v, "dp", self.tail[0])

    def last_sum(self):
        for mask in self.tail[1:]:
            self.v = self.step(add_up, self.v, self.got, self.bits)
            self.got = exchange(self.v, "dp", mask)
        self.v = self.step(add_up, self.v, self.got, self.bits)
        self.got = exchange(self.v, "dp", 4)

    def third_back(self):
        vectors = self.vectors, self.src.small[0].shape[1] if self.src.small else None
        *self.sums, self.l, self.r = self.step(join_both, self.v, self.got, self.src.m // 16, vectors, self.bits)
        self.gl, self.gr = exchange(self.l, "dp", 2), exchange(self.r, "dp", 1)

    def second_back(self):
        self.l, self.r = self.step(join_sides, self.l, self.gl, self.r, self.gr, self.bits)
        self.gl, self.gr = exchange(self.l, "dp", 1), exchange(self.r, "dp", 2)

    def first_back(self):
        self.v = self.step(join_half, self.l, self.gl, self.r, self.gr, self.bits)
        self.got = exchange(self.v, "stream", 1)

    def finish_own(self):
        self.out = self.step(widen, self.v, 0, None, self.widths, self.bits)[:-1]

    def finish(self):
        return self.step(widen, self.got, 1, self.out, self.widths, self.bits)[:-1]


class Clock:
    def __init__(self, start):
        self.last = start

    def now(self):
        return (self.last,)

    def set(self, value):
        self.last = value


def shards(
    embedded, seq_cotangent, pair_ids, w_qkv, b_qv, w_out, b_out, ln1_gain, ln1_bias, w_in, b_in, w_down, b_down,
    ln2_gain, ln2_bias, w_pool, b_pool,
):
    x = embedded[0]
    tokens, width = x.shape
    sents = tokens // SEQ
    ffn = w_in.shape[1]
    dp = lax.axis_size("dp")
    stream, place_dp = lax.axis_index("stream"), lax.axis_index("dp")
    bits = jnp.stack([stream, place_dp & 1, (place_dp >> 1) & 1, (place_dp >> 2) & 1, place_dp]).astype(jnp.int32)
    later = [
        w_in, w_down, seq_cotangent[0], w_pool, b_in, b_down, ln2_gain, ln2_bias, b_pool, pair_ids
    ]
    proj, probs, context, hidden, hidden_low, inv_one, *later = attention_forward(
        bits, x, w_qkv, b_qv, w_out, b_out, ln1_gain, ln1_bias, later
    )
    w_in, w_down, cotangent, w_pool, b_in, b_down, ln2_gain, ln2_bias, b_pool, ids = later
    hid3 = hidden.reshape(sents, SEQ, width)
    cot3 = cotangent.reshape(sents, SEQ, width)
    upper = (w_in, b_in, w_down, b_down, ln2_gain, ln2_bias)
    enc, act, gate_in, phi, normed_two, inv_two, first_low = ffn_group(0, hid3, cot3, upper, ())
    masks = [1 << i for i in range(dp.bit_length() - 1)]
    state = [enc, act]
    gathered = first_low
    group = 1
    order = [inv_two]
    for low_bit in range(0, len(masks), 2):
        span = 4 if low_bit + 1 < len(masks) else 2
        blocks = [gathered] + [exchange(gathered, "dp", i << low_bit) for i in range(1, span)]
        if group < SEQ // GROUP:
            state = ffn_group(group, hid3, cot3, upper, state, after=order)
            group += 1
            order = [state[-1]]
        gathered = put_in_order(blocks, bits, low_bit, order)
        order = [gathered]
    other = exchange(gathered, "stream", 1)
    while group < SEQ // GROUP:
        state = ffn_group(group, hid3, cot3, upper, state, after=order)
        group += 1
        order = [state[-1]]
    enc, act, gate, two, small_up, bin_sum = state
    grad_first, grad_w_pool, grad_b_pool = contrastive(
        gathered, other, bits, sents, ids, w_pool, b_pool, order
    )
    gate, two, small_up, bin_sum = ffn_first_back(
        cot3, grad_first, normed_two, inv_two, gate_in, phi, ln2_gain, w_down, gate, two, small_up, bin_sum
    )
    clock = Clock(small_up)
    act, gate, two = (v.reshape(tokens, -1) for v in (act, gate, two))
    tail = masks[3:]
    down = Reduction(Sources([(act, two)]), [width], bits, clock, tail)
    into = Reduction(Sources([(hidden_low, gate)]), [ffn], bits, clock, tail)
    down.core_send()
    into.core_send()
    down.core_sum()
    lower = (two, gate, hidden, inv_one, proj, probs, w_in, w_out, ln1_gain, ln1_bias)
    state = lower_backward(0, 2, *lower, after=clock.now())
    clock.set(state[-1])
    state = lower_backward(1, 2, *lower, before=state, after=clock.now())
    grad_one, grad_proj, small_low, bqv = state
    clock.set(bqv)
    down.first_sum()
    into.core_sum()
    low_part = Reduction(
        Sources([(x, grad_proj), (context, grad_one)], [small_up, bin_sum, small_low, bqv]),
        [3 * width, width],
        bits,
        clock,
        tail,
        (width, width, width, ffn, width, width, width, 2 * width),
    )
    down.second_sum()
    low_part.core_send()
    down.third_sum()
    into.first_sum()
    low_part.core_sum()
    into.second_sum()
    down.last_sum()
    grad_input, token = input_gradient(grad_proj, w_qkv, grad_one, after=clock.now())
    clock.set(token)
    low_part.first_sum()
    into.third_sum()
    down.third_back()
    low_part.second_sum()
    down.second_back()
    into.last_sum()
    low_part.third_sum()
    into.third_back()
    down.first_back()
    down.finish_own()
    into.second_back()
    low_part.last_sum()
    (out_down,) = down.finish()
    low_part.third_back()
    into.first_back()
    into.finish_own()
    low_part.second_back()
    (out_in,) = into.finish()
    low_part.first_back()
    low_part.finish_own()
    out_qkv, out_out = low_part.finish()
    g_ln2_gain, g_ln2_bias, g_b_down, g_b_in, g_ln1_gain, g_ln1_bias, g_b_out, g_b_qv = low_part.sums
    return (
        enc.reshape(1, tokens, width),
        grad_input[None],
        out_qkv,
        g_b_qv,
        out_out,
        g_b_out,
        g_ln1_gain,
        g_ln1_bias,
        out_in,
        g_b_in,
        out_down,
        g_b_down,
        g_ln2_gain,
        g_ln2_bias,
        grad_w_pool,
        grad_b_pool,
    )


def solution(mesh):
    sharded = P("stream", "dp", None)
    return jax.shard_map(
        shards,
        mesh=mesh,
        in_specs=(sharded, sharded) + (P(),) * 15,
        out_specs=(sharded, sharded) + (P(),) * 14,
        check_vma=False,
    )
```

```python
import functools
import math

import jax
import jax.numpy as jnp
from jax import lax
from jax.experimental import pallas as pl
from jax.experimental.pallas import tpu as pltpu
from jax.sharding import PartitionSpec as P

HEAD_DIM = 64
SEQ = 64
GROUP = 16
CHUNK = 512

epsilon = 1e-06
score_scale = 10.0
margin_shift = score_scale * 0.3
root_half = 0.7071067811865476
gauss_norm = 0.3989422804014327

low = jnp.bfloat16
wide = jnp.float32
ANY = pl.BlockSpec(memory_space=pl.ANY)
VMEM = pl.BlockSpec(memory_space=pltpu.VMEM)
SMEM = pl.BlockSpec(memory_space=pltpu.SMEM)
HBM = pl.BlockSpec(memory_space=pltpu.HBM)
MIB = 1 << 20


def struct(shape, dtype):
    return jax.ShapeDtypeStruct(shape, dtype)


def call(body, ins, outs, bits=None, scratch=(), aliases=None, after=(), limit=10, far=(), far_out=(), hand_out=(), cost=460):
    first = 0 if bits is None else 1
    ins = [pltpu.with_memory_space_constraint(a, pltpu.HBM) if i in far else a for i, a in enumerate(ins)]

    def wrapped(*refs):
        body(*refs[: first + len(ins)], *refs[first + len(ins) + len(after) :])

    return pl.pallas_call(
        wrapped,
        in_specs=[SMEM] * first + [HBM if i in far else VMEM for i in range(len(ins))] + [ANY] * len(after),
        out_specs=[HBM if i in hand_out else VMEM for i in range(len(outs))],
        out_shape=[(pltpu.HBM if i in far_out or i in hand_out else pltpu.VMEM)(o.shape, o.dtype) for i, o in enumerate(outs)],
        scratch_shapes=list(scratch),
        input_output_aliases={first + k: v for k, v in (aliases or {}).items()},
        cost_estimate=pl.CostEstimate(flops=int(cost * 2 * 10**7), bytes_accessed=0, transcendentals=0),
        compiler_params=pltpu.CompilerParams(vmem_limit_bytes=limit * MIB),
    )(*([] if bits is None else [bits]), *ins, *after)


def row_of(ref, start=0, size=None):
    return ref[pl.ds(start, ref.shape[0] if size is None else size)].reshape(1, -1)


def mat_mul(a, b):
    return jnp.dot(a, b, preferred_element_type=wide)


def trans_left(a, b):
    return lax.dot_general(a, b, (((0,), (0,)), ((), ())), preferred_element_type=wide)


def trans_right(a, b):
    return lax.dot_general(a, b, (((1,), (1,)), ((), ())), preferred_element_type=wide)


def normalize(h):
    center = h - jnp.mean(h, axis=-1, keepdims=True)
    inv = lax.rsqrt(jnp.mean(center * center, axis=-1, keepdims=True) + epsilon)
    return center * inv, inv


def norm_input_grad(grad, normed, inv):
    return inv * (
        grad
        - jnp.mean(grad, axis=-1, keepdims=True)
        - normed * jnp.mean(grad * normed, axis=-1, keepdims=True)
    )


def split_heads(pair, first):
    zero = jnp.zeros_like(pair)
    return jnp.concatenate([jnp.where(first, pair, zero), jnp.where(first, zero, pair)], axis=0)


def join_heads(rows, first):
    return jnp.where(first, rows[:SEQ], rows[SEQ:])


def heads_product(left, right, cols, first):
    zero = jnp.zeros_like(right[0][:, cols[0]])
    out = ([], [])
    for c in cols:
        both = jnp.concatenate([left[0][:, c], left[1][:, c]], axis=0)
        apart = jnp.concatenate(
            [jnp.concatenate([right[0][:, c], zero], axis=1), jnp.concatenate([zero, right[1][:, c]], axis=1)], axis=0
        )
        rows = trans_left(both, apart)
        for i in range(2):
            out[i].append(join_heads(rows[:, i * 128 : (i + 1) * 128], first))
    return [jnp.concatenate(o, axis=1) for o in out]


def attention_forward(bits, x, w_qkv, b_qv, w_out, b_out, gain, bias, later):
    tokens, width = x.shape
    rows = 4 * SEQ
    pairs = width // (2 * HEAD_DIM)
    scale = 1.0 / math.sqrt(HEAD_DIM)

    def body(_bits, *refs):
        n = len(later)
        far, far_later, outs, near_later, near, sems = (
            refs[:7], refs[7 : 7 + n], refs[7 + n : 13 + n], refs[13 + n : 13 + 2 * n], refs[13 + 2 * n : -1], refs[-1]
        )
        proj_ref, prob_ref, ctx_ref, hid_ref, low_ref, inv_ref = outs
        x_ref, wq_ref, bqv_ref, wo_ref, bo_ref, g_ref, b_ref = near
        pairs_of = zip(far + far_later, near + near_later)
        copies = [pltpu.make_async_copy(f, near_f, sems.at[i]) for i, (f, near_f) in enumerate(pairs_of)]
        for copy in copies[:3]:
            copy.start()
        for copy in copies[:3]:
            copy.wait()
        for copy in copies[3:]:
            copy.start()
        first = lax.broadcasted_iota(jnp.int32, (SEQ, 128), 1) < HEAD_DIM
        cols = [slice(p * 128, (p + 1) * 128) for p in range(pairs)]

        for part in range(3):
            c = slice(part * width, (part + 1) * width)
            value = mat_mul(x_ref[...], wq_ref[:, c])
            if part != 1:
                value = value + row_of(bqv_ref, (part // 2) * width, width)
            proj_ref[:, c] = value.astype(low)

        @pl.loop(0, tokens // rows)
        def _(step):
            base = step * rows
            for two in range(2):
                at = [pl.ds(pl.multiple_of(base + (2 * two + i) * SEQ, SEQ), SEQ) for i in range(2)]
                probs = []
                for r in at:
                    q = proj_ref[r, :width]
                    k = proj_ref[r, width : 2 * width]
                    scores = (
                        jnp.concatenate([trans_right(k[:, c], split_heads(q[:, c], first)) for c in cols], axis=1) * scale
                    )
                    e = jnp.exp(scores - jnp.max(scores, axis=0, keepdims=True))
                    probs.append((e * (1.0 / jnp.sum(e, axis=0, keepdims=True))).astype(low))
                    prob_ref[r, :] = probs[-1]
                values = [proj_ref[r, 2 * width :] for r in at]
                for r, context in zip(at, heads_product(probs, values, cols, first)):
                    ctx_ref[r, :] = context.astype(low)

        for copy in copies[3:7]:
            copy.wait()

        for start in range(0, tokens, tokens // 2):
            block = slice(start, start + tokens // 2)
            h = x_ref[block, :].astype(wide) + mat_mul(ctx_ref[block, :], wo_ref[...]) + row_of(bo_ref)
            normed, inv = normalize(h)
            hidden = normed * row_of(g_ref) + row_of(b_ref)
            hid_ref[block, :] = hidden
            low_ref[block, :] = hidden.astype(low)
            inv_ref[block, :] = inv

        for copy in copies[7:]:
            copy.wait()

    return call(
        body,
        [x, w_qkv, b_qv, w_out, b_out, gain, bias] + later,
        [
            struct((tokens, 3 * width), low),
            struct((tokens, width), low),
            struct((tokens, width), low),
            struct((tokens, width), wide),
            struct((tokens, width), low),
            struct((tokens, 1), wide),
        ]
        + [struct(v.shape, v.dtype) for v in later],
        scratch=[pltpu.VMEM(v.shape, v.dtype) for v in (x, w_qkv, b_qv, w_out, b_out, gain, bias)]
        + [pltpu.SemaphoreType.DMA((7 + len(later),))],
        bits=bits,
        far=range(7 + len(later)),
        limit=14,
    )


def ffn_forward_rows(hidden, wi_ref, bi_ref, wd_ref, bd_ref, store_act, store_gate_in):
    h_low = hidden.astype(low)
    total = hidden + row_of(bd_ref)
    for c in range(0, wi_ref.shape[1], CHUNK):
        u = mat_mul(h_low, wi_ref[:, c : c + CHUNK]) + row_of(bi_ref, c, CHUNK)
        phi = 0.5 + 0.5 * lax.erf(u * root_half)
        act = (u * phi).astype(low)
        store_act(c, act)
        store_gate_in(c, u.astype(low), phi.astype(low))
        total = total + mat_mul(act, wd_ref[c : c + CHUNK, :])
    return normalize(total)


def ffn_backward_rows(grad_block, normed, inv, gain, wd_ref, gate_in, store_gate, small_ref, bin_ref):
    grad_two = norm_input_grad(grad_block * gain, normed, inv)
    small_ref[0:1, :] += jnp.sum(grad_block * normed, axis=0, keepdims=True)
    small_ref[1:2, :] += jnp.sum(grad_block, axis=0, keepdims=True)
    small_ref[2:3, :] += jnp.sum(grad_two, axis=0, keepdims=True)
    grad_low = grad_two.astype(low)
    for c in range(0, wd_ref.shape[0], CHUNK):
        u, phi = gate_in(c)
        slope = phi + u * jnp.exp(u * u * low(-0.5)) * low(gauss_norm)
        gate = trans_right(grad_low, wd_ref[c : c + CHUNK, :]) * slope.astype(wide)
        bin_ref[:, c : c + CHUNK] += jnp.sum(gate, axis=0, keepdims=True)
        store_gate(c, gate.astype(low))
    return grad_low


def ffn_group(index, hidden, cot, upper, state, after=()):
    w_in, b_in, w_down, b_down, gain, bias = upper
    sents, _, width = hidden.shape
    ffn = w_in.shape[1]
    rows = sents * GROUP
    at = slice(index * GROUP, (index + 1) * GROUP)
    first = index == 0
    second = index == 1

    def stores(act_ref, u_ref, phi_ref):
        def store_act(c, v):
            act_ref[:, at, c : c + CHUNK] = v.reshape(sents, GROUP, CHUNK)

        def store_gate_in(c, u, phi):
            u_ref[:, c : c + CHUNK] = u
            phi_ref[:, c : c + CHUNK] = phi

        return store_act, store_gate_in

    def forward(h_ref, wi_ref, bi_ref, wd_ref, bd_ref, act_ref, u_ref, phi_ref):
        return ffn_forward_rows(
            h_ref[:, at, :].reshape(rows, width), wi_ref, bi_ref, wd_ref, bd_ref, *stores(act_ref, u_ref, phi_ref)
        )

    def body_first(h_ref, wi_ref, bi_ref, wd_ref, bd_ref, g_ref, b_ref, enc_hbm, act_ref, u_ref, phi_ref, n_ref, inv_ref, first_ref, enc_ref, sem):
        normed, inv = forward(h_ref, wi_ref, bi_ref, wd_ref, bd_ref, act_ref, u_ref, phi_ref)
        n_ref[...] = normed
        inv_ref[...] = inv
        block = (normed * row_of(g_ref) + row_of(b_ref)).reshape(sents, GROUP, width)
        enc_ref[...] = block.astype(low)
        copy = pltpu.make_async_copy(enc_ref, enc_hbm.at[:, pl.ds(index * GROUP, GROUP), :], sem)
        copy.start()
        first_ref[...] = block[:, 0, :].astype(low)
        copy.wait()

    enc_shape = struct((sents, SEQ, width), low)
    enc_scratch = [pltpu.VMEM((sents, GROUP, width), low), pltpu.SemaphoreType.DMA]
    act_shape = struct((sents, SEQ, ffn), low)
    if first:
        return call(
            body_first,
            [hidden, w_in, b_in, w_down, b_down, gain, bias],
            [
                enc_shape,
                act_shape,
                struct((rows, ffn), low),
                struct((rows, ffn), low),
                struct((rows, width), wide),
                struct((rows, 1), wide),
                struct((sents, width), low),
            ],
            scratch=enc_scratch,
            hand_out=[0],
        )

    def body(h_ref, cot_ref, wi_ref, bi_ref, wd_ref, bd_ref, g_ref, b_ref, *refs):
        refs = refs[2 if second else 4 :]
        if not second:
            sin_ref, bin_in_ref = refs[:2]
            refs = refs[2:]
        enc_hbm, act_ref, gate_ref, two_ref, small_ref, bin_ref, u_ref, phi_ref, enc_ref, sem = refs
        small_ref[...] = jnp.zeros_like(small_ref) if second else sin_ref[...]
        bin_ref[...] = jnp.zeros_like(bin_ref) if second else bin_in_ref[...]

        def store_gate(c, v):
            gate_ref[:, at, c : c + CHUNK] = v.reshape(sents, GROUP, CHUNK)

        normed, inv = forward(h_ref, wi_ref, bi_ref, wd_ref, bd_ref, act_ref, u_ref, phi_ref)
        gain_row = row_of(g_ref)
        enc_ref[...] = (normed * gain_row + row_of(b_ref)).astype(low).reshape(sents, GROUP, width)
        copy = pltpu.make_async_copy(enc_ref, enc_hbm.at[:, pl.ds(index * GROUP, GROUP), :], sem)
        copy.start()
        grad_block = cot_ref[:, at, :].reshape(rows, width).astype(wide)
        got = ffn_backward_rows(
            grad_block, normed, inv, gain_row, wd_ref, lambda c: (u_ref[:, c : c + CHUNK], phi_ref[:, c : c + CHUNK]),
            store_gate, small_ref, bin_ref,
        )
        two_ref[:, at, :] = got.reshape(sents, GROUP, width)
        copy.wait()

    aliases = {8: 0, 9: 1}
    if not second:
        aliases.update({10: 2, 11: 3})
    return call(
        body,
        [hidden, cot, w_in, b_in, w_down, b_down, gain, bias] + list(state),
        [enc_shape, act_shape, act_shape, enc_shape, struct((8, width), wide), struct((1, ffn), wide)],
        scratch=[pltpu.VMEM((rows, ffn), low)] * 2 + enc_scratch,
        aliases=aliases,
        after=after,
        far=[8],
        hand_out=[0],
    )


def ffn_first_back(cot, grad_first, normed, inv, gate_in, phi, gain, w_down, gate, two, small, bin_sum):
    sents, _, width = cot.shape
    ffn = w_down.shape[0]
    rows = sents * GROUP
    at = slice(0, GROUP)

    def body(cot_ref, first_ref, n_ref, inv_ref, u_ref, phi_ref, g_ref, wd_ref, sin_ref, bin_in_ref, _g, _t, gate_ref, two_ref, small_ref, bin_ref):
        small_ref[...] = sin_ref[...]
        bin_ref[...] = bin_in_ref[...]
        position = lax.broadcasted_iota(jnp.int32, (sents, GROUP, width), 1)
        at_first = jnp.broadcast_to(first_ref[...][:, None, :], (sents, GROUP, width))
        grad_block = cot_ref[:, at, :].astype(wide) + jnp.where(position == 0, at_first, 0.0)

        def store_gate(c, v):
            gate_ref[:, at, c : c + CHUNK] = v.reshape(sents, GROUP, CHUNK)

        got = ffn_backward_rows(
            grad_block.reshape(rows, width), n_ref[...], inv_ref[...], row_of(g_ref), wd_ref,
            lambda c: (u_ref[:, c : c + CHUNK], phi_ref[:, c : c + CHUNK]), store_gate, small_ref, bin_ref,
        )
        two_ref[:, at, :] = got.reshape(sents, GROUP, width)

    return call(
        body,
        [cot, grad_first, normed, inv, gate_in, phi, gain, w_down, small, bin_sum, gate, two],
        [struct((sents, SEQ, ffn), low), struct((sents, SEQ, width), low), struct((8, width), wide), struct((1, ffn), wide)],
        aliases={10: 0, 11: 1},
    )


def lower_backward(part, parts, two, gate, hidden, inv, proj, probs, w_in, w_out, gain, bias, before=None, after=()):
    tokens, width = hidden.shape
    ffn = w_in.shape[1]
    rows = 4 * SEQ
    steps = tokens // rows // parts
    pairs = width // (2 * HEAD_DIM)
    scale = 1.0 / math.sqrt(HEAD_DIM)
    fresh = before is None

    def body(two_ref, gate_ref, hid_ref, inv_ref, proj_ref, prob_ref, wi_ref, wo_ref, g_ref, b_ref, *refs):
        if not fresh:
            sin_ref, bin_ref = refs[2:4]
            refs = refs[4:]
        one_ref, gp_ref, small_ref, bqv_ref, ctx_ref = refs
        small_ref[...] = jnp.zeros_like(small_ref) if fresh else sin_ref[...]
        bqv_ref[...] = jnp.zeros_like(bqv_ref) if fresh else bin_ref[...]
        first = lax.broadcasted_iota(jnp.int32, (SEQ, 128), 1) < HEAD_DIM
        cols = [slice(p * 128, (p + 1) * 128) for p in range(pairs)]

        block = slice(part * steps * rows, (part + 1) * steps * rows)
        gain_row = row_of(g_ref)
        grad_hidden = two_ref[block, :].astype(wide) + trans_right(gate_ref[block, :], wi_ref[...])
        normed = (hid_ref[block, :] - row_of(b_ref)) * (1.0 / gain_row)
        small_ref[0:1, :] += jnp.sum(grad_hidden * normed, axis=0, keepdims=True)
        small_ref[1:2, :] += jnp.sum(grad_hidden, axis=0, keepdims=True)
        grad_one = norm_input_grad(grad_hidden * gain_row, normed, inv_ref[block, :])
        small_ref[2:3, :] += jnp.sum(grad_one, axis=0, keepdims=True)
        one_ref[block, :] = grad_one.astype(low)
        ctx_ref[...] = trans_right(one_ref[block, :], wo_ref[...]).astype(low)

        @pl.loop(0, steps)
        def _(step):
            base = step * rows + part * steps * rows
            sum_q = jnp.zeros((1, width), wide)
            sum_v = jnp.zeros((1, width), wide)
            for two in range(2):
                at = [pl.ds(pl.multiple_of(base + (2 * two + i) * SEQ, SEQ), SEQ) for i in range(2)]
                grads = []
                for i, r in enumerate(at):
                    q_all = proj_ref[r, :width]
                    v = proj_ref[r, 2 * width :]
                    d_all = ctx_ref[pl.ds(pl.multiple_of(step * rows + (2 * two + i) * SEQ, SEQ), SEQ), :]
                    p_low = prob_ref[r, :]
                    q = [split_heads(q_all[:, c], first) for c in cols]
                    d = [split_heads(d_all[:, c], first) for c in cols]
                    p = p_low.astype(wide)
                    grad_p = jnp.concatenate([trans_right(v[:, c], dd) for c, dd in zip(cols, d)], axis=1)
                    grad_v = jnp.concatenate([mat_mul(p_low[:, c], dd) for c, dd in zip(cols, d)], axis=1)
                    gp = grad_p * p
                    grad_s = (gp - p * jnp.sum(gp, axis=0, keepdims=True)).astype(low)
                    grad_k = jnp.concatenate([mat_mul(grad_s[:, c], qq) for c, qq in zip(cols, q)], axis=1) * scale
                    sum_v += jnp.sum(grad_v, axis=0, keepdims=True)
                    gp_ref[r, width : 2 * width] = grad_k.astype(low)
                    gp_ref[r, 2 * width :] = grad_v.astype(low)
                    grads.append(grad_s)
                keys = [proj_ref[r, width : 2 * width] for r in at]
                for r, product in zip(at, heads_product(grads, keys, cols, first)):
                    grad_q = product * scale
                    sum_q += jnp.sum(grad_q, axis=0, keepdims=True)
                    gp_ref[r, :width] = grad_q.astype(low)
            bqv_ref[0:1, :] += sum_q
            bqv_ref[1:2, :] += sum_v

    return call(
        body,
        [two, gate, hidden, inv, proj, probs, w_in, w_out, gain, bias] + ([] if fresh else list(before)),
        [struct((tokens, width), low), struct((tokens, 3 * width), low), struct((8, width), wide), struct((8, width), wide)],
        scratch=[pltpu.VMEM((rows * steps, width), low)],
        aliases=None if fresh else {10: 0, 11: 1},
        after=after,
    )


def input_gradient(grad_proj, w_qkv, grad_one, after=()):
    tokens, width = grad_one.shape
    rows = tokens // 2

    def body(gp_ref, w_ref, one_ref, out_ref, token):
        token[...] = jnp.zeros_like(token)

        for start in range(0, tokens, rows):
            block = slice(start, start + rows)
            out_ref[block, :] = (one_ref[block, :].astype(wide) + trans_right(gp_ref[block, :], w_ref[...])).astype(low)

    return call(
        body, [grad_proj, w_qkv, grad_one], [struct((tokens, width), low), struct((8, 128), wide)], after=after, far_out=[0]
    )


def pooler_gradients(flat, id_row, w_pool, b_pool):
    total = flat.shape[0] // 2
    pooled = jnp.tanh(mat_mul(flat, w_pool) + b_pool)
    inv_len = lax.rsqrt(jnp.sum(pooled * pooled, axis=-1, keepdims=True) + epsilon)
    unit = pooled * inv_len
    embed = unit.astype(low)
    zero, one = embed[:total], embed[total:]
    square = (total, total)
    eye = (lax.broadcasted_iota(jnp.int32, square, 0) == lax.broadcasted_iota(jnp.int32, square, 1)).astype(wide)
    logits = score_scale * trans_right(zero, one) - margin_shift * eye
    id_column = jnp.sum(jnp.where(eye > 0, id_row, 0), axis=1, keepdims=True)
    masked = jnp.where(id_column == id_row, logits, -jnp.inf)

    def soft(axis):
        e = jnp.exp(masked - jnp.max(masked, axis=axis, keepdims=True))
        return (score_scale * (e / jnp.sum(e, axis=axis, keepdims=True) - eye)).astype(low)

    by_row, by_col = soft(1), soft(0)
    grad_embed = jnp.concatenate(
        [mat_mul(by_row, one) + mat_mul(by_col, one), trans_left(by_row, zero) + trans_left(by_col, zero)], axis=0
    )
    grad_pre = (
        inv_len * (grad_embed - unit * jnp.sum(unit * grad_embed, axis=-1, keepdims=True)) * (1.0 - pooled * pooled)
    )
    pre_low = grad_pre.astype(low)
    return pre_low, trans_left(flat, pre_low), jnp.sum(grad_pre, axis=0, keepdims=True)


def contrastive(own, got, bits, sents, ids, w_pool, b_pool, after):
    total, width = own.shape
    if total > 512:
        start = bits[CORE] * total + bits[PLACE] * sents
        flat = jnp.where(bits[CORE] == 0, jnp.concatenate([own, got]), jnp.concatenate([got, own]))
        pre_low, grad_w, grad_b = pooler_gradients(flat, ids.reshape(1, -1), w_pool, b_pool.reshape(1, -1))
        return trans_right(lax.dynamic_slice_in_dim(pre_low, start, sents), w_pool), grad_w, grad_b.reshape(-1)

    def body(b, own_ref, got_ref, ids_ref, w_ref, b_ref, first_ref, gw_ref, gb_ref, flat_ref, pre_ref):
        flat_ref[pl.ds(pl.multiple_of(b[CORE] * total, total), total), :] = own_ref[...]
        flat_ref[pl.ds(pl.multiple_of((1 - b[CORE]) * total, total), total), :] = got_ref[...]
        pre_low, grad_w, grad_b = pooler_gradients(flat_ref[...], row_of(ids_ref), w_ref[...], row_of(b_ref))
        pre_ref[...] = pre_low
        gw_ref[...] = grad_w
        gb_ref[...] = grad_b.reshape(-1)
        first_ref[...] = trans_right(pre_ref[pl.ds(pl.multiple_of(b[CORE] * total + b[PLACE] * sents, sents), sents), :], w_ref[...])

    return call(
        body,
        [own, got, ids, w_pool, b_pool],
        [struct((sents, width), wide), struct((width, width), wide), struct((width,), wide)],
        bits=bits,
        scratch=[pltpu.VMEM((2 * total, width), low)] * 2,
        after=after,
        far_out=[1, 2],
    )


def put_in_order(blocks, bits, low_bit, after):
    rows, width = blocks[0].shape

    def body(b, *refs):
        me = (b[PLACE] >> low_bit) & (len(blocks) - 1)
        for i, ref in enumerate(refs[:-1]):
            at = pl.multiple_of((me ^ i) * rows, rows)
            refs[-1][pl.ds(at, rows), :] = ref[...]

    return call(
        body, blocks, [struct((rows * len(blocks), width), low)], bits=bits, after=after, limit=8, cost=690
    )[0]


CORE, FIRST, SECOND, THIRD, PLACE = range(5)
SMALL = 16
MASKS = {FIRST: (1, 2), SECOND: (2, 1), THIRD: (4, 4)}


def exchange(a, masks):
    size = lax.axis_size("dp")
    pairs = [(core * size + i, core * size + (i ^ masks[core])) for core in range(2) for i in range(size)]
    return lax.ppermute(a, ("stream", "dp"), pairs)


def cross(a):
    return lax.ppermute(a, "stream", [(0, 1), (1, 0)])


class Sources:
    def __init__(self, products, small=()):
        self.products = products
        self.small = list(small)
        self.m = products[0][0].shape[1]
        self.n = sum(hi - lo for _, _, lo, hi in products)
        self.arrays = [a for left, right, _, _ in products for a in (left, right)]

    def pieces(self, refs):
        at = 0
        for i, (_, _, lo, hi) in enumerate(self.products):
            yield refs[2 * i], refs[2 * i + 1], lo, at, hi - lo
            at += hi - lo


def gradient_to_send(src, bits, after=()):
    m, n = src.m, src.n
    half = m // 2
    count = len(src.arrays)
    small = src.small

    def body(b, *refs):
        out = refs[count + len(small)]
        rows = pl.ds(pl.multiple_of((1 - b[CORE]) * half, 128), half)
        for a, g, lo, at, size in src.pieces(refs):
            out[:half, at : at + size] = trans_left(a[:, rows], g[:, lo : lo + size]).astype(low)
        if small:
            up, bin_sum, down, bqv = refs[count : count + 4]
            kept = refs[-1]
            width = up.shape[1]
            parts = [up[:3]] + [bin_sum[:, c : c + width] for c in range(0, bin_sum.shape[1], width)] + [down[:3], bqv[:2]]
            parts.append(jnp.zeros((SMALL - sum(p.shape[0] for p in parts), width), wide))
            kept[...] = jnp.concatenate(parts, axis=0).astype(low)
            out[half:, :] = jnp.zeros((SMALL, n), low)
            out[half:, :width] = kept[...]

    shapes = [struct((half + (SMALL if small else 0), n), low)]
    if small:
        shapes.append(struct((SMALL, small[0].shape[1]), low))
    return call(body, src.arrays + small, shapes, bits=bits, after=after)


def gradient_sum(src, bits, got, kept, bit, after=()):
    m, n = src.m, src.n
    half, quarter = m // 2, m // 4
    count = len(src.arrays)
    extra = SMALL if src.small else 0

    def body(b, *refs):
        got_ref, send, keep = refs[-3:]
        if extra:
            mine = refs[count]
            total = (mine[...].astype(wide) + got_ref[half:, : mine.shape[1]].astype(wide)).astype(low)
            for ref in (send, keep):
                ref[quarter:, :] = jnp.zeros((SMALL, n), low)
                ref[quarter:, : mine.shape[1]] = total
        rows = pl.ds(pl.multiple_of(b[CORE] * half, 128), half)
        for a, g, lo, at, size in src.pieces(refs):
            c = slice(at, at + size)
            value = (trans_left(a[:, rows], g[:, lo : lo + size]) + got_ref[:half, c].astype(wide)).astype(low)

            def put(kept_half, c=c, value=value):
                keep[:quarter, c] = value[kept_half * quarter : (kept_half + 1) * quarter]
                send[:quarter, c] = value[(1 - kept_half) * quarter : (2 - kept_half) * quarter]

            pl.when(b[bit] == 0)(functools.partial(put, 0))
            pl.when(b[bit] != 0)(functools.partial(put, 1))

    return call(
        body,
        src.arrays + ([kept] if extra else []) + [got],
        [struct((quarter + extra, n), low)] * 2,
        bits=bits,
        after=after,
    )


def whole_call(body, arrays, shapes, bits, after=(), **kwargs):
    return call(body, arrays, shapes, bits=bits, after=after, limit=8, cost=690, **kwargs)


def halve(mine, got, bit, extra, bits, after=()):
    rows, cols = (mine.shape[0] - extra) // 2, mine.shape[1]

    def body(b, m, g, send, keep):
        for which, out in ((1 - b[bit], send), (b[bit], keep)):
            at = pl.ds(pl.multiple_of(which * rows, rows), rows)
            out[:rows, :] = (m[at, :].astype(wide) + g[at, :].astype(wide)).astype(low)
        if extra:
            total = (m[2 * rows :, :].astype(wide) + g[2 * rows :, :].astype(wide)).astype(low)
            send[rows:, :] = total
            keep[rows:, :] = total

    return whole_call(body, [mine, got], [struct((rows + extra, cols), low)] * 2, bits, after)


def add_up(mine, got, bits, after=()):
    def body(b, m, g, out):
        out[...] = (m[...].astype(wide) + g[...].astype(wide)).astype(low)

    return whole_call(body, [mine, got], [struct(mine.shape, low)], bits, after)


def add_last(mine, got, lengths, width, bits, after=()):
    rows = mine.shape[0] - SMALL

    def body(b, m, g, *refs):
        *vectors, out = refs
        out[...] = (m[:rows, :].astype(wide) + g[:rows, :].astype(wide)).astype(low)
        total = (m[rows:, :width].astype(wide) + g[rows:, :width].astype(wide)).astype(low).astype(wide)
        at = 0
        for vector in vectors:
            for c in range(0, vector.shape[0], width):
                vector[pl.ds(c, width)] = total[at : at + 1].reshape(-1)
                at += 1

    shapes = [struct((v,), wide) for v in lengths] + [struct((rows, mine.shape[1]), low)]
    return whole_call(body, [mine, got], shapes, bits, after, far_out=range(len(lengths)))


def join(mine, got, bit, bits, after=()):
    rows, cols = mine.shape

    def body(b, m, g, out):
        out[pl.ds(pl.multiple_of(b[bit] * rows, rows), rows), :] = m[...]
        out[pl.ds(pl.multiple_of((1 - b[bit]) * rows, rows), rows), :] = g[...]

    return whole_call(body, [mine, got], [struct((2 * rows, cols), low)], bits, after)


def widen(source, which, targets, before, bits, after=()):
    half = source.shape[0]
    parts = 4
    tile = half // parts
    old = [(i, a) for i, a in enumerate(before) if a is not None]

    def body(b, src, *refs):
        refs = refs[len(old) :]
        n = len(targets)
        outs, token, bufs, sems = refs[:n], refs[n], refs[n + 1 : -1], refs[-1]
        token[...] = jnp.zeros_like(token)
        start = (1 - b[CORE] if which else b[CORE]) * half
        copies = []
        for t in range(parts):
            at = 0
            for out, buf, (_, first, size) in zip(outs, bufs, targets):
                buf[t] = src[t * tile : (t + 1) * tile, at : at + size].astype(wide)
                rows = pl.ds(pl.multiple_of(start + t * tile, tile), tile)
                copies.append(pltpu.make_async_copy(buf.at[t], out.at[rows, pl.ds(first, size)], sems.at[len(copies)]))
                copies[-1].start()
                at += size
        for copy in copies:
            copy.wait()

    return call(
        body,
        [source] + [a for _, a in old],
        [struct(shape, wide) for shape, _, _ in targets] + [struct((8, 128), wide)],
        bits=bits,
        scratch=[pltpu.VMEM((parts, tile, size), wide) for _, _, size in targets]
        + [pltpu.SemaphoreType.DMA((parts * len(targets),))],
        aliases={1 + k: i for k, (i, _) in enumerate(old)},
        after=after,
        far=range(1, 1 + len(old)),
        hand_out=range(len(targets)),
        limit=12,
        cost=690,
    )


class Reduction:
    def __init__(self, src, order, targets, outs, bits, clock, tail, lengths=()):
        self.src, self.order, self.targets, self.outs = src, order, targets, outs
        self.bits, self.clock, self.tail, self.lengths = bits, clock, tail, lengths
        self.extra = SMALL if src.small else 0

    def step(self, fn, *args):
        out = fn(*args, self.bits, after=self.clock.now())
        self.clock.set(out[-1])
        return out

    def core_send(self):
        send, *self.kept = self.step(gradient_to_send, self.src)
        self.got = cross(send)

    def core_sum(self):
        out = gradient_sum(
            self.src, self.bits, self.got, self.kept[0] if self.kept else None, self.order[0], after=self.clock.now()
        )
        self.clock.set(out[-1])
        self.v = out[1]
        self.got = exchange(out[0], MASKS[self.order[0]])

    def halve(self, i):
        send, self.v = self.step(halve, self.v, self.got, self.order[i], self.extra)
        self.got = exchange(send, MASKS[self.order[i]])

    def first_sum(self):
        self.halve(1)

    def second_sum(self):
        self.halve(2)

    def third_sum(self):
        for mask in self.tail:
            (self.v,) = self.step(add_up, self.v, self.got)
            self.got = exchange(self.v, (mask, mask))

    def last_sum(self):
        if self.extra:
            *self.sums, self.v = self.step(add_last, self.v, self.got, self.lengths, self.src.small[0].shape[1])
        else:
            (self.v,) = self.step(add_up, self.v, self.got)
        self.got = exchange(self.v, MASKS[self.order[2]])

    def join(self, i):
        (self.v,) = self.step(join, self.v, self.got, self.order[i])
        self.got = exchange(self.v, MASKS[self.order[i - 1]]) if i else cross(self.v)

    def third_back(self):
        self.join(2)

    def second_back(self):
        self.join(1)

    def first_back(self):
        self.join(0)

    def write(self, which, source):
        before = [self.outs.get(name) for name, *_ in self.targets]
        *arrays, _ = self.step(widen, source, which, [t[1:] for t in self.targets], before)
        for (name, *_), array in zip(self.targets, arrays):
            self.outs[name] = array

    def finish_own(self):
        self.write(0, self.v)

    def finish(self):
        self.write(1, self.got)


class Clock:
    def __init__(self, start):
        self.last = start

    def now(self):
        return (self.last,)

    def set(self, value):
        self.last = value


def shards(
    embedded, seq_cotangent, pair_ids, w_qkv, b_qv, w_out, b_out, ln1_gain, ln1_bias, w_in, b_in, w_down, b_down,
    ln2_gain, ln2_bias, w_pool, b_pool,
):
    x = embedded[0]
    tokens, width = x.shape
    sents = tokens // SEQ
    ffn = w_in.shape[1]
    dp = lax.axis_size("dp")
    stream, place_dp = lax.axis_index("stream"), lax.axis_index("dp")
    first, second = (place_dp >> stream) & 1, (place_dp >> (1 - stream)) & 1
    bits = jnp.stack([stream, first, second, (place_dp >> 2) & 1, place_dp]).astype(jnp.int32)
    later = [
        w_in, w_down, seq_cotangent[0], w_pool, b_in, b_down, ln2_gain, ln2_bias, b_pool, pair_ids
    ]
    proj, probs, context, hidden, hidden_low, inv_one, *later = attention_forward(
        bits, x, w_qkv, b_qv, w_out, b_out, ln1_gain, ln1_bias, later
    )
    w_in, w_down, cotangent, w_pool, b_in, b_down, ln2_gain, ln2_bias, b_pool, ids = later
    hid3 = hidden.reshape(sents, SEQ, width)
    cot3 = cotangent.reshape(sents, SEQ, width)
    upper = (w_in, b_in, w_down, b_down, ln2_gain, ln2_bias)
    enc, act, gate_in, phi, normed_two, inv_two, first_low = ffn_group(0, hid3, cot3, upper, ())
    masks = [1 << i for i in range(dp.bit_length() - 1)]
    state = [enc, act]
    gathered = first_low
    group = 1
    order = [inv_two]
    for low_bit in range(0, len(masks), 2):
        span = 4 if low_bit + 1 < len(masks) else 2
        blocks = [gathered] + [exchange(gathered, (i << low_bit,) * 2) for i in range(1, span)]
        if group < SEQ // GROUP:
            state = ffn_group(group, hid3, cot3, upper, state, after=order)
            group += 1
            order = [state[-1]]
        gathered = put_in_order(blocks, bits, low_bit, order)
        order = [gathered]
    other = cross(gathered)
    while group < SEQ // GROUP:
        state = ffn_group(group, hid3, cot3, upper, state, after=order)
        group += 1
        order = [state[-1]]
    enc, act, gate, two, small_up, bin_sum = state
    grad_first, grad_w_pool, grad_b_pool = contrastive(
        gathered, other, bits, sents, ids, w_pool, b_pool, order
    )
    gate, two, small_up, bin_sum = ffn_first_back(
        cot3, grad_first, normed_two, inv_two, gate_in, phi, ln2_gain, w_down, gate, two, small_up, bin_sum
    )
    clock = Clock(small_up)
    act, gate, two = (v.reshape(tokens, -1) for v in (act, gate, two))
    tail = masks[3:]
    outs = {}
    shape_of = {"down": (ffn, width), "into": (width, ffn), "qkv": (width, 3 * width), "out": (width, width)}

    def target(name, first, size):
        return name, shape_of[name], first, size

    plain, third_first = (FIRST, SECOND, THIRD), (THIRD, FIRST, SECOND)
    rest = (outs, bits, clock, tail)
    down = Reduction(Sources([(act, two, 0, width)]), plain, [target("down", 0, width)], *rest)
    into = Reduction(Sources([(hidden_low, gate, 0, ffn)]), third_first, [target("into", 0, ffn)], *rest)
    lower = (two, gate, hidden, inv_one, proj, probs, w_in, w_out, ln1_gain, ln1_bias)

    def lower_reductions(grad_one, grad_proj, small_low, bqv):
        edge, end = 2 * width, 3 * width
        lengths = (width, width, width, ffn, width, width, width, 2 * width)
        part_a = Sources([(x, grad_proj, 0, edge)], [small_up, bin_sum, small_low, bqv])
        part_b = Sources([(x, grad_proj, edge, end), (context, grad_one, 0, width)])
        return (
            Reduction(part_a, plain, [target("qkv", 0, edge)], *rest, lengths),
            Reduction(part_b, plain, [target("qkv", edge, end - edge), target("out", 0, width)], *rest),
        )

    into.core_send()
    down.core_send()
    into.core_sum()
    down.core_sum()
    state = lower_backward(0, 2, *lower, after=clock.now())
    clock.set(state[-1])
    state = lower_backward(1, 2, *lower, before=state, after=clock.now())
    grad_one, grad_proj, small_low, bqv = state
    clock.set(bqv)
    lower_a, lower_b = lower_reductions(grad_one, grad_proj, small_low, bqv)
    down.first_sum()
    lower_a.core_send()
    into.first_sum()
    down.second_sum()
    lower_a.core_sum()
    into.second_sum()
    down.third_sum()
    lower_b.core_send()
    lower_a.first_sum()
    lower_b.core_sum()
    into.third_sum()
    lower_a.second_sum()
    grad_input, token = input_gradient(grad_proj, w_qkv, grad_one, after=clock.now())
    clock.set(token)
    down.last_sum()
    lower_b.first_sum()
    lower_a.third_sum()
    into.last_sum()
    down.third_back()
    lower_b.second_sum()
    into.third_back()
    lower_b.third_sum()
    down.second_back()
    lower_a.last_sum()
    lower_b.last_sum()
    into.second_back()
    lower_a.third_back()
    lower_b.third_back()
    down.first_back()
    lower_a.second_back()
    down.finish_own()
    lower_b.second_back()
    down.finish()
    lower_a.first_back()
    lower_a.finish_own()
    lower_a.finish()
    lower_b.first_back()
    into.first_back()
    lower_b.finish_own()
    into.finish_own()
    lower_b.finish()
    into.finish()
    g_ln2_gain, g_ln2_bias, g_b_down, g_b_in, g_ln1_gain, g_ln1_bias, g_b_out, g_b_qv = lower_a.sums
    return (
        enc.reshape(1, tokens, width),
        grad_input[None],
        outs["qkv"],
        g_b_qv,
        outs["out"],
        g_b_out,
        g_ln1_gain,
        g_ln1_bias,
        outs["into"],
        g_b_in,
        outs["down"],
        g_b_down,
        g_ln2_gain,
        g_ln2_bias,
        grad_w_pool,
        grad_b_pool,
    )


def solution(mesh):
    sharded = P("stream", "dp", None)
    return jax.shard_map(
        shards,
        mesh=mesh,
        in_specs=(sharded, sharded) + (P(),) * 15,
        out_specs=(sharded, sharded) + (P(),) * 14,
        check_vma=False,
    )
```

```python
import functools
import math

import jax
import jax.numpy as jnp
from jax import lax
from jax.experimental import pallas as pl
from jax.experimental.pallas import tpu as pltpu
from jax.sharding import PartitionSpec as P

HEAD_DIM = 64
SEQ = 64
GROUP = 16
CHUNK = 512

epsilon = 1e-06
score_scale = 10.0
margin_shift = score_scale * 0.3
root_half = 0.7071067811865476
gauss_norm = 0.3989422804014327

low = jnp.bfloat16
wide = jnp.float32
ANY = pl.BlockSpec(memory_space=pl.ANY)
VMEM = pl.BlockSpec(memory_space=pltpu.VMEM)
SMEM = pl.BlockSpec(memory_space=pltpu.SMEM)
HBM = pl.BlockSpec(memory_space=pltpu.HBM)
MIB = 1 << 20


def struct(shape, dtype):
    return jax.ShapeDtypeStruct(shape, dtype)


def call(body, ins, outs, bits=None, scratch=(), aliases=None, after=(), limit=10, far=(), far_out=(), hand_out=(), cost=460):
    first = 0 if bits is None else 1
    ins = [pltpu.with_memory_space_constraint(a, pltpu.HBM) if i in far else a for i, a in enumerate(ins)]

    def wrapped(*refs):
        body(*refs[: first + len(ins)], *refs[first + len(ins) + len(after) :])

    return pl.pallas_call(
        wrapped,
        in_specs=[SMEM] * first + [HBM if i in far else VMEM for i in range(len(ins))] + [ANY] * len(after),
        out_specs=[HBM if i in hand_out else VMEM for i in range(len(outs))],
        out_shape=[(pltpu.HBM if i in far_out or i in hand_out else pltpu.VMEM)(o.shape, o.dtype) for i, o in enumerate(outs)],
        scratch_shapes=list(scratch),
        input_output_aliases={first + k: v for k, v in (aliases or {}).items()},
        cost_estimate=pl.CostEstimate(flops=int(cost * 1.5 * 10**7), bytes_accessed=0, transcendentals=0),
        compiler_params=pltpu.CompilerParams(vmem_limit_bytes=limit * MIB),
    )(*([] if bits is None else [bits]), *ins, *after)


def row_of(ref, start=0, size=None):
    return ref[pl.ds(start, ref.shape[0] if size is None else size)].reshape(1, -1)


def mat_mul(a, b):
    return jnp.dot(a, b, preferred_element_type=wide)


def trans_left(a, b):
    return lax.dot_general(a, b, (((0,), (0,)), ((), ())), preferred_element_type=wide)


def trans_right(a, b):
    return lax.dot_general(a, b, (((1,), (1,)), ((), ())), preferred_element_type=wide)


def normalize(h):
    center = h - jnp.mean(h, axis=-1, keepdims=True)
    inv = lax.rsqrt(jnp.mean(center * center, axis=-1, keepdims=True) + epsilon)
    return center * inv, inv


def norm_input_grad(grad, normed, inv):
    return inv * (
        grad
        - jnp.mean(grad, axis=-1, keepdims=True)
        - normed * jnp.mean(grad * normed, axis=-1, keepdims=True)
    )


def split_heads(pair, first):
    zero = jnp.zeros_like(pair)
    return jnp.concatenate([jnp.where(first, pair, zero), jnp.where(first, zero, pair)], axis=0)


def join_heads(rows, first):
    return jnp.where(first, rows[:SEQ], rows[SEQ:])


def heads_product(left, right, cols, first):
    zero = jnp.zeros_like(right[0][:, cols[0]])
    out = ([], [])
    for c in cols:
        both = jnp.concatenate([left[0][:, c], left[1][:, c]], axis=0)
        apart = jnp.concatenate(
            [jnp.concatenate([right[0][:, c], zero], axis=1), jnp.concatenate([zero, right[1][:, c]], axis=1)], axis=0
        )
        rows = trans_left(both, apart)
        for i in range(2):
            out[i].append(join_heads(rows[:, i * 128 : (i + 1) * 128], first))
    return [jnp.concatenate(o, axis=1) for o in out]


def attention_forward(bits, x, w_qkv, b_qv, w_out, b_out, gain, bias, later):
    tokens, width = x.shape
    rows = 4 * SEQ
    pairs = width // (2 * HEAD_DIM)
    scale = 1.0 / math.sqrt(HEAD_DIM)

    def body(_bits, *refs):
        n = len(later)
        far, far_later, outs, near_later, near, sems = (
            refs[:7], refs[7 : 7 + n], refs[7 + n : 13 + n], refs[13 + n : 13 + 2 * n], refs[13 + 2 * n : -1], refs[-1]
        )
        proj_ref, prob_ref, ctx_ref, hid_ref, low_ref, inv_ref = outs
        x_ref, wq_ref, bqv_ref, wo_ref, bo_ref, g_ref, b_ref = near
        pairs_of = zip(far + far_later, near + near_later)
        copies = [pltpu.make_async_copy(f, near_f, sems.at[i]) for i, (f, near_f) in enumerate(pairs_of)]
        for copy in copies[:3]:
            copy.start()
        for copy in copies[:3]:
            copy.wait()
        for copy in copies[3:]:
            copy.start()
        first = lax.broadcasted_iota(jnp.int32, (SEQ, 128), 1) < HEAD_DIM
        cols = [slice(p * 128, (p + 1) * 128) for p in range(pairs)]

        def project(block):
            for part in range(3):
                c = slice(part * width, (part + 1) * width)
                value = mat_mul(x_ref[block, :], wq_ref[:, c])
                if part != 1:
                    value = value + row_of(bqv_ref, (part // 2) * width, width)
                proj_ref[block, c] = value.astype(low)

        def attend(base):
            for two in range(2):
                at = [slice(base + (2 * two + i) * SEQ, base + (2 * two + i + 1) * SEQ) for i in range(2)]
                probs = []
                for r in at:
                    q = proj_ref[r, :width]
                    k = proj_ref[r, width : 2 * width]
                    scores = (
                        jnp.concatenate([trans_right(k[:, c], split_heads(q[:, c], first)) for c in cols], axis=1) * scale
                    )
                    e = jnp.exp(scores - jnp.max(scores, axis=0, keepdims=True))
                    probs.append((e * (1.0 / jnp.sum(e, axis=0, keepdims=True))).astype(low))
                    prob_ref[r, :] = probs[-1]
                values = [proj_ref[r, 2 * width :] for r in at]
                for r, context in zip(at, heads_product(probs, values, cols, first)):
                    ctx_ref[r, :] = context.astype(low)

        def finish(block):
            h = x_ref[block, :].astype(wide) + mat_mul(ctx_ref[block, :], wo_ref[...]) + row_of(bo_ref)
            normed, inv = normalize(h)
            hidden = normed * row_of(g_ref) + row_of(b_ref)
            hid_ref[block, :] = hidden
            low_ref[block, :] = hidden.astype(low)
            inv_ref[block, :] = inv

        blocks = [slice(start, start + rows) for start in range(0, tokens, rows)]
        project(blocks[0])
        for copy in copies[3:7]:
            copy.wait()
        for i, block in enumerate(blocks):
            if i + 1 < len(blocks):
                project(blocks[i + 1])
            attend(block.start)
            if i:
                finish(blocks[i - 1])
        finish(blocks[-1])

        for copy in copies[7:]:
            copy.wait()

    return call(
        body,
        [x, w_qkv, b_qv, w_out, b_out, gain, bias] + later,
        [
            struct((tokens, 3 * width), low),
            struct((tokens, width), low),
            struct((tokens, width), low),
            struct((tokens, width), wide),
            struct((tokens, width), low),
            struct((tokens, 1), wide),
        ]
        + [struct(v.shape, v.dtype) for v in later],
        scratch=[pltpu.VMEM(v.shape, v.dtype) for v in (x, w_qkv, b_qv, w_out, b_out, gain, bias)]
        + [pltpu.SemaphoreType.DMA((7 + len(later),))],
        bits=bits,
        far=range(7 + len(later)),
        limit=14,
    )


def ffn_forward_rows(hidden, wi_ref, bi_ref, wd_ref, bd_ref, store_act, store_gate_in):
    h_low = hidden.astype(low)
    total = hidden + row_of(bd_ref)
    for c in range(0, wi_ref.shape[1], CHUNK):
        u = mat_mul(h_low, wi_ref[:, c : c + CHUNK]) + row_of(bi_ref, c, CHUNK)
        phi = 0.5 + 0.5 * lax.erf(u * root_half)
        act = (u * phi).astype(low)
        store_act(c, act)
        store_gate_in(c, u.astype(low), phi.astype(low))
        total = total + mat_mul(act, wd_ref[c : c + CHUNK, :])
    return normalize(total)


def ffn_backward_rows(grad_block, normed, inv, gain, wd_ref, gate_in, store_gate, small_ref, bin_ref):
    grad_two = norm_input_grad(grad_block * gain, normed, inv)
    small_ref[0:1, :] += jnp.sum(grad_block * normed, axis=0, keepdims=True)
    small_ref[1:2, :] += jnp.sum(grad_block, axis=0, keepdims=True)
    small_ref[2:3, :] += jnp.sum(grad_two, axis=0, keepdims=True)
    grad_low = grad_two.astype(low)
    for c in range(0, wd_ref.shape[0], CHUNK):
        u, phi = gate_in(c)
        slope = phi + u * jnp.exp(u * u * low(-0.5)) * low(gauss_norm)
        gate = trans_right(grad_low, wd_ref[c : c + CHUNK, :]) * slope.astype(wide)
        bin_ref[:, c : c + CHUNK] += jnp.sum(gate, axis=0, keepdims=True)
        store_gate(c, gate.astype(low))
    return grad_low


def ffn_group(index, hidden, cot, upper, state, after=()):
    w_in, b_in, w_down, b_down, gain, bias = upper
    sents, _, width = hidden.shape
    ffn = w_in.shape[1]
    rows = sents * GROUP
    at = slice(index * GROUP, (index + 1) * GROUP)
    first = index == 0
    second = index == 1

    def stores(act_ref, u_ref, phi_ref):
        def store_act(c, v):
            act_ref[:, at, c : c + CHUNK] = v.reshape(sents, GROUP, CHUNK)

        def store_gate_in(c, u, phi):
            u_ref[:, c : c + CHUNK] = u
            phi_ref[:, c : c + CHUNK] = phi

        return store_act, store_gate_in

    def forward(h_ref, wi_ref, bi_ref, wd_ref, bd_ref, act_ref, u_ref, phi_ref):
        return ffn_forward_rows(
            h_ref[:, at, :].reshape(rows, width), wi_ref, bi_ref, wd_ref, bd_ref, *stores(act_ref, u_ref, phi_ref)
        )

    def body_first(h_ref, wi_ref, bi_ref, wd_ref, bd_ref, g_ref, b_ref, enc_hbm, act_ref, u_ref, phi_ref, n_ref, inv_ref, first_ref, enc_ref, sem):
        normed, inv = forward(h_ref, wi_ref, bi_ref, wd_ref, bd_ref, act_ref, u_ref, phi_ref)
        n_ref[...] = normed
        inv_ref[...] = inv
        block = (normed * row_of(g_ref) + row_of(b_ref)).reshape(sents, GROUP, width)
        enc_ref[...] = block.astype(low)
        copy = pltpu.make_async_copy(enc_ref, enc_hbm.at[:, pl.ds(index * GROUP, GROUP), :], sem)
        copy.start()
        first_ref[...] = block[:, 0, :].astype(low)
        copy.wait()

    enc_shape = struct((sents, SEQ, width), low)
    enc_scratch = [pltpu.VMEM((sents, GROUP, width), low), pltpu.SemaphoreType.DMA]
    act_shape = struct((sents, SEQ, ffn), low)
    if first:
        return call(
            body_first,
            [hidden, w_in, b_in, w_down, b_down, gain, bias],
            [
                enc_shape,
                act_shape,
                struct((rows, ffn), low),
                struct((rows, ffn), low),
                struct((rows, width), wide),
                struct((rows, 1), wide),
                struct((sents, width), low),
            ],
            scratch=enc_scratch,
            hand_out=[0],
        )

    def body(h_ref, cot_ref, wi_ref, bi_ref, wd_ref, bd_ref, g_ref, b_ref, *refs):
        refs = refs[2 if second else 4 :]
        if not second:
            sin_ref, bin_in_ref = refs[:2]
            refs = refs[2:]
        enc_hbm, act_ref, gate_ref, two_ref, small_ref, bin_ref, u_ref, phi_ref, enc_ref, sem = refs
        small_ref[...] = jnp.zeros_like(small_ref) if second else sin_ref[...]
        bin_ref[...] = jnp.zeros_like(bin_ref) if second else bin_in_ref[...]

        def store_gate(c, v):
            gate_ref[:, at, c : c + CHUNK] = v.reshape(sents, GROUP, CHUNK)

        normed, inv = forward(h_ref, wi_ref, bi_ref, wd_ref, bd_ref, act_ref, u_ref, phi_ref)
        gain_row = row_of(g_ref)
        enc_ref[...] = (normed * gain_row + row_of(b_ref)).astype(low).reshape(sents, GROUP, width)
        copy = pltpu.make_async_copy(enc_ref, enc_hbm.at[:, pl.ds(index * GROUP, GROUP), :], sem)
        copy.start()
        grad_block = cot_ref[:, at, :].reshape(rows, width).astype(wide)
        got = ffn_backward_rows(
            grad_block, normed, inv, gain_row, wd_ref, lambda c: (u_ref[:, c : c + CHUNK], phi_ref[:, c : c + CHUNK]),
            store_gate, small_ref, bin_ref,
        )
        two_ref[:, at, :] = got.reshape(sents, GROUP, width)
        copy.wait()

    aliases = {8: 0, 9: 1}
    if not second:
        aliases.update({10: 2, 11: 3})
    return call(
        body,
        [hidden, cot, w_in, b_in, w_down, b_down, gain, bias] + list(state),
        [enc_shape, act_shape, act_shape, enc_shape, struct((8, width), wide), struct((1, ffn), wide)],
        scratch=[pltpu.VMEM((rows, ffn), low)] * 2 + enc_scratch,
        aliases=aliases,
        after=after,
        far=[8],
        hand_out=[0],
    )


def ffn_first_back(cot, grad_first, normed, inv, gate_in, phi, gain, w_down, gate, two, small, bin_sum):
    sents, _, width = cot.shape
    ffn = w_down.shape[0]
    rows = sents * GROUP
    at = slice(0, GROUP)

    def body(cot_ref, first_ref, n_ref, inv_ref, u_ref, phi_ref, g_ref, wd_ref, sin_ref, bin_in_ref, _g, _t, gate_ref, two_ref, small_ref, bin_ref):
        small_ref[...] = sin_ref[...]
        bin_ref[...] = bin_in_ref[...]
        position = lax.broadcasted_iota(jnp.int32, (sents, GROUP, width), 1)
        at_first = jnp.broadcast_to(first_ref[...][:, None, :], (sents, GROUP, width))
        grad_block = cot_ref[:, at, :].astype(wide) + jnp.where(position == 0, at_first, 0.0)

        def store_gate(c, v):
            gate_ref[:, at, c : c + CHUNK] = v.reshape(sents, GROUP, CHUNK)

        got = ffn_backward_rows(
            grad_block.reshape(rows, width), n_ref[...], inv_ref[...], row_of(g_ref), wd_ref,
            lambda c: (u_ref[:, c : c + CHUNK], phi_ref[:, c : c + CHUNK]), store_gate, small_ref, bin_ref,
        )
        two_ref[:, at, :] = got.reshape(sents, GROUP, width)

    return call(
        body,
        [cot, grad_first, normed, inv, gate_in, phi, gain, w_down, small, bin_sum, gate, two],
        [struct((sents, SEQ, ffn), low), struct((sents, SEQ, width), low), struct((8, width), wide), struct((1, ffn), wide)],
        aliases={10: 0, 11: 1},
    )


def lower_backward(part, parts, two, gate, hidden, inv, proj, probs, w_in, w_out, gain, bias, before=None, after=()):
    tokens, width = hidden.shape
    ffn = w_in.shape[1]
    rows = 4 * SEQ
    steps = tokens // rows // parts
    pairs = width // (2 * HEAD_DIM)
    scale = 1.0 / math.sqrt(HEAD_DIM)
    fresh = before is None

    def body(two_ref, gate_ref, hid_ref, inv_ref, proj_ref, prob_ref, wi_ref, wo_ref, g_ref, b_ref, *refs):
        if not fresh:
            sin_ref, bin_ref = refs[2:4]
            refs = refs[4:]
        one_ref, gp_ref, small_ref, bqv_ref, ctx_ref = refs
        small_ref[...] = jnp.zeros_like(small_ref) if fresh else sin_ref[...]
        bqv_ref[...] = jnp.zeros_like(bqv_ref) if fresh else bin_ref[...]
        first = lax.broadcasted_iota(jnp.int32, (SEQ, 128), 1) < HEAD_DIM
        cols = [slice(p * 128, (p + 1) * 128) for p in range(pairs)]

        gain_row = row_of(g_ref)

        def first_norm(block, at):
            grad_hidden = two_ref[block, :].astype(wide) + trans_right(gate_ref[block, :], wi_ref[...])
            normed = (hid_ref[block, :] - row_of(b_ref)) * (1.0 / gain_row)
            small_ref[0:1, :] += jnp.sum(grad_hidden * normed, axis=0, keepdims=True)
            small_ref[1:2, :] += jnp.sum(grad_hidden, axis=0, keepdims=True)
            grad_one = norm_input_grad(grad_hidden * gain_row, normed, inv_ref[block, :])
            small_ref[2:3, :] += jnp.sum(grad_one, axis=0, keepdims=True)
            one_ref[block, :] = grad_one.astype(low)
            ctx_ref[at : at + rows, :] = trans_right(grad_one.astype(low), wo_ref[...]).astype(low)

        def attention(base, from_ctx):
            sum_q = jnp.zeros((1, width), wide)
            sum_v = jnp.zeros((1, width), wide)
            for two in range(2):
                at = [slice(base + (2 * two + i) * SEQ, base + (2 * two + i + 1) * SEQ) for i in range(2)]
                grads = []
                for i, r in enumerate(at):
                    q_all = proj_ref[r, :width]
                    v = proj_ref[r, 2 * width :]
                    start = from_ctx + (2 * two + i) * SEQ
                    d_all = ctx_ref[start : start + SEQ, :]
                    p_low = prob_ref[r, :]
                    q = [split_heads(q_all[:, c], first) for c in cols]
                    d = [split_heads(d_all[:, c], first) for c in cols]
                    p = p_low.astype(wide)
                    grad_p = jnp.concatenate([trans_right(v[:, c], dd) for c, dd in zip(cols, d)], axis=1)
                    grad_v = jnp.concatenate([mat_mul(p_low[:, c], dd) for c, dd in zip(cols, d)], axis=1)
                    gp = grad_p * p
                    grad_s = (gp - p * jnp.sum(gp, axis=0, keepdims=True)).astype(low)
                    grad_k = jnp.concatenate([mat_mul(grad_s[:, c], qq) for c, qq in zip(cols, q)], axis=1) * scale
                    sum_v += jnp.sum(grad_v, axis=0, keepdims=True)
                    gp_ref[r, width : 2 * width] = grad_k.astype(low)
                    gp_ref[r, 2 * width :] = grad_v.astype(low)
                    grads.append(grad_s)
                keys = [proj_ref[r, width : 2 * width] for r in at]
                for r, product in zip(at, heads_product(grads, keys, cols, first)):
                    grad_q = product * scale
                    sum_q += jnp.sum(grad_q, axis=0, keepdims=True)
                    gp_ref[r, :width] = grad_q.astype(low)
            bqv_ref[0:1, :] += sum_q
            bqv_ref[1:2, :] += sum_v

        base = part * steps * rows
        first_norm(slice(base, base + rows), 0)
        for i in range(steps):
            if i + 1 < steps:
                start = base + (i + 1) * rows
                first_norm(slice(start, start + rows), ((i + 1) % 2) * rows)
            attention(base + i * rows, (i % 2) * rows)

    return call(
        body,
        [two, gate, hidden, inv, proj, probs, w_in, w_out, gain, bias] + ([] if fresh else list(before)),
        [struct((tokens, width), low), struct((tokens, 3 * width), low), struct((8, width), wide), struct((8, width), wide)],
        scratch=[pltpu.VMEM((2 * rows, width), low)],
        aliases=None if fresh else {10: 0, 11: 1},
        after=after,
    )


def input_gradient(grad_proj, w_qkv, grad_one, after=()):
    tokens, width = grad_one.shape
    rows = tokens // 2

    def body(gp_ref, w_ref, one_ref, out_ref, token):
        token[...] = jnp.zeros_like(token)

        for start in range(0, tokens, rows):
            block = slice(start, start + rows)
            out_ref[block, :] = (one_ref[block, :].astype(wide) + trans_right(gp_ref[block, :], w_ref[...])).astype(low)

    return call(
        body, [grad_proj, w_qkv, grad_one], [struct((tokens, width), low), struct((8, 128), wide)], after=after, far_out=[0]
    )


def pooler_gradients(flat, id_row, w_pool, b_pool):
    total = flat.shape[0] // 2
    pooled = jnp.tanh(mat_mul(flat, w_pool) + b_pool)
    inv_len = lax.rsqrt(jnp.sum(pooled * pooled, axis=-1, keepdims=True) + epsilon)
    unit = pooled * inv_len
    embed = unit.astype(low)
    zero, one = embed[:total], embed[total:]
    square = (total, total)
    eye = (lax.broadcasted_iota(jnp.int32, square, 0) == lax.broadcasted_iota(jnp.int32, square, 1)).astype(wide)
    logits = score_scale * trans_right(zero, one) - margin_shift * eye
    id_column = jnp.sum(jnp.where(eye > 0, id_row, 0), axis=1, keepdims=True)
    masked = jnp.where(id_column == id_row, logits, -jnp.inf)

    def soft(axis):
        e = jnp.exp(masked - jnp.max(masked, axis=axis, keepdims=True))
        return (score_scale * (e / jnp.sum(e, axis=axis, keepdims=True) - eye)).astype(low)

    by_row, by_col = soft(1), soft(0)
    grad_embed = jnp.concatenate(
        [mat_mul(by_row, one) + mat_mul(by_col, one), trans_left(by_row, zero) + trans_left(by_col, zero)], axis=0
    )
    grad_pre = (
        inv_len * (grad_embed - unit * jnp.sum(unit * grad_embed, axis=-1, keepdims=True)) * (1.0 - pooled * pooled)
    )
    pre_low = grad_pre.astype(low)
    return pre_low, trans_left(flat, pre_low), jnp.sum(grad_pre, axis=0, keepdims=True)


def contrastive(own, got, bits, sents, ids, w_pool, b_pool, after):
    total, width = own.shape
    if total > 512:
        start = bits[CORE] * total + bits[PLACE] * sents
        flat = jnp.where(bits[CORE] == 0, jnp.concatenate([own, got]), jnp.concatenate([got, own]))
        pre_low, grad_w, grad_b = pooler_gradients(flat, ids.reshape(1, -1), w_pool, b_pool.reshape(1, -1))
        return trans_right(lax.dynamic_slice_in_dim(pre_low, start, sents), w_pool), grad_w, grad_b.reshape(-1)

    def body(b, own_ref, got_ref, ids_ref, w_ref, b_ref, first_ref, gw_ref, gb_ref, flat_ref, pre_ref):
        flat_ref[pl.ds(pl.multiple_of(b[CORE] * total, total), total), :] = own_ref[...]
        flat_ref[pl.ds(pl.multiple_of((1 - b[CORE]) * total, total), total), :] = got_ref[...]
        pre_low, grad_w, grad_b = pooler_gradients(flat_ref[...], row_of(ids_ref), w_ref[...], row_of(b_ref))
        pre_ref[...] = pre_low
        gw_ref[...] = grad_w
        gb_ref[...] = grad_b.reshape(-1)
        first_ref[...] = trans_right(pre_ref[pl.ds(pl.multiple_of(b[CORE] * total + b[PLACE] * sents, sents), sents), :], w_ref[...])

    return call(
        body,
        [own, got, ids, w_pool, b_pool],
        [struct((sents, width), wide), struct((width, width), wide), struct((width,), wide)],
        bits=bits,
        scratch=[pltpu.VMEM((2 * total, width), low)] * 2,
        after=after,
        far_out=[1, 2],
    )


def put_in_order(blocks, bits, low_bit, after):
    rows, width = blocks[0].shape

    def body(b, *refs):
        me = (b[PLACE] >> low_bit) & (len(blocks) - 1)
        for i, ref in enumerate(refs[:-1]):
            at = pl.multiple_of((me ^ i) * rows, rows)
            refs[-1][pl.ds(at, rows), :] = ref[...]

    return call(
        body, blocks, [struct((rows * len(blocks), width), low)], bits=bits, after=after, limit=8, cost=920
    )[0]


CORE, FIRST, SECOND, THIRD, PLACE = range(5)
SMALL = 16
MASKS = {FIRST: (1, 2), SECOND: (2, 1), THIRD: (4, 4)}


def exchange(a, masks):
    size = lax.axis_size("dp")
    pairs = [(core * size + i, core * size + (i ^ masks[core])) for core in range(2) for i in range(size)]
    return lax.ppermute(a, ("stream", "dp"), pairs)


def cross(a):
    return lax.ppermute(a, "stream", [(0, 1), (1, 0)])


class Sources:
    def __init__(self, products, small=()):
        self.products = products
        self.small = list(small)
        self.m = products[0][0].shape[1]
        self.n = sum(hi - lo for _, _, lo, hi in products)
        self.arrays = [a for left, right, _, _ in products for a in (left, right)]

    def pieces(self, refs):
        at = 0
        for i, (_, _, lo, hi) in enumerate(self.products):
            yield refs[2 * i], refs[2 * i + 1], lo, at, hi - lo
            at += hi - lo


def gradient_to_send(src, bits, after=()):
    m, n = src.m, src.n
    half = m // 2
    count = len(src.arrays)
    small = src.small

    def body(b, *refs):
        out = refs[count + len(small)]
        rows = pl.ds(pl.multiple_of((1 - b[CORE]) * half, 128), half)
        for a, g, lo, at, size in src.pieces(refs):
            out[:half, at : at + size] = trans_left(a[:, rows], g[:, lo : lo + size]).astype(low)
        if small:
            up, bin_sum, down, bqv = refs[count : count + 4]
            kept = refs[-1]
            width = up.shape[1]
            parts = [up[:3]] + [bin_sum[:, c : c + width] for c in range(0, bin_sum.shape[1], width)] + [down[:3], bqv[:2]]
            parts.append(jnp.zeros((SMALL - sum(p.shape[0] for p in parts), width), wide))
            kept[...] = jnp.concatenate(parts, axis=0).astype(low)
            out[half:, :] = jnp.zeros((SMALL, n), low)
            out[half:, :width] = kept[...]

    shapes = [struct((half + (SMALL if small else 0), n), low)]
    if small:
        shapes.append(struct((SMALL, small[0].shape[1]), low))
    return call(body, src.arrays + small, shapes, bits=bits, after=after)


def gradient_sum(src, bits, got, kept, bit, after=()):
    m, n = src.m, src.n
    half, quarter = m // 2, m // 4
    count = len(src.arrays)
    extra = SMALL if src.small else 0

    def body(b, *refs):
        got_ref, send, keep = refs[-3:]
        if extra:
            mine = refs[count]
            total = (mine[...].astype(wide) + got_ref[half:, : mine.shape[1]].astype(wide)).astype(low)
            for ref in (send, keep):
                ref[quarter:, :] = jnp.zeros((SMALL, n), low)
                ref[quarter:, : mine.shape[1]] = total
        rows = pl.ds(pl.multiple_of(b[CORE] * half, 128), half)
        for a, g, lo, at, size in src.pieces(refs):
            c = slice(at, at + size)
            value = (trans_left(a[:, rows], g[:, lo : lo + size]) + got_ref[:half, c].astype(wide)).astype(low)

            def put(kept_half, c=c, value=value):
                keep[:quarter, c] = value[kept_half * quarter : (kept_half + 1) * quarter]
                send[:quarter, c] = value[(1 - kept_half) * quarter : (2 - kept_half) * quarter]

            pl.when(b[bit] == 0)(functools.partial(put, 0))
            pl.when(b[bit] != 0)(functools.partial(put, 1))

    return call(
        body,
        src.arrays + ([kept] if extra else []) + [got],
        [struct((quarter + extra, n), low)] * 2,
        bits=bits,
        after=after,
    )


def whole_call(body, arrays, shapes, bits, after=(), **kwargs):
    return call(body, arrays, shapes, bits=bits, after=after, limit=8, cost=920, **kwargs)


def halve(mine, got, bit, extra, bits, after=()):
    rows, cols = (mine.shape[0] - extra) // 2, mine.shape[1]

    def body(b, m, g, send, keep):
        for which, out in ((1 - b[bit], send), (b[bit], keep)):
            at = pl.ds(pl.multiple_of(which * rows, rows), rows)
            out[:rows, :] = (m[at, :].astype(wide) + g[at, :].astype(wide)).astype(low)
        if extra:
            total = (m[2 * rows :, :].astype(wide) + g[2 * rows :, :].astype(wide)).astype(low)
            send[rows:, :] = total
            keep[rows:, :] = total

    return whole_call(body, [mine, got], [struct((rows + extra, cols), low)] * 2, bits, after)


def add_up(mine, got, bits, after=()):
    def body(b, m, g, out):
        out[...] = (m[...].astype(wide) + g[...].astype(wide)).astype(low)

    return whole_call(body, [mine, got], [struct(mine.shape, low)], bits, after)


def add_last(mine, got, lengths, width, bits, after=()):
    rows = mine.shape[0] - SMALL

    def body(b, m, g, *refs):
        *vectors, out = refs
        out[...] = (m[:rows, :].astype(wide) + g[:rows, :].astype(wide)).astype(low)
        total = (m[rows:, :width].astype(wide) + g[rows:, :width].astype(wide)).astype(low).astype(wide)
        at = 0
        for vector in vectors:
            for c in range(0, vector.shape[0], width):
                vector[pl.ds(c, width)] = total[at : at + 1].reshape(-1)
                at += 1

    shapes = [struct((v,), wide) for v in lengths] + [struct((rows, mine.shape[1]), low)]
    return whole_call(body, [mine, got], shapes, bits, after, far_out=range(len(lengths)))


def join(mine, got, bit, bits, after=()):
    rows, cols = mine.shape

    def body(b, m, g, out):
        out[pl.ds(pl.multiple_of(b[bit] * rows, rows), rows), :] = m[...]
        out[pl.ds(pl.multiple_of((1 - b[bit]) * rows, rows), rows), :] = g[...]

    return whole_call(body, [mine, got], [struct((2 * rows, cols), low)], bits, after)


def widen(source, which, targets, before, bits, after=()):
    half = source.shape[0]
    parts = 4
    tile = half // parts
    old = [(i, a) for i, a in enumerate(before) if a is not None]

    def body(b, src, *refs):
        refs = refs[len(old) :]
        n = len(targets)
        outs, token, bufs, sems = refs[:n], refs[n], refs[n + 1 : -1], refs[-1]
        token[...] = jnp.zeros_like(token)
        start = (1 - b[CORE] if which else b[CORE]) * half
        copies = []
        for t in range(parts):
            at = 0
            for out, buf, (_, first, size) in zip(outs, bufs, targets):
                buf[t] = src[t * tile : (t + 1) * tile, at : at + size].astype(wide)
                rows = pl.ds(pl.multiple_of(start + t * tile, tile), tile)
                copies.append(pltpu.make_async_copy(buf.at[t], out.at[rows, pl.ds(first, size)], sems.at[len(copies)]))
                copies[-1].start()
                at += size
        for copy in copies:
            copy.wait()

    return call(
        body,
        [source] + [a for _, a in old],
        [struct(shape, wide) for shape, _, _ in targets] + [struct((8, 128), wide)],
        bits=bits,
        scratch=[pltpu.VMEM((parts, tile, size), wide) for _, _, size in targets]
        + [pltpu.SemaphoreType.DMA((parts * len(targets),))],
        aliases={1 + k: i for k, (i, _) in enumerate(old)},
        after=after,
        far=range(1, 1 + len(old)),
        hand_out=range(len(targets)),
        limit=12,
        cost=920,
    )


class Reduction:
    def __init__(self, src, order, targets, outs, bits, clock, tail, lengths=()):
        self.src, self.order, self.targets, self.outs = src, order, targets, outs
        self.bits, self.clock, self.tail, self.lengths = bits, clock, tail, lengths
        self.extra = SMALL if src.small else 0

    def step(self, fn, *args):
        out = fn(*args, self.bits, after=self.clock.now())
        self.clock.set(out[-1])
        return out

    def core_send(self):
        send, *self.kept = self.step(gradient_to_send, self.src)
        self.got = cross(send)

    def core_sum(self):
        out = gradient_sum(
            self.src, self.bits, self.got, self.kept[0] if self.kept else None, self.order[0], after=self.clock.now()
        )
        self.clock.set(out[-1])
        self.v = out[1]
        self.got = exchange(out[0], MASKS[self.order[0]])

    def halve(self, i):
        send, self.v = self.step(halve, self.v, self.got, self.order[i], self.extra)
        self.got = exchange(send, MASKS[self.order[i]])

    def first_sum(self):
        self.halve(1)

    def second_sum(self):
        self.halve(2)

    def third_sum(self):
        for mask in self.tail:
            (self.v,) = self.step(add_up, self.v, self.got)
            self.got = exchange(self.v, (mask, mask))

    def last_sum(self):
        if self.extra:
            *self.sums, self.v = self.step(add_last, self.v, self.got, self.lengths, self.src.small[0].shape[1])
        else:
            (self.v,) = self.step(add_up, self.v, self.got)
        self.got = exchange(self.v, MASKS[self.order[2]])

    def join(self, i):
        (self.v,) = self.step(join, self.v, self.got, self.order[i])
        self.got = exchange(self.v, MASKS[self.order[i - 1]]) if i else cross(self.v)

    def third_back(self):
        self.join(2)

    def second_back(self):
        self.join(1)

    def first_back(self):
        self.join(0)

    def write(self, which, source):
        before = [self.outs.get(name) for name, *_ in self.targets]
        *arrays, _ = self.step(widen, source, which, [t[1:] for t in self.targets], before)
        for (name, *_), array in zip(self.targets, arrays):
            self.outs[name] = array

    def finish_own(self):
        self.write(0, self.v)

    def finish(self):
        self.write(1, self.got)


class Clock:
    def __init__(self, start):
        self.last = start

    def now(self):
        return (self.last,)

    def set(self, value):
        self.last = value


def shards(
    embedded, seq_cotangent, pair_ids, w_qkv, b_qv, w_out, b_out, ln1_gain, ln1_bias, w_in, b_in, w_down, b_down,
    ln2_gain, ln2_bias, w_pool, b_pool,
):
    x = embedded[0]
    tokens, width = x.shape
    sents = tokens // SEQ
    ffn = w_in.shape[1]
    dp = lax.axis_size("dp")
    stream, place_dp = lax.axis_index("stream"), lax.axis_index("dp")
    first, second = (place_dp >> stream) & 1, (place_dp >> (1 - stream)) & 1
    bits = jnp.stack([stream, first, second, (place_dp >> 2) & 1, place_dp]).astype(jnp.int32)
    later = [
        w_in, w_down, seq_cotangent[0], w_pool, b_in, b_down, ln2_gain, ln2_bias, b_pool, pair_ids
    ]
    proj, probs, context, hidden, hidden_low, inv_one, *later = attention_forward(
        bits, x, w_qkv, b_qv, w_out, b_out, ln1_gain, ln1_bias, later
    )
    w_in, w_down, cotangent, w_pool, b_in, b_down, ln2_gain, ln2_bias, b_pool, ids = later
    hid3 = hidden.reshape(sents, SEQ, width)
    cot3 = cotangent.reshape(sents, SEQ, width)
    upper = (w_in, b_in, w_down, b_down, ln2_gain, ln2_bias)
    enc, act, gate_in, phi, normed_two, inv_two, first_low = ffn_group(0, hid3, cot3, upper, ())
    masks = [1 << i for i in range(dp.bit_length() - 1)]
    state = [enc, act]
    gathered = first_low
    group = 1
    order = [inv_two]
    for low_bit in range(0, len(masks), 2):
        span = 4 if low_bit + 1 < len(masks) else 2
        blocks = [gathered] + [exchange(gathered, (i << low_bit,) * 2) for i in range(1, span)]
        if group < SEQ // GROUP:
            state = ffn_group(group, hid3, cot3, upper, state, after=order)
            group += 1
            order = [state[-1]]
        gathered = put_in_order(blocks, bits, low_bit, order)
        order = [gathered]
    other = cross(gathered)
    while group < SEQ // GROUP:
        state = ffn_group(group, hid3, cot3, upper, state, after=order)
        group += 1
        order = [state[-1]]
    enc, act, gate, two, small_up, bin_sum = state
    grad_first, grad_w_pool, grad_b_pool = contrastive(
        gathered, other, bits, sents, ids, w_pool, b_pool, order
    )
    gate, two, small_up, bin_sum = ffn_first_back(
        cot3, grad_first, normed_two, inv_two, gate_in, phi, ln2_gain, w_down, gate, two, small_up, bin_sum
    )
    clock = Clock(small_up)
    act, gate, two = (v.reshape(tokens, -1) for v in (act, gate, two))
    tail = masks[3:]
    outs = {}
    shape_of = {"down": (ffn, width), "into": (width, ffn), "qkv": (width, 3 * width), "out": (width, width)}

    def target(name, first, size):
        return name, shape_of[name], first, size

    plain, third_first = (FIRST, SECOND, THIRD), (THIRD, FIRST, SECOND)
    rest = (outs, bits, clock, tail)
    down = Reduction(Sources([(act, two, 0, width)]), plain, [target("down", 0, width)], *rest)
    into = Reduction(Sources([(hidden_low, gate, 0, ffn)]), third_first, [target("into", 0, ffn)], *rest)
    lower = (two, gate, hidden, inv_one, proj, probs, w_in, w_out, ln1_gain, ln1_bias)

    def lower_reductions(grad_one, grad_proj, small_low, bqv):
        edge, end = 2 * width, 3 * width
        lengths = (width, width, width, ffn, width, width, width, 2 * width)
        part_a = Sources([(x, grad_proj, 0, edge)], [small_up, bin_sum, small_low, bqv])
        part_b = Sources([(x, grad_proj, edge, end), (context, grad_one, 0, width)])
        return (
            Reduction(part_a, plain, [target("qkv", 0, edge)], *rest, lengths),
            Reduction(part_b, plain, [target("qkv", edge, end - edge), target("out", 0, width)], *rest),
        )

    into.core_send()
    down.core_send()
    into.core_sum()
    down.core_sum()
    state = lower_backward(0, 2, *lower, after=clock.now())
    clock.set(state[-1])
    state = lower_backward(1, 2, *lower, before=state, after=clock.now())
    grad_one, grad_proj, small_low, bqv = state
    clock.set(bqv)
    lower_a, lower_b = lower_reductions(grad_one, grad_proj, small_low, bqv)
    lower_a.core_send()
    down.first_sum()
    lower_a.core_sum()
    down.second_sum()
    into.first_sum()
    lower_b.core_send()
    down.third_sum()
    lower_a.first_sum()
    into.second_sum()
    lower_b.core_sum()
    lower_a.second_sum()
    into.third_sum()
    grad_input, token = input_gradient(grad_proj, w_qkv, grad_one, after=clock.now())
    clock.set(token)
    lower_b.first_sum()
    down.last_sum()
    lower_b.second_sum()
    lower_a.third_sum()
    into.last_sum()
    down.third_back()
    into.third_back()
    lower_b.third_sum()
    down.second_back()
    lower_a.last_sum()
    lower_b.last_sum()
    into.second_back()
    lower_a.third_back()
    lower_b.third_back()
    down.first_back()
    lower_a.second_back()
    down.finish_own()
    lower_b.second_back()
    down.finish()
    lower_a.first_back()
    lower_a.finish_own()
    lower_a.finish()
    lower_b.first_back()
    into.first_back()
    lower_b.finish_own()
    lower_b.finish()
    into.finish_own()
    into.finish()
    g_ln2_gain, g_ln2_bias, g_b_down, g_b_in, g_ln1_gain, g_ln1_bias, g_b_out, g_b_qv = lower_a.sums
    return (
        enc.reshape(1, tokens, width),
        grad_input[None],
        outs["qkv"],
        g_b_qv,
        outs["out"],
        g_b_out,
        g_ln1_gain,
        g_ln1_bias,
        outs["into"],
        g_b_in,
        outs["down"],
        g_b_down,
        g_ln2_gain,
        g_ln2_bias,
        grad_w_pool,
        grad_b_pool,
    )


def solution(mesh):
    sharded = P("stream", "dp", None)
    return jax.shard_map(
        shards,
        mesh=mesh,
        in_specs=(sharded, sharded) + (P(),) * 15,
        out_specs=(sharded, sharded) + (P(),) * 14,
        check_vma=False,
    )
```

```python
import functools
import math

import jax
import jax.numpy as jnp
from jax import lax
from jax.experimental import pallas as pl
from jax.experimental.pallas import tpu as pltpu
from jax.sharding import PartitionSpec as P

HEAD_DIM = 64
SEQ = 64
GROUP = 16
CHUNK = 1536

epsilon = 1e-06
score_scale = 10.0
margin_shift = score_scale * 0.3
root_half = 0.7071067811865476
gauss_norm = 0.3989422804014327

low = jnp.bfloat16
wide = jnp.float32
ANY = pl.BlockSpec(memory_space=pl.ANY)
VMEM = pl.BlockSpec(memory_space=pltpu.VMEM)
SMEM = pl.BlockSpec(memory_space=pltpu.SMEM)
HBM = pl.BlockSpec(memory_space=pltpu.HBM)
MIB = 1 << 20


def struct(shape, dtype):
    return jax.ShapeDtypeStruct(shape, dtype)


def call(body, ins, outs, bits=None, scratch=(), aliases=None, after=(), limit=10, far=(), far_out=(), hand_out=(), cost=460):
    first = 0 if bits is None else 1
    ins = [pltpu.with_memory_space_constraint(a, pltpu.HBM) if i in far else a for i, a in enumerate(ins)]

    def wrapped(*refs):
        body(*refs[: first + len(ins)], *refs[first + len(ins) + len(after) :])

    return pl.pallas_call(
        wrapped,
        in_specs=[SMEM] * first + [HBM if i in far else VMEM for i in range(len(ins))] + [ANY] * len(after),
        out_specs=[HBM if i in hand_out else VMEM for i in range(len(outs))],
        out_shape=[(pltpu.HBM if i in far_out or i in hand_out else pltpu.VMEM)(o.shape, o.dtype) for i, o in enumerate(outs)],
        scratch_shapes=list(scratch),
        input_output_aliases={first + k: v for k, v in (aliases or {}).items()},
        cost_estimate=pl.CostEstimate(flops=int(cost * 1.5 * 10**7), bytes_accessed=0, transcendentals=0),
        compiler_params=pltpu.CompilerParams(vmem_limit_bytes=limit * MIB),
    )(*([] if bits is None else [bits]), *ins, *after)


def row_of(ref, start=0, size=None):
    return ref[pl.ds(start, ref.shape[0] if size is None else size)].reshape(1, -1)


def mat_mul(a, b):
    return jnp.dot(a, b, preferred_element_type=wide)


def trans_left(a, b):
    return lax.dot_general(a, b, (((0,), (0,)), ((), ())), preferred_element_type=wide)


def trans_right(a, b):
    return lax.dot_general(a, b, (((1,), (1,)), ((), ())), preferred_element_type=wide)


def normalize(h):
    center = h - jnp.mean(h, axis=-1, keepdims=True)
    inv = lax.rsqrt(jnp.mean(center * center, axis=-1, keepdims=True) + epsilon)
    return center * inv, inv


def norm_input_grad(grad, normed, inv):
    return inv * (
        grad
        - jnp.mean(grad, axis=-1, keepdims=True)
        - normed * jnp.mean(grad * normed, axis=-1, keepdims=True)
    )


def split_heads(pair, first):
    zero = jnp.zeros_like(pair)
    return jnp.concatenate([jnp.where(first, pair, zero), jnp.where(first, zero, pair)], axis=0)


def join_heads(rows, first):
    return jnp.where(first, rows[:SEQ], rows[SEQ:])


def heads_product(left, right, cols, first):
    zero = jnp.zeros_like(right[0][:, cols[0]])
    out = ([], [])
    for c in cols:
        both = jnp.concatenate([left[0][:, c], left[1][:, c]], axis=0)
        apart = jnp.concatenate(
            [jnp.concatenate([right[0][:, c], zero], axis=1), jnp.concatenate([zero, right[1][:, c]], axis=1)], axis=0
        )
        rows = trans_left(both, apart)
        for i in range(2):
            out[i].append(join_heads(rows[:, i * 128 : (i + 1) * 128], first))
    return [jnp.concatenate(o, axis=1) for o in out]


def attention_forward(bits, x, w_qkv, b_qv, w_out, b_out, gain, bias, later):
    tokens, width = x.shape
    rows = 4 * SEQ
    pairs = width // (2 * HEAD_DIM)
    scale = 1.0 / math.sqrt(HEAD_DIM)

    def body(_bits, *refs):
        n = len(later)
        far, far_later, outs, near_later, near, sems = (
            refs[:7], refs[7 : 7 + n], refs[7 + n : 13 + n], refs[13 + n : 13 + 2 * n], refs[13 + 2 * n : -1], refs[-1]
        )
        proj_ref, prob_ref, ctx_ref, hid_ref, low_ref, inv_ref = outs
        x_ref, wq_ref, bqv_ref, wo_ref, bo_ref, g_ref, b_ref = near
        pairs_of = zip(far + far_later, near + near_later)
        copies = [pltpu.make_async_copy(f, near_f, sems.at[i]) for i, (f, near_f) in enumerate(pairs_of)]
        for copy in copies[:3]:
            copy.start()
        for copy in copies[:3]:
            copy.wait()
        for copy in copies[3:]:
            copy.start()
        first = lax.broadcasted_iota(jnp.int32, (SEQ, 128), 1) < HEAD_DIM
        cols = [slice(p * 128, (p + 1) * 128) for p in range(pairs)]

        def project(block):
            for part in range(3):
                c = slice(part * width, (part + 1) * width)
                value = mat_mul(x_ref[block, :], wq_ref[:, c])
                if part != 1:
                    value = value + row_of(bqv_ref, (part // 2) * width, width)
                proj_ref[block, c] = value.astype(low)

        def attend(base):
            for two in range(2):
                at = [slice(base + (2 * two + i) * SEQ, base + (2 * two + i + 1) * SEQ) for i in range(2)]
                probs = []
                for r in at:
                    q = proj_ref[r, :width]
                    k = proj_ref[r, width : 2 * width]
                    scores = (
                        jnp.concatenate([trans_right(k[:, c], split_heads(q[:, c], first)) for c in cols], axis=1) * scale
                    )
                    e = jnp.exp(scores - jnp.max(scores, axis=0, keepdims=True))
                    probs.append((e * (1.0 / jnp.sum(e, axis=0, keepdims=True))).astype(low))
                    prob_ref[r, :] = probs[-1]
                values = [proj_ref[r, 2 * width :] for r in at]
                for r, context in zip(at, heads_product(probs, values, cols, first)):
                    ctx_ref[r, :] = context.astype(low)

        def finish(block):
            h = x_ref[block, :].astype(wide) + mat_mul(ctx_ref[block, :], wo_ref[...]) + row_of(bo_ref)
            normed, inv = normalize(h)
            hidden = normed * row_of(g_ref) + row_of(b_ref)
            hid_ref[block, :] = hidden
            low_ref[block, :] = hidden.astype(low)
            inv_ref[block, :] = inv

        blocks = [slice(start, start + rows) for start in range(0, tokens, rows)]
        project(blocks[0])
        for copy in copies[3:7]:
            copy.wait()
        for i, block in enumerate(blocks):
            if i + 1 < len(blocks):
                project(blocks[i + 1])
            attend(block.start)
            if i:
                finish(blocks[i - 1])
        finish(blocks[-1])

        for copy in copies[7:]:
            copy.wait()

    return call(
        body,
        [x, w_qkv, b_qv, w_out, b_out, gain, bias] + later,
        [
            struct((tokens, 3 * width), low),
            struct((tokens, width), low),
            struct((tokens, width), low),
            struct((tokens, width), wide),
            struct((tokens, width), low),
            struct((tokens, 1), wide),
        ]
        + [struct(v.shape, v.dtype) for v in later],
        scratch=[pltpu.VMEM(v.shape, v.dtype) for v in (x, w_qkv, b_qv, w_out, b_out, gain, bias)]
        + [pltpu.SemaphoreType.DMA((7 + len(later),))],
        bits=bits,
        far=range(7 + len(later)),
        limit=14,
    )


def ffn_forward_rows(hidden, wi_ref, bi_ref, wd_ref, bd_ref, store_act, store_gate_in):
    h_low = hidden.astype(low)
    total = hidden + row_of(bd_ref)
    for c in range(0, wi_ref.shape[1], CHUNK):
        u = mat_mul(h_low, wi_ref[:, c : c + CHUNK]) + row_of(bi_ref, c, CHUNK)
        phi = 0.5 + 0.5 * lax.erf(u * root_half)
        act = (u * phi).astype(low)
        store_act(c, act)
        store_gate_in(c, u.astype(low), phi.astype(low))
        total = total + mat_mul(act, wd_ref[c : c + CHUNK, :])
    return normalize(total)


def ffn_backward_rows(grad_block, normed, inv, gain, wd_ref, gate_in, store_gate, small_ref, bin_ref):
    grad_two = norm_input_grad(grad_block * gain, normed, inv)
    small_ref[0:1, :] += jnp.sum(grad_block * normed, axis=0, keepdims=True)
    small_ref[1:2, :] += jnp.sum(grad_block, axis=0, keepdims=True)
    small_ref[2:3, :] += jnp.sum(grad_two, axis=0, keepdims=True)
    grad_low = grad_two.astype(low)
    for c in range(0, wd_ref.shape[0], CHUNK):
        u, phi = gate_in(c)
        slope = phi + u * jnp.exp(u * u * low(-0.5)) * low(gauss_norm)
        gate = trans_right(grad_low, wd_ref[c : c + CHUNK, :]) * slope.astype(wide)
        bin_ref[:, c : c + CHUNK] += jnp.sum(gate, axis=0, keepdims=True)
        store_gate(c, gate.astype(low))
    return grad_low


def ffn_group(index, hidden, cot, upper, state, after=()):
    w_in, b_in, w_down, b_down, gain, bias = upper
    sents, _, width = hidden.shape
    ffn = w_in.shape[1]
    rows = sents * GROUP
    at = slice(index * GROUP, (index + 1) * GROUP)
    first = index == 0
    second = index == 1

    def stores(act_ref, u_ref, phi_ref):
        def store_act(c, v):
            act_ref[:, at, c : c + CHUNK] = v.reshape(sents, GROUP, CHUNK)

        def store_gate_in(c, u, phi):
            u_ref[:, c : c + CHUNK] = u
            phi_ref[:, c : c + CHUNK] = phi

        return store_act, store_gate_in

    def forward(h_ref, wi_ref, bi_ref, wd_ref, bd_ref, act_ref, u_ref, phi_ref):
        return ffn_forward_rows(
            h_ref[:, at, :].reshape(rows, width), wi_ref, bi_ref, wd_ref, bd_ref, *stores(act_ref, u_ref, phi_ref)
        )

    def body_first(h_ref, wi_ref, bi_ref, wd_ref, bd_ref, g_ref, b_ref, enc_hbm, act_ref, u_ref, phi_ref, n_ref, inv_ref, first_ref, enc_ref, sem):
        normed, inv = forward(h_ref, wi_ref, bi_ref, wd_ref, bd_ref, act_ref, u_ref, phi_ref)
        n_ref[...] = normed
        inv_ref[...] = inv
        block = (normed * row_of(g_ref) + row_of(b_ref)).reshape(sents, GROUP, width)
        enc_ref[...] = block.astype(low)
        copy = pltpu.make_async_copy(enc_ref, enc_hbm.at[:, pl.ds(index * GROUP, GROUP), :], sem)
        copy.start()
        first_ref[...] = block[:, 0, :].astype(low)
        copy.wait()

    enc_shape = struct((sents, SEQ, width), low)
    enc_scratch = [pltpu.VMEM((sents, GROUP, width), low), pltpu.SemaphoreType.DMA]
    act_shape = struct((sents, SEQ, ffn), low)
    if first:
        return call(
            body_first,
            [hidden, w_in, b_in, w_down, b_down, gain, bias],
            [
                enc_shape,
                act_shape,
                struct((rows, ffn), low),
                struct((rows, ffn), low),
                struct((rows, width), wide),
                struct((rows, 1), wide),
                struct((sents, width), low),
            ],
            scratch=enc_scratch,
            hand_out=[0],
        )

    def body(h_ref, cot_ref, wi_ref, bi_ref, wd_ref, bd_ref, g_ref, b_ref, *refs):
        refs = refs[2 if second else 4 :]
        if not second:
            sin_ref, bin_in_ref = refs[:2]
            refs = refs[2:]
        enc_hbm, act_ref, gate_ref, two_ref, small_ref, bin_ref, u_ref, phi_ref, enc_ref, sem = refs
        small_ref[...] = jnp.zeros_like(small_ref) if second else sin_ref[...]
        bin_ref[...] = jnp.zeros_like(bin_ref) if second else bin_in_ref[...]

        def store_gate(c, v):
            gate_ref[:, at, c : c + CHUNK] = v.reshape(sents, GROUP, CHUNK)

        normed, inv = forward(h_ref, wi_ref, bi_ref, wd_ref, bd_ref, act_ref, u_ref, phi_ref)
        gain_row = row_of(g_ref)
        enc_ref[...] = (normed * gain_row + row_of(b_ref)).astype(low).reshape(sents, GROUP, width)
        copy = pltpu.make_async_copy(enc_ref, enc_hbm.at[:, pl.ds(index * GROUP, GROUP), :], sem)
        copy.start()
        grad_block = cot_ref[:, at, :].reshape(rows, width).astype(wide)
        got = ffn_backward_rows(
            grad_block, normed, inv, gain_row, wd_ref, lambda c: (u_ref[:, c : c + CHUNK], phi_ref[:, c : c + CHUNK]),
            store_gate, small_ref, bin_ref,
        )
        two_ref[:, at, :] = got.reshape(sents, GROUP, width)
        copy.wait()

    aliases = {8: 0, 9: 1}
    if not second:
        aliases.update({10: 2, 11: 3})
    return call(
        body,
        [hidden, cot, w_in, b_in, w_down, b_down, gain, bias] + list(state),
        [enc_shape, act_shape, act_shape, enc_shape, struct((8, width), wide), struct((1, ffn), wide)],
        scratch=[pltpu.VMEM((rows, ffn), low)] * 2 + enc_scratch,
        aliases=aliases,
        after=after,
        far=[8],
        hand_out=[0],
    )


def ffn_first_back(cot, grad_first, normed, inv, gate_in, phi, gain, w_down, gate, two, small, bin_sum):
    sents, _, width = cot.shape
    ffn = w_down.shape[0]
    rows = sents * GROUP
    at = slice(0, GROUP)

    def body(cot_ref, first_ref, n_ref, inv_ref, u_ref, phi_ref, g_ref, wd_ref, sin_ref, bin_in_ref, _g, _t, gate_ref, two_ref, small_ref, bin_ref):
        small_ref[...] = sin_ref[...]
        bin_ref[...] = bin_in_ref[...]
        position = lax.broadcasted_iota(jnp.int32, (sents, GROUP, width), 1)
        at_first = jnp.broadcast_to(first_ref[...][:, None, :], (sents, GROUP, width))
        grad_block = cot_ref[:, at, :].astype(wide) + jnp.where(position == 0, at_first, 0.0)

        def store_gate(c, v):
            gate_ref[:, at, c : c + CHUNK] = v.reshape(sents, GROUP, CHUNK)

        got = ffn_backward_rows(
            grad_block.reshape(rows, width), n_ref[...], inv_ref[...], row_of(g_ref), wd_ref,
            lambda c: (u_ref[:, c : c + CHUNK], phi_ref[:, c : c + CHUNK]), store_gate, small_ref, bin_ref,
        )
        two_ref[:, at, :] = got.reshape(sents, GROUP, width)

    return call(
        body,
        [cot, grad_first, normed, inv, gate_in, phi, gain, w_down, small, bin_sum, gate, two],
        [struct((sents, SEQ, ffn), low), struct((sents, SEQ, width), low), struct((8, width), wide), struct((1, ffn), wide)],
        aliases={10: 0, 11: 1},
    )


def lower_backward(part, parts, two, gate, hidden, inv, proj, probs, w_in, w_out, gain, bias, before=None, after=()):
    tokens, width = hidden.shape
    ffn = w_in.shape[1]
    rows = 4 * SEQ
    steps = tokens // rows // parts
    pairs = width // (2 * HEAD_DIM)
    scale = 1.0 / math.sqrt(HEAD_DIM)
    fresh = before is None

    def body(two_ref, gate_ref, hid_ref, inv_ref, proj_ref, prob_ref, wi_ref, wo_ref, g_ref, b_ref, *refs):
        if not fresh:
            sin_ref, bin_ref = refs[2:4]
            refs = refs[4:]
        one_ref, gp_ref, small_ref, bqv_ref, ctx_ref = refs
        small_ref[...] = jnp.zeros_like(small_ref) if fresh else sin_ref[...]
        bqv_ref[...] = jnp.zeros_like(bqv_ref) if fresh else bin_ref[...]
        first = lax.broadcasted_iota(jnp.int32, (SEQ, 128), 1) < HEAD_DIM
        cols = [slice(p * 128, (p + 1) * 128) for p in range(pairs)]

        gain_row = row_of(g_ref)

        def first_norm(block, at):
            grad_hidden = two_ref[block, :].astype(wide) + trans_right(gate_ref[block, :], wi_ref[...])
            normed = (hid_ref[block, :] - row_of(b_ref)) * (1.0 / gain_row)
            small_ref[0:1, :] += jnp.sum(grad_hidden * normed, axis=0, keepdims=True)
            small_ref[1:2, :] += jnp.sum(grad_hidden, axis=0, keepdims=True)
            grad_one = norm_input_grad(grad_hidden * gain_row, normed, inv_ref[block, :])
            small_ref[2:3, :] += jnp.sum(grad_one, axis=0, keepdims=True)
            one_ref[block, :] = grad_one.astype(low)
            ctx_ref[at : at + rows, :] = trans_right(grad_one.astype(low), wo_ref[...]).astype(low)

        def attention(base, from_ctx):
            sum_q = jnp.zeros((1, width), wide)
            sum_v = jnp.zeros((1, width), wide)
            for two in range(2):
                at = [slice(base + (2 * two + i) * SEQ, base + (2 * two + i + 1) * SEQ) for i in range(2)]
                grads = []
                for i, r in enumerate(at):
                    q_all = proj_ref[r, :width]
                    v = proj_ref[r, 2 * width :]
                    start = from_ctx + (2 * two + i) * SEQ
                    d_all = ctx_ref[start : start + SEQ, :]
                    p_low = prob_ref[r, :]
                    q = [split_heads(q_all[:, c], first) for c in cols]
                    d = [split_heads(d_all[:, c], first) for c in cols]
                    p = p_low.astype(wide)
                    grad_p = jnp.concatenate([trans_right(v[:, c], dd) for c, dd in zip(cols, d)], axis=1)
                    grad_v = jnp.concatenate([mat_mul(p_low[:, c], dd) for c, dd in zip(cols, d)], axis=1)
                    gp = grad_p * p
                    grad_s = (gp - p * jnp.sum(gp, axis=0, keepdims=True)).astype(low)
                    grad_k = jnp.concatenate([mat_mul(grad_s[:, c], qq) for c, qq in zip(cols, q)], axis=1) * scale
                    sum_v += jnp.sum(grad_v, axis=0, keepdims=True)
                    gp_ref[r, width : 2 * width] = grad_k.astype(low)
                    gp_ref[r, 2 * width :] = grad_v.astype(low)
                    grads.append(grad_s)
                keys = [proj_ref[r, width : 2 * width] for r in at]
                for r, product in zip(at, heads_product(grads, keys, cols, first)):
                    grad_q = product * scale
                    sum_q += jnp.sum(grad_q, axis=0, keepdims=True)
                    gp_ref[r, :width] = grad_q.astype(low)
            bqv_ref[0:1, :] += sum_q
            bqv_ref[1:2, :] += sum_v

        base = part * steps * rows
        first_norm(slice(base, base + rows), 0)
        for i in range(steps):
            if i + 1 < steps:
                start = base + (i + 1) * rows
                first_norm(slice(start, start + rows), ((i + 1) % 2) * rows)
            attention(base + i * rows, (i % 2) * rows)

    return call(
        body,
        [two, gate, hidden, inv, proj, probs, w_in, w_out, gain, bias] + ([] if fresh else list(before)),
        [struct((tokens, width), low), struct((tokens, 3 * width), low), struct((8, width), wide), struct((8, width), wide)],
        scratch=[pltpu.VMEM((2 * rows, width), low)],
        aliases=None if fresh else {10: 0, 11: 1},
        after=after,
    )


def input_gradient(grad_proj, w_qkv, grad_one, after=()):
    tokens, width = grad_one.shape
    rows = tokens // 2

    def body(gp_ref, w_ref, one_ref, out_ref, token):
        token[...] = jnp.zeros_like(token)

        for start in range(0, tokens, rows):
            block = slice(start, start + rows)
            out_ref[block, :] = (one_ref[block, :].astype(wide) + trans_right(gp_ref[block, :], w_ref[...])).astype(low)

    return call(
        body, [grad_proj, w_qkv, grad_one], [struct((tokens, width), low), struct((8, 128), wide)], after=after, far_out=[0]
    )


def pooler_gradients(flat, id_row, w_pool, b_pool):
    total = flat.shape[0] // 2
    pooled = jnp.tanh(mat_mul(flat, w_pool) + b_pool)
    inv_len = lax.rsqrt(jnp.sum(pooled * pooled, axis=-1, keepdims=True) + epsilon)
    unit = pooled * inv_len
    embed = unit.astype(low)
    zero, one = embed[:total], embed[total:]
    square = (total, total)
    eye = (lax.broadcasted_iota(jnp.int32, square, 0) == lax.broadcasted_iota(jnp.int32, square, 1)).astype(wide)
    logits = score_scale * trans_right(zero, one) - margin_shift * eye
    id_column = jnp.sum(jnp.where(eye > 0, id_row, 0), axis=1, keepdims=True)
    masked = jnp.where(id_column == id_row, logits, -jnp.inf)

    def soft(axis):
        e = jnp.exp(masked - jnp.max(masked, axis=axis, keepdims=True))
        return (score_scale * (e / jnp.sum(e, axis=axis, keepdims=True) - eye)).astype(low)

    by_row, by_col = soft(1), soft(0)
    grad_embed = jnp.concatenate(
        [mat_mul(by_row, one) + mat_mul(by_col, one), trans_left(by_row, zero) + trans_left(by_col, zero)], axis=0
    )
    grad_pre = (
        inv_len * (grad_embed - unit * jnp.sum(unit * grad_embed, axis=-1, keepdims=True)) * (1.0 - pooled * pooled)
    )
    pre_low = grad_pre.astype(low)
    return pre_low, trans_left(flat, pre_low), jnp.sum(grad_pre, axis=0, keepdims=True)


def contrastive(own, got, bits, sents, ids, w_pool, b_pool, after):
    total, width = own.shape
    if total > 512:
        start = bits[CORE] * total + bits[PLACE] * sents
        flat = jnp.where(bits[CORE] == 0, jnp.concatenate([own, got]), jnp.concatenate([got, own]))
        pre_low, grad_w, grad_b = pooler_gradients(flat, ids.reshape(1, -1), w_pool, b_pool.reshape(1, -1))
        return trans_right(lax.dynamic_slice_in_dim(pre_low, start, sents), w_pool), grad_w, grad_b.reshape(-1)

    def body(b, own_ref, got_ref, ids_ref, w_ref, b_ref, first_ref, gw_ref, gb_ref, flat_ref, pre_ref):
        flat_ref[pl.ds(pl.multiple_of(b[CORE] * total, total), total), :] = own_ref[...]
        flat_ref[pl.ds(pl.multiple_of((1 - b[CORE]) * total, total), total), :] = got_ref[...]
        pre_low, grad_w, grad_b = pooler_gradients(flat_ref[...], row_of(ids_ref), w_ref[...], row_of(b_ref))
        pre_ref[...] = pre_low
        gw_ref[...] = grad_w
        gb_ref[...] = grad_b.reshape(-1)
        first_ref[...] = trans_right(pre_ref[pl.ds(pl.multiple_of(b[CORE] * total + b[PLACE] * sents, sents), sents), :], w_ref[...])

    return call(
        body,
        [own, got, ids, w_pool, b_pool],
        [struct((sents, width), wide), struct((width, width), wide), struct((width,), wide)],
        bits=bits,
        scratch=[pltpu.VMEM((2 * total, width), low)] * 2,
        after=after,
        far_out=[1, 2],
    )


def put_in_order(blocks, bits, low_bit, after):
    rows, width = blocks[0].shape

    def body(b, *refs):
        me = (b[PLACE] >> low_bit) & (len(blocks) - 1)
        for i, ref in enumerate(refs[:-1]):
            at = pl.multiple_of((me ^ i) * rows, rows)
            refs[-1][pl.ds(at, rows), :] = ref[...]

    return call(
        body, blocks, [struct((rows * len(blocks), width), low)], bits=bits, after=after, limit=8, cost=920
    )[0]


CORE, FIRST, SECOND, THIRD, PLACE = range(5)
SMALL = 16
MASKS = {FIRST: (1, 2), SECOND: (2, 1), THIRD: (4, 4)}


def exchange(a, masks):
    size = lax.axis_size("dp")
    pairs = [(core * size + i, core * size + (i ^ masks[core])) for core in range(2) for i in range(size)]
    return lax.ppermute(a, ("stream", "dp"), pairs)


def cross(a):
    return lax.ppermute(a, "stream", [(0, 1), (1, 0)])


class Sources:
    def __init__(self, products, small=()):
        self.products = products
        self.small = list(small)
        self.m = products[0][0].shape[1]
        self.n = sum(hi - lo for _, _, lo, hi in products)
        self.arrays = [a for left, right, _, _ in products for a in (left, right)]

    def pieces(self, refs):
        at = 0
        for i, (_, _, lo, hi) in enumerate(self.products):
            yield refs[2 * i], refs[2 * i + 1], lo, at, hi - lo
            at += hi - lo


def gradient_to_send(src, bits, after=()):
    m, n = src.m, src.n
    half = m // 2
    count = len(src.arrays)
    small = src.small

    def body(b, *refs):
        out = refs[count + len(small)]
        rows = pl.ds(pl.multiple_of((1 - b[CORE]) * half, 128), half)
        for a, g, lo, at, size in src.pieces(refs):
            out[:half, at : at + size] = trans_left(a[:, rows], g[:, lo : lo + size]).astype(low)
        if small:
            up, bin_sum, down, bqv = refs[count : count + 4]
            kept = refs[-1]
            width = up.shape[1]
            parts = [up[:3]] + [bin_sum[:, c : c + width] for c in range(0, bin_sum.shape[1], width)] + [down[:3], bqv[:2]]
            parts.append(jnp.zeros((SMALL - sum(p.shape[0] for p in parts), width), wide))
            kept[...] = jnp.concatenate(parts, axis=0).astype(low)
            out[half:, :] = jnp.zeros((SMALL, n), low)
            out[half:, :width] = kept[...]

    shapes = [struct((half + (SMALL if small else 0), n), low)]
    if small:
        shapes.append(struct((SMALL, small[0].shape[1]), low))
    return call(body, src.arrays + small, shapes, bits=bits, after=after)


def gradient_sum(src, bits, got, kept, bit, after=()):
    m, n = src.m, src.n
    half, quarter = m // 2, m // 4
    count = len(src.arrays)
    extra = SMALL if src.small else 0

    def body(b, *refs):
        got_ref, send, keep = refs[-3:]
        if extra:
            mine = refs[count]
            total = (mine[...].astype(wide) + got_ref[half:, : mine.shape[1]].astype(wide)).astype(low)
            for ref in (send, keep):
                ref[quarter:, :] = jnp.zeros((SMALL, n), low)
                ref[quarter:, : mine.shape[1]] = total
        rows = pl.ds(pl.multiple_of(b[CORE] * half, 128), half)
        for a, g, lo, at, size in src.pieces(refs):
            c = slice(at, at + size)
            value = (trans_left(a[:, rows], g[:, lo : lo + size]) + got_ref[:half, c].astype(wide)).astype(low)

            def put(kept_half, c=c, value=value):
                keep[:quarter, c] = value[kept_half * quarter : (kept_half + 1) * quarter]
                send[:quarter, c] = value[(1 - kept_half) * quarter : (2 - kept_half) * quarter]

            pl.when(b[bit] == 0)(functools.partial(put, 0))
            pl.when(b[bit] != 0)(functools.partial(put, 1))

    return call(
        body,
        src.arrays + ([kept] if extra else []) + [got],
        [struct((quarter + extra, n), low)] * 2,
        bits=bits,
        after=after,
    )


def whole_call(body, arrays, shapes, bits, after=(), **kwargs):
    return call(body, arrays, shapes, bits=bits, after=after, limit=8, cost=920, **kwargs)


def halve(mine, got, bit, extra, bits, after=()):
    rows, cols = (mine.shape[0] - extra) // 2, mine.shape[1]

    def body(b, m, g, send, keep):
        for which, out in ((1 - b[bit], send), (b[bit], keep)):
            at = pl.ds(pl.multiple_of(which * rows, rows), rows)
            out[:rows, :] = (m[at, :].astype(wide) + g[at, :].astype(wide)).astype(low)
        if extra:
            total = (m[2 * rows :, :].astype(wide) + g[2 * rows :, :].astype(wide)).astype(low)
            send[rows:, :] = total
            keep[rows:, :] = total

    return whole_call(body, [mine, got], [struct((rows + extra, cols), low)] * 2, bits, after)


def add_up(mine, got, bits, after=()):
    def body(b, m, g, out):
        out[...] = (m[...].astype(wide) + g[...].astype(wide)).astype(low)

    return whole_call(body, [mine, got], [struct(mine.shape, low)], bits, after)


def add_last(mine, got, lengths, width, bits, after=()):
    rows = mine.shape[0] - SMALL

    def body(b, m, g, *refs):
        *vectors, out = refs
        out[...] = (m[:rows, :].astype(wide) + g[:rows, :].astype(wide)).astype(low)
        total = (m[rows:, :width].astype(wide) + g[rows:, :width].astype(wide)).astype(low).astype(wide)
        at = 0
        for vector in vectors:
            for c in range(0, vector.shape[0], width):
                vector[pl.ds(c, width)] = total[at : at + 1].reshape(-1)
                at += 1

    shapes = [struct((v,), wide) for v in lengths] + [struct((rows, mine.shape[1]), low)]
    return whole_call(body, [mine, got], shapes, bits, after, far_out=range(len(lengths)))


def join(mine, got, bit, bits, after=()):
    rows, cols = mine.shape

    def body(b, m, g, out):
        out[pl.ds(pl.multiple_of(b[bit] * rows, rows), rows), :] = m[...]
        out[pl.ds(pl.multiple_of((1 - b[bit]) * rows, rows), rows), :] = g[...]

    return whole_call(body, [mine, got], [struct((2 * rows, cols), low)], bits, after)


def widen(source, which, targets, before, bits, after=()):
    half = source.shape[0]
    parts = 4
    tile = half // parts
    old = [(i, a) for i, a in enumerate(before) if a is not None]

    def body(b, src, *refs):
        refs = refs[len(old) :]
        n = len(targets)
        outs, token, bufs, sems = refs[:n], refs[n], refs[n + 1 : -1], refs[-1]
        token[...] = jnp.zeros_like(token)
        start = (1 - b[CORE] if which else b[CORE]) * half
        copies = []
        for t in range(parts):
            at = 0
            for out, buf, (_, first, size) in zip(outs, bufs, targets):
                buf[t] = src[t * tile : (t + 1) * tile, at : at + size].astype(wide)
                rows = pl.ds(pl.multiple_of(start + t * tile, tile), tile)
                copies.append(pltpu.make_async_copy(buf.at[t], out.at[rows, pl.ds(first, size)], sems.at[len(copies)]))
                copies[-1].start()
                at += size
        for copy in copies:
            copy.wait()

    return call(
        body,
        [source] + [a for _, a in old],
        [struct(shape, wide) for shape, _, _ in targets] + [struct((8, 128), wide)],
        bits=bits,
        scratch=[pltpu.VMEM((parts, tile, size), wide) for _, _, size in targets]
        + [pltpu.SemaphoreType.DMA((parts * len(targets),))],
        aliases={1 + k: i for k, (i, _) in enumerate(old)},
        after=after,
        far=range(1, 1 + len(old)),
        hand_out=range(len(targets)),
        limit=12,
        cost=920,
    )


class Reduction:
    def __init__(self, src, order, targets, outs, bits, clock, tail, lengths=()):
        self.src, self.order, self.targets, self.outs = src, order, targets, outs
        self.bits, self.clock, self.tail, self.lengths = bits, clock, tail, lengths
        self.extra = SMALL if src.small else 0

    def step(self, fn, *args):
        out = fn(*args, self.bits, after=self.clock.now())
        self.clock.set(out[-1])
        return out

    def core_send(self):
        send, *self.kept = self.step(gradient_to_send, self.src)
        self.got = cross(send)

    def core_sum(self):
        out = gradient_sum(
            self.src, self.bits, self.got, self.kept[0] if self.kept else None, self.order[0], after=self.clock.now()
        )
        self.clock.set(out[-1])
        self.v = out[1]
        self.got = exchange(out[0], MASKS[self.order[0]])

    def halve(self, i):
        send, self.v = self.step(halve, self.v, self.got, self.order[i], self.extra)
        self.got = exchange(send, MASKS[self.order[i]])

    def first_sum(self):
        self.halve(1)

    def second_sum(self):
        self.halve(2)

    def third_sum(self):
        for mask in self.tail:
            (self.v,) = self.step(add_up, self.v, self.got)
            self.got = exchange(self.v, (mask, mask))

    def last_sum(self):
        if self.extra:
            *self.sums, self.v = self.step(add_last, self.v, self.got, self.lengths, self.src.small[0].shape[1])
        else:
            (self.v,) = self.step(add_up, self.v, self.got)
        self.got = exchange(self.v, MASKS[self.order[2]])

    def join(self, i):
        (self.v,) = self.step(join, self.v, self.got, self.order[i])
        self.got = exchange(self.v, MASKS[self.order[i - 1]]) if i else cross(self.v)

    def third_back(self):
        self.join(2)

    def second_back(self):
        self.join(1)

    def first_back(self):
        self.join(0)

    def write(self, which, source):
        before = [self.outs.get(name) for name, *_ in self.targets]
        *arrays, _ = self.step(widen, source, which, [t[1:] for t in self.targets], before)
        for (name, *_), array in zip(self.targets, arrays):
            self.outs[name] = array

    def finish_own(self):
        self.write(0, self.v)

    def finish(self):
        self.write(1, self.got)


class Clock:
    def __init__(self, start):
        self.last = start

    def now(self):
        return (self.last,)

    def set(self, value):
        self.last = value


def shards(
    embedded, seq_cotangent, pair_ids, w_qkv, b_qv, w_out, b_out, ln1_gain, ln1_bias, w_in, b_in, w_down, b_down,
    ln2_gain, ln2_bias, w_pool, b_pool,
):
    x = embedded[0]
    tokens, width = x.shape
    sents = tokens // SEQ
    ffn = w_in.shape[1]
    dp = lax.axis_size("dp")
    stream, place_dp = lax.axis_index("stream"), lax.axis_index("dp")
    first, second = (place_dp >> stream) & 1, (place_dp >> (1 - stream)) & 1
    bits = jnp.stack([stream, first, second, (place_dp >> 2) & 1, place_dp]).astype(jnp.int32)
    later = [
        w_in, w_down, seq_cotangent[0], w_pool, b_in, b_down, ln2_gain, ln2_bias, b_pool, pair_ids
    ]
    proj, probs, context, hidden, hidden_low, inv_one, *later = attention_forward(
        bits, x, w_qkv, b_qv, w_out, b_out, ln1_gain, ln1_bias, later
    )
    w_in, w_down, cotangent, w_pool, b_in, b_down, ln2_gain, ln2_bias, b_pool, ids = later
    hid3 = hidden.reshape(sents, SEQ, width)
    cot3 = cotangent.reshape(sents, SEQ, width)
    upper = (w_in, b_in, w_down, b_down, ln2_gain, ln2_bias)
    enc, act, gate_in, phi, normed_two, inv_two, first_low = ffn_group(0, hid3, cot3, upper, ())
    masks = [1 << i for i in range(dp.bit_length() - 1)]
    state = [enc, act]
    gathered = first_low
    group = 1
    order = [inv_two]
    for low_bit in range(0, len(masks), 2):
        span = 4 if low_bit + 1 < len(masks) else 2
        blocks = [gathered] + [exchange(gathered, (i << low_bit,) * 2) for i in range(1, span)]
        if group < SEQ // GROUP:
            state = ffn_group(group, hid3, cot3, upper, state, after=order)
            group += 1
            order = [state[-1]]
        gathered = put_in_order(blocks, bits, low_bit, order)
        order = [gathered]
    other = cross(gathered)
    while group < SEQ // GROUP:
        state = ffn_group(group, hid3, cot3, upper, state, after=order)
        group += 1
        order = [state[-1]]
    enc, act, gate, two, small_up, bin_sum = state
    grad_first, grad_w_pool, grad_b_pool = contrastive(
        gathered, other, bits, sents, ids, w_pool, b_pool, order
    )
    gate, two, small_up, bin_sum = ffn_first_back(
        cot3, grad_first, normed_two, inv_two, gate_in, phi, ln2_gain, w_down, gate, two, small_up, bin_sum
    )
    clock = Clock(small_up)
    act, gate, two = (v.reshape(tokens, -1) for v in (act, gate, two))
    tail = masks[3:]
    outs = {}
    shape_of = {"down": (ffn, width), "into": (width, ffn), "qkv": (width, 3 * width), "out": (width, width)}

    def target(name, first, size):
        return name, shape_of[name], first, size

    plain, third_first = (FIRST, SECOND, THIRD), (THIRD, FIRST, SECOND)
    rest = (outs, bits, clock, tail)
    down = Reduction(Sources([(act, two, 0, width)]), plain, [target("down", 0, width)], *rest)
    into = Reduction(Sources([(hidden_low, gate, 0, ffn)]), third_first, [target("into", 0, ffn)], *rest)
    lower = (two, gate, hidden, inv_one, proj, probs, w_in, w_out, ln1_gain, ln1_bias)

    def lower_reductions(grad_one, grad_proj, small_low, bqv):
        edge, end = 2 * width, 3 * width
        lengths = (width, width, width, ffn, width, width, width, 2 * width)
        part_a = Sources([(x, grad_proj, 0, edge)], [small_up, bin_sum, small_low, bqv])
        part_b = Sources([(x, grad_proj, edge, end), (context, grad_one, 0, width)])
        return (
            Reduction(part_a, plain, [target("qkv", 0, edge)], *rest, lengths),
            Reduction(part_b, plain, [target("qkv", edge, end - edge), target("out", 0, width)], *rest),
        )

    into.core_send()
    down.core_send()
    into.core_sum()
    down.core_sum()
    state = lower_backward(0, 2, *lower, after=clock.now())
    clock.set(state[-1])
    state = lower_backward(1, 2, *lower, before=state, after=clock.now())
    grad_one, grad_proj, small_low, bqv = state
    clock.set(bqv)
    lower_a, lower_b = lower_reductions(grad_one, grad_proj, small_low, bqv)
    lower_a.core_send()
    down.first_sum()
    lower_a.core_sum()
    down.second_sum()
    into.first_sum()
    lower_b.core_send()
    down.third_sum()
    lower_a.first_sum()
    into.second_sum()
    lower_b.core_sum()
    lower_a.second_sum()
    into.third_sum()
    grad_input, token = input_gradient(grad_proj, w_qkv, grad_one, after=clock.now())
    clock.set(token)
    lower_b.first_sum()
    down.last_sum()
    lower_b.second_sum()
    lower_a.third_sum()
    into.last_sum()
    down.third_back()
    into.third_back()
    lower_b.third_sum()
    down.second_back()
    lower_a.last_sum()
    lower_b.last_sum()
    into.second_back()
    lower_a.third_back()
    lower_b.third_back()
    down.first_back()
    lower_a.second_back()
    down.finish_own()
    lower_b.second_back()
    down.finish()
    lower_a.first_back()
    lower_a.finish_own()
    lower_a.finish()
    lower_b.first_back()
    into.first_back()
    lower_b.finish_own()
    lower_b.finish()
    into.finish_own()
    into.finish()
    g_ln2_gain, g_ln2_bias, g_b_down, g_b_in, g_ln1_gain, g_ln1_bias, g_b_out, g_b_qv = lower_a.sums
    return (
        enc.reshape(1, tokens, width),
        grad_input[None],
        outs["qkv"],
        g_b_qv,
        outs["out"],
        g_b_out,
        g_ln1_gain,
        g_ln1_bias,
        outs["into"],
        g_b_in,
        outs["down"],
        g_b_down,
        g_ln2_gain,
        g_ln2_bias,
        grad_w_pool,
        grad_b_pool,
    )


def solution(mesh):
    sharded = P("stream", "dp", None)
    return jax.shard_map(
        shards,
        mesh=mesh,
        in_specs=(sharded, sharded) + (P(),) * 15,
        out_specs=(sharded, sharded) + (P(),) * 14,
        check_vma=False,
    )
```

```python
import functools
import math

import jax
import jax.numpy as jnp
from jax import lax
from jax.experimental import pallas as pl
from jax.experimental.pallas import tpu as pltpu
from jax.sharding import PartitionSpec as P

HEAD_DIM = 64
SEQ = 64
GROUP = 16
CHUNK = 1536

epsilon = 1e-06
score_scale = 10.0
margin_shift = score_scale * 0.3
root_half = 0.7071067811865476
gauss_norm = 0.3989422804014327

low = jnp.bfloat16
wide = jnp.float32
ANY = pl.BlockSpec(memory_space=pl.ANY)
VMEM = pl.BlockSpec(memory_space=pltpu.VMEM)
SMEM = pl.BlockSpec(memory_space=pltpu.SMEM)
HBM = pl.BlockSpec(memory_space=pltpu.HBM)
MIB = 1 << 20


def struct(shape, dtype):
    return jax.ShapeDtypeStruct(shape, dtype)


def call(body, ins, outs, bits=None, scratch=(), aliases=None, after=(), limit=10, far=(), far_out=(), hand_out=(), cost=460):
    first = 0 if bits is None else 1
    ins = [pltpu.with_memory_space_constraint(a, pltpu.HBM) if i in far else a for i, a in enumerate(ins)]

    def wrapped(*refs):
        body(*refs[: first + len(ins)], *refs[first + len(ins) + len(after) :])

    return pl.pallas_call(
        wrapped,
        in_specs=[SMEM] * first + [HBM if i in far else VMEM for i in range(len(ins))] + [ANY] * len(after),
        out_specs=[HBM if i in hand_out else VMEM for i in range(len(outs))],
        out_shape=[(pltpu.HBM if i in far_out or i in hand_out else pltpu.VMEM)(o.shape, o.dtype) for i, o in enumerate(outs)],
        scratch_shapes=list(scratch),
        input_output_aliases={first + k: v for k, v in (aliases or {}).items()},
        cost_estimate=pl.CostEstimate(flops=int(cost * 1.5 * 10**7), bytes_accessed=0, transcendentals=0),
        compiler_params=pltpu.CompilerParams(vmem_limit_bytes=limit * MIB),
    )(*([] if bits is None else [bits]), *ins, *after)


def row_of(ref, start=0, size=None):
    return ref[pl.ds(start, ref.shape[0] if size is None else size)].reshape(1, -1)


def mat_mul(a, b):
    return jnp.dot(a, b, preferred_element_type=wide)


def trans_left(a, b):
    return lax.dot_general(a, b, (((0,), (0,)), ((), ())), preferred_element_type=wide)


def trans_right(a, b):
    return lax.dot_general(a, b, (((1,), (1,)), ((), ())), preferred_element_type=wide)


def normalize(h):
    center = h - jnp.mean(h, axis=-1, keepdims=True)
    inv = lax.rsqrt(jnp.mean(center * center, axis=-1, keepdims=True) + epsilon)
    return center * inv, inv


def norm_input_grad(grad, normed, inv):
    return inv * (
        grad
        - jnp.mean(grad, axis=-1, keepdims=True)
        - normed * jnp.mean(grad * normed, axis=-1, keepdims=True)
    )


def split_heads(pair, first):
    zero = jnp.zeros_like(pair)
    return jnp.concatenate([jnp.where(first, pair, zero), jnp.where(first, zero, pair)], axis=0)


def join_heads(rows, first):
    return jnp.where(first, rows[:SEQ], rows[SEQ:])


def heads_product(left, right, cols, first):
    zero = jnp.zeros_like(right[0][:, cols[0]])
    out = ([], [])
    for c in cols:
        both = jnp.concatenate([left[0][:, c], left[1][:, c]], axis=0)
        apart = jnp.concatenate(
            [jnp.concatenate([right[0][:, c], zero], axis=1), jnp.concatenate([zero, right[1][:, c]], axis=1)], axis=0
        )
        rows = trans_left(both, apart)
        for i in range(2):
            out[i].append(join_heads(rows[:, i * 128 : (i + 1) * 128], first))
    return [jnp.concatenate(o, axis=1) for o in out]


def attention_forward(bits, x, w_qkv, b_qv, w_out, b_out, gain, bias, later):
    tokens, width = x.shape
    rows = 4 * SEQ
    pairs = width // (2 * HEAD_DIM)
    scale = 1.0 / math.sqrt(HEAD_DIM)

    def body(_bits, *refs):
        n = len(later)
        far, far_later, outs, near_later, near, sems = (
            refs[:7], refs[7 : 7 + n], refs[7 + n : 13 + n], refs[13 + n : 13 + 2 * n], refs[13 + 2 * n : -1], refs[-1]
        )
        proj_ref, prob_ref, ctx_ref, hid_ref, low_ref, inv_ref = outs
        x_ref, wq_ref, bqv_ref, wo_ref, bo_ref, g_ref, b_ref = near
        pairs_of = zip(far + far_later, near + near_later)
        copies = [pltpu.make_async_copy(f, near_f, sems.at[i]) for i, (f, near_f) in enumerate(pairs_of)]
        for copy in copies[:3]:
            copy.start()
        for copy in copies[:3]:
            copy.wait()
        for copy in copies[3:]:
            copy.start()
        first = lax.broadcasted_iota(jnp.int32, (SEQ, 128), 1) < HEAD_DIM
        cols = [slice(p * 128, (p + 1) * 128) for p in range(pairs)]

        def project(block):
            for part in range(3):
                c = slice(part * width, (part + 1) * width)
                value = mat_mul(x_ref[block, :], wq_ref[:, c])
                if part != 1:
                    value = value + row_of(bqv_ref, (part // 2) * width, width)
                proj_ref[block, c] = value.astype(low)

        def attend(base):
            for two in range(2):
                at = [slice(base + (2 * two + i) * SEQ, base + (2 * two + i + 1) * SEQ) for i in range(2)]
                probs = []
                for r in at:
                    q = proj_ref[r, :width]
                    k = proj_ref[r, width : 2 * width]
                    scores = (
                        jnp.concatenate([trans_right(k[:, c], split_heads(q[:, c], first)) for c in cols], axis=1) * scale
                    )
                    e = jnp.exp(scores - jnp.max(scores, axis=0, keepdims=True))
                    probs.append((e * (1.0 / jnp.sum(e, axis=0, keepdims=True))).astype(low))
                    prob_ref[r, :] = probs[-1]
                values = [proj_ref[r, 2 * width :] for r in at]
                for r, context in zip(at, heads_product(probs, values, cols, first)):
                    ctx_ref[r, :] = context.astype(low)

        def finish(block):
            h = x_ref[block, :].astype(wide) + mat_mul(ctx_ref[block, :], wo_ref[...]) + row_of(bo_ref)
            normed, inv = normalize(h)
            hidden = normed * row_of(g_ref) + row_of(b_ref)
            hid_ref[block, :] = hidden
            low_ref[block, :] = hidden.astype(low)
            inv_ref[block, :] = inv

        blocks = [slice(start, start + rows) for start in range(0, tokens, rows)]
        project(blocks[0])
        for copy in copies[3:7]:
            copy.wait()
        for i, block in enumerate(blocks):
            if i + 1 < len(blocks):
                project(blocks[i + 1])
            attend(block.start)
            if i:
                finish(blocks[i - 1])
        finish(blocks[-1])

        for copy in copies[7:]:
            copy.wait()

    return call(
        body,
        [x, w_qkv, b_qv, w_out, b_out, gain, bias] + later,
        [
            struct((tokens, 3 * width), low),
            struct((tokens, width), low),
            struct((tokens, width), low),
            struct((tokens, width), wide),
            struct((tokens, width), low),
            struct((tokens, 1), wide),
        ]
        + [struct(v.shape, v.dtype) for v in later],
        scratch=[pltpu.VMEM(v.shape, v.dtype) for v in (x, w_qkv, b_qv, w_out, b_out, gain, bias)]
        + [pltpu.SemaphoreType.DMA((7 + len(later),))],
        bits=bits,
        far=range(7 + len(later)),
        limit=14,
    )


def ffn_forward_rows(hidden, wi_ref, bi_ref, wd_ref, bd_ref, store_act, store_gate_in):
    h_low = hidden.astype(low)
    total = hidden + row_of(bd_ref)
    for c in range(0, wi_ref.shape[1], CHUNK):
        u = mat_mul(h_low, wi_ref[:, c : c + CHUNK]) + row_of(bi_ref, c, CHUNK)
        phi = 0.5 + 0.5 * lax.erf(u * root_half)
        act = (u * phi).astype(low)
        store_act(c, act)
        store_gate_in(c, u.astype(low), phi.astype(low))
        total = total + mat_mul(act, wd_ref[c : c + CHUNK, :])
    return normalize(total)


def ffn_backward_rows(grad_block, normed, inv, gain, wd_ref, gate_in, store_gate, small_ref, bin_ref):
    grad_two = norm_input_grad(grad_block * gain, normed, inv)
    small_ref[0:1, :] += jnp.sum(grad_block * normed, axis=0, keepdims=True)
    small_ref[1:2, :] += jnp.sum(grad_block, axis=0, keepdims=True)
    small_ref[2:3, :] += jnp.sum(grad_two, axis=0, keepdims=True)
    grad_low = grad_two.astype(low)
    for c in range(0, wd_ref.shape[0], CHUNK):
        u, phi = gate_in(c)
        slope = phi + u * jnp.exp(u * u * low(-0.5)) * low(gauss_norm)
        gate = trans_right(grad_low, wd_ref[c : c + CHUNK, :]) * slope.astype(wide)
        bin_ref[:, c : c + CHUNK] += jnp.sum(gate, axis=0, keepdims=True)
        store_gate(c, gate.astype(low))
    return grad_low


def ffn_group(index, hidden, cot, upper, state, after=()):
    w_in, b_in, w_down, b_down, gain, bias = upper
    sents, _, width = hidden.shape
    ffn = w_in.shape[1]
    rows = sents * GROUP
    at = slice(index * GROUP, (index + 1) * GROUP)
    first = index == 0
    second = index == 1

    def stores(act_ref, u_ref, phi_ref):
        def store_act(c, v):
            act_ref[:, at, c : c + CHUNK] = v.reshape(sents, GROUP, CHUNK)

        def store_gate_in(c, u, phi):
            u_ref[:, c : c + CHUNK] = u
            phi_ref[:, c : c + CHUNK] = phi

        return store_act, store_gate_in

    def forward(h_ref, wi_ref, bi_ref, wd_ref, bd_ref, act_ref, u_ref, phi_ref):
        return ffn_forward_rows(
            h_ref[:, at, :].reshape(rows, width), wi_ref, bi_ref, wd_ref, bd_ref, *stores(act_ref, u_ref, phi_ref)
        )

    def body_first(h_ref, wi_ref, bi_ref, wd_ref, bd_ref, g_ref, b_ref, enc_hbm, act_ref, u_ref, phi_ref, n_ref, inv_ref, first_ref, enc_ref, sem):
        normed, inv = forward(h_ref, wi_ref, bi_ref, wd_ref, bd_ref, act_ref, u_ref, phi_ref)
        n_ref[...] = normed
        inv_ref[...] = inv
        block = (normed * row_of(g_ref) + row_of(b_ref)).reshape(sents, GROUP, width)
        enc_ref[...] = block.astype(low)
        copy = pltpu.make_async_copy(enc_ref, enc_hbm.at[:, pl.ds(index * GROUP, GROUP), :], sem)
        copy.start()
        first_ref[...] = block[:, 0, :].astype(low)
        copy.wait()

    enc_shape = struct((sents, SEQ, width), low)
    enc_scratch = [pltpu.VMEM((sents, GROUP, width), low), pltpu.SemaphoreType.DMA]
    act_shape = struct((sents, SEQ, ffn), low)
    if first:
        return call(
            body_first,
            [hidden, w_in, b_in, w_down, b_down, gain, bias],
            [
                enc_shape,
                act_shape,
                struct((rows, ffn), low),
                struct((rows, ffn), low),
                struct((rows, width), wide),
                struct((rows, 1), wide),
                struct((sents, width), low),
            ],
            scratch=enc_scratch,
            hand_out=[0],
        )

    def body(h_ref, cot_ref, wi_ref, bi_ref, wd_ref, bd_ref, g_ref, b_ref, *refs):
        refs = refs[2 if second else 4 :]
        if not second:
            sin_ref, bin_in_ref = refs[:2]
            refs = refs[2:]
        enc_hbm, act_ref, gate_ref, two_ref, small_ref, bin_ref, u_ref, phi_ref, enc_ref, sem = refs
        small_ref[...] = jnp.zeros_like(small_ref) if second else sin_ref[...]
        bin_ref[...] = jnp.zeros_like(bin_ref) if second else bin_in_ref[...]

        def store_gate(c, v):
            gate_ref[:, at, c : c + CHUNK] = v.reshape(sents, GROUP, CHUNK)

        normed, inv = forward(h_ref, wi_ref, bi_ref, wd_ref, bd_ref, act_ref, u_ref, phi_ref)
        gain_row = row_of(g_ref)
        enc_ref[...] = (normed * gain_row + row_of(b_ref)).astype(low).reshape(sents, GROUP, width)
        copy = pltpu.make_async_copy(enc_ref, enc_hbm.at[:, pl.ds(index * GROUP, GROUP), :], sem)
        copy.start()
        grad_block = cot_ref[:, at, :].reshape(rows, width).astype(wide)
        got = ffn_backward_rows(
            grad_block, normed, inv, gain_row, wd_ref, lambda c: (u_ref[:, c : c + CHUNK], phi_ref[:, c : c + CHUNK]),
            store_gate, small_ref, bin_ref,
        )
        two_ref[:, at, :] = got.reshape(sents, GROUP, width)
        copy.wait()

    aliases = {8: 0, 9: 1}
    if not second:
        aliases.update({10: 2, 11: 3})
    return call(
        body,
        [hidden, cot, w_in, b_in, w_down, b_down, gain, bias] + list(state),
        [enc_shape, act_shape, act_shape, enc_shape, struct((8, width), wide), struct((1, ffn), wide)],
        scratch=[pltpu.VMEM((rows, ffn), low)] * 2 + enc_scratch,
        aliases=aliases,
        after=after,
        far=[8],
        hand_out=[0],
    )


def ffn_first_back(cot, grad_first, normed, inv, gate_in, phi, gain, w_down, gate, two, small, bin_sum):
    sents, _, width = cot.shape
    ffn = w_down.shape[0]
    rows = sents * GROUP
    at = slice(0, GROUP)

    def body(cot_ref, first_ref, n_ref, inv_ref, u_ref, phi_ref, g_ref, wd_ref, sin_ref, bin_in_ref, _g, _t, gate_ref, two_ref, small_ref, bin_ref):
        small_ref[...] = sin_ref[...]
        bin_ref[...] = bin_in_ref[...]
        position = lax.broadcasted_iota(jnp.int32, (sents, GROUP, width), 1)
        at_first = jnp.broadcast_to(first_ref[...][:, None, :], (sents, GROUP, width))
        grad_block = cot_ref[:, at, :].astype(wide) + jnp.where(position == 0, at_first, 0.0)

        def store_gate(c, v):
            gate_ref[:, at, c : c + CHUNK] = v.reshape(sents, GROUP, CHUNK)

        got = ffn_backward_rows(
            grad_block.reshape(rows, width), n_ref[...], inv_ref[...], row_of(g_ref), wd_ref,
            lambda c: (u_ref[:, c : c + CHUNK], phi_ref[:, c : c + CHUNK]), store_gate, small_ref, bin_ref,
        )
        two_ref[:, at, :] = got.reshape(sents, GROUP, width)

    return call(
        body,
        [cot, grad_first, normed, inv, gate_in, phi, gain, w_down, small, bin_sum, gate, two],
        [struct((sents, SEQ, ffn), low), struct((sents, SEQ, width), low), struct((8, width), wide), struct((1, ffn), wide)],
        aliases={10: 0, 11: 1},
    )


def lower_backward(part, parts, two, gate, hidden, inv, proj, probs, w_in, w_out, gain, bias, before=None, after=()):
    tokens, width = hidden.shape
    ffn = w_in.shape[1]
    rows = 4 * SEQ
    steps = tokens // rows // parts
    pairs = width // (2 * HEAD_DIM)
    scale = 1.0 / math.sqrt(HEAD_DIM)
    fresh = before is None

    def body(two_ref, gate_ref, hid_ref, inv_ref, proj_ref, prob_ref, wi_ref, wo_ref, g_ref, b_ref, *refs):
        if not fresh:
            sin_ref, bin_ref = refs[2:4]
            refs = refs[4:]
        one_ref, gp_ref, small_ref, bqv_ref, ctx_ref = refs
        small_ref[...] = jnp.zeros_like(small_ref) if fresh else sin_ref[...]
        bqv_ref[...] = jnp.zeros_like(bqv_ref) if fresh else bin_ref[...]
        first = lax.broadcasted_iota(jnp.int32, (SEQ, 128), 1) < HEAD_DIM
        cols = [slice(p * 128, (p + 1) * 128) for p in range(pairs)]

        gain_row = row_of(g_ref)

        def first_norm(block, at):
            grad_hidden = two_ref[block, :].astype(wide) + trans_right(gate_ref[block, :], wi_ref[...])
            normed = (hid_ref[block, :] - row_of(b_ref)) * (1.0 / gain_row)
            small_ref[0:1, :] += jnp.sum(grad_hidden * normed, axis=0, keepdims=True)
            small_ref[1:2, :] += jnp.sum(grad_hidden, axis=0, keepdims=True)
            grad_one = norm_input_grad(grad_hidden * gain_row, normed, inv_ref[block, :])
            small_ref[2:3, :] += jnp.sum(grad_one, axis=0, keepdims=True)
            one_ref[block, :] = grad_one.astype(low)
            ctx_ref[at : at + rows, :] = trans_right(grad_one.astype(low), wo_ref[...]).astype(low)

        def attention(base, from_ctx):
            sum_q = jnp.zeros((1, width), wide)
            sum_v = jnp.zeros((1, width), wide)
            for two in range(2):
                at = [slice(base + (2 * two + i) * SEQ, base + (2 * two + i + 1) * SEQ) for i in range(2)]
                grads = []
                for i, r in enumerate(at):
                    q_all = proj_ref[r, :width]
                    v = proj_ref[r, 2 * width :]
                    start = from_ctx + (2 * two + i) * SEQ
                    d_all = ctx_ref[start : start + SEQ, :]
                    p_low = prob_ref[r, :]
                    q = [split_heads(q_all[:, c], first) for c in cols]
                    d = [split_heads(d_all[:, c], first) for c in cols]
                    p = p_low.astype(wide)
                    grad_p = jnp.concatenate([trans_right(v[:, c], dd) for c, dd in zip(cols, d)], axis=1)
                    grad_v = jnp.concatenate([mat_mul(p_low[:, c], dd) for c, dd in zip(cols, d)], axis=1)
                    gp = grad_p * p
                    grad_s = (gp - p * jnp.sum(gp, axis=0, keepdims=True)).astype(low)
                    grad_k = jnp.concatenate([mat_mul(grad_s[:, c], qq) for c, qq in zip(cols, q)], axis=1) * scale
                    sum_v += jnp.sum(grad_v, axis=0, keepdims=True)
                    gp_ref[r, width : 2 * width] = grad_k.astype(low)
                    gp_ref[r, 2 * width :] = grad_v.astype(low)
                    grads.append(grad_s)
                keys = [proj_ref[r, width : 2 * width] for r in at]
                for r, product in zip(at, heads_product(grads, keys, cols, first)):
                    grad_q = product * scale
                    sum_q += jnp.sum(grad_q, axis=0, keepdims=True)
                    gp_ref[r, :width] = grad_q.astype(low)
            bqv_ref[0:1, :] += sum_q
            bqv_ref[1:2, :] += sum_v

        base = part * steps * rows
        first_norm(slice(base, base + rows), 0)
        for i in range(steps):
            if i + 1 < steps:
                start = base + (i + 1) * rows
                first_norm(slice(start, start + rows), ((i + 1) % 2) * rows)
            attention(base + i * rows, (i % 2) * rows)

    return call(
        body,
        [two, gate, hidden, inv, proj, probs, w_in, w_out, gain, bias] + ([] if fresh else list(before)),
        [struct((tokens, width), low), struct((tokens, 3 * width), low), struct((8, width), wide), struct((8, width), wide)],
        scratch=[pltpu.VMEM((2 * rows, width), low)],
        aliases=None if fresh else {10: 0, 11: 1},
        after=after,
    )


def input_gradient(grad_proj, w_qkv, grad_one, after=()):
    tokens, width = grad_one.shape
    rows = tokens // 2

    def body(gp_ref, w_ref, one_ref, out_ref, token):
        token[...] = jnp.zeros_like(token)

        for start in range(0, tokens, rows):
            block = slice(start, start + rows)
            out_ref[block, :] = (one_ref[block, :].astype(wide) + trans_right(gp_ref[block, :], w_ref[...])).astype(low)

    return call(
        body, [grad_proj, w_qkv, grad_one], [struct((tokens, width), low), struct((8, 128), wide)], after=after, far_out=[0]
    )


def pooler_gradients(flat, id_row, w_pool, b_pool):
    total = flat.shape[0] // 2
    pooled = jnp.tanh(mat_mul(flat, w_pool) + b_pool)
    inv_len = lax.rsqrt(jnp.sum(pooled * pooled, axis=-1, keepdims=True) + epsilon)
    unit = pooled * inv_len
    embed = unit.astype(low)
    zero, one = embed[:total], embed[total:]
    square = (total, total)
    eye = (lax.broadcasted_iota(jnp.int32, square, 0) == lax.broadcasted_iota(jnp.int32, square, 1)).astype(wide)
    logits = score_scale * trans_right(zero, one) - margin_shift * eye
    id_column = jnp.sum(jnp.where(eye > 0, id_row, 0), axis=1, keepdims=True)
    masked = jnp.where(id_column == id_row, logits, -jnp.inf)

    def soft(axis):
        e = jnp.exp(masked - jnp.max(masked, axis=axis, keepdims=True))
        return (score_scale * (e / jnp.sum(e, axis=axis, keepdims=True) - eye)).astype(low)

    by_row, by_col = soft(1), soft(0)
    grad_embed = jnp.concatenate(
        [mat_mul(by_row, one) + mat_mul(by_col, one), trans_left(by_row, zero) + trans_left(by_col, zero)], axis=0
    )
    grad_pre = (
        inv_len * (grad_embed - unit * jnp.sum(unit * grad_embed, axis=-1, keepdims=True)) * (1.0 - pooled * pooled)
    )
    pre_low = grad_pre.astype(low)
    return pre_low, trans_left(flat, pre_low), jnp.sum(grad_pre, axis=0, keepdims=True)


def contrastive(own, got, bits, sents, ids, w_pool, b_pool, after):
    total, width = own.shape
    if total > 512:
        start = bits[CORE] * total + bits[PLACE] * sents
        flat = jnp.where(bits[CORE] == 0, jnp.concatenate([own, got]), jnp.concatenate([got, own]))
        pre_low, grad_w, grad_b = pooler_gradients(flat, ids.reshape(1, -1), w_pool, b_pool.reshape(1, -1))
        return trans_right(lax.dynamic_slice_in_dim(pre_low, start, sents), w_pool), grad_w, grad_b.reshape(-1)

    def body(b, own_ref, got_ref, ids_ref, w_ref, b_ref, first_ref, gw_ref, gb_ref, flat_ref, pre_ref):
        flat_ref[pl.ds(pl.multiple_of(b[CORE] * total, total), total), :] = own_ref[...]
        flat_ref[pl.ds(pl.multiple_of((1 - b[CORE]) * total, total), total), :] = got_ref[...]
        pre_low, grad_w, grad_b = pooler_gradients(flat_ref[...], row_of(ids_ref), w_ref[...], row_of(b_ref))
        pre_ref[...] = pre_low
        gw_ref[...] = grad_w
        gb_ref[...] = grad_b.reshape(-1)
        first_ref[...] = trans_right(pre_ref[pl.ds(pl.multiple_of(b[CORE] * total + b[PLACE] * sents, sents), sents), :], w_ref[...])

    return call(
        body,
        [own, got, ids, w_pool, b_pool],
        [struct((sents, width), wide), struct((width, width), wide), struct((width,), wide)],
        bits=bits,
        scratch=[pltpu.VMEM((2 * total, width), low)] * 2,
        after=after,
        far_out=[1, 2],
    )


def put_in_order(blocks, bits, low_bit, after):
    rows, width = blocks[0].shape

    def body(b, *refs):
        me = (b[PLACE] >> low_bit) & (len(blocks) - 1)
        for i, ref in enumerate(refs[:-1]):
            at = pl.multiple_of((me ^ i) * rows, rows)
            refs[-1][pl.ds(at, rows), :] = ref[...]

    return call(
        body, blocks, [struct((rows * len(blocks), width), low)], bits=bits, after=after, limit=8, cost=920
    )[0]


CORE, FIRST, SECOND, THIRD, PLACE = range(5)
SMALL = 16
MASKS = {FIRST: (1, 2), SECOND: (2, 1), THIRD: (4, 4)}


def exchange(a, masks):
    size = lax.axis_size("dp")
    pairs = [(core * size + i, core * size + (i ^ masks[core])) for core in range(2) for i in range(size)]
    return lax.ppermute(a, ("stream", "dp"), pairs)


def cross(a):
    return lax.ppermute(a, "stream", [(0, 1), (1, 0)])


class Sources:
    def __init__(self, products, small=()):
        self.products = products
        self.small = list(small)
        self.m = products[0][0].shape[1]
        self.n = sum(hi - lo for _, _, lo, hi in products)
        self.arrays = [a for left, right, _, _ in products for a in (left, right)]

    def pieces(self, refs):
        at = 0
        for i, (_, _, lo, hi) in enumerate(self.products):
            yield refs[2 * i], refs[2 * i + 1], lo, at, hi - lo
            at += hi - lo


def gradient_to_send(src, bits, after=()):
    m, n = src.m, src.n
    half = m // 2
    count = len(src.arrays)
    small = src.small

    def body(b, *refs):
        out = refs[count + len(small)]
        rows = pl.ds(pl.multiple_of((1 - b[CORE]) * half, 128), half)
        for a, g, lo, at, size in src.pieces(refs):
            out[:half, at : at + size] = trans_left(a[:, rows], g[:, lo : lo + size]).astype(low)
        if small:
            up, bin_sum, down, bqv = refs[count : count + 4]
            kept = refs[-1]
            width = up.shape[1]
            parts = [up[:3]] + [bin_sum[:, c : c + width] for c in range(0, bin_sum.shape[1], width)] + [down[:3], bqv[:2]]
            parts.append(jnp.zeros((SMALL - sum(p.shape[0] for p in parts), width), wide))
            kept[...] = jnp.concatenate(parts, axis=0).astype(low)
            out[half:, :] = jnp.zeros((SMALL, n), low)
            out[half:, :width] = kept[...]

    shapes = [struct((half + (SMALL if small else 0), n), low)]
    if small:
        shapes.append(struct((SMALL, small[0].shape[1]), low))
    return call(body, src.arrays + small, shapes, bits=bits, after=after)


def gradient_sum(src, bits, got, kept, bit, after=()):
    m, n = src.m, src.n
    half, quarter = m // 2, m // 4
    count = len(src.arrays)
    extra = SMALL if src.small else 0

    def body(b, *refs):
        got_ref, send, keep = refs[-3:]
        if extra:
            mine = refs[count]
            total = (mine[...].astype(wide) + got_ref[half:, : mine.shape[1]].astype(wide)).astype(low)
            for ref in (send, keep):
                ref[quarter:, :] = jnp.zeros((SMALL, n), low)
                ref[quarter:, : mine.shape[1]] = total
        rows = pl.ds(pl.multiple_of(b[CORE] * half, 128), half)
        for a, g, lo, at, size in src.pieces(refs):
            c = slice(at, at + size)
            value = (trans_left(a[:, rows], g[:, lo : lo + size]) + got_ref[:half, c].astype(wide)).astype(low)

            def put(kept_half, c=c, value=value):
                keep[:quarter, c] = value[kept_half * quarter : (kept_half + 1) * quarter]
                send[:quarter, c] = value[(1 - kept_half) * quarter : (2 - kept_half) * quarter]

            pl.when(b[bit] == 0)(functools.partial(put, 0))
            pl.when(b[bit] != 0)(functools.partial(put, 1))

    return call(
        body,
        src.arrays + ([kept] if extra else []) + [got],
        [struct((quarter + extra, n), low)] * 2,
        bits=bits,
        after=after,
    )


def whole_call(body, arrays, shapes, bits, after=(), **kwargs):
    return call(body, arrays, shapes, bits=bits, after=after, limit=8, cost=920, **kwargs)


def halve(mine, got, bit, extra, bits, after=()):
    rows, cols = (mine.shape[0] - extra) // 2, mine.shape[1]

    def body(b, m, g, send, keep):
        for which, out in ((1 - b[bit], send), (b[bit], keep)):
            at = pl.ds(pl.multiple_of(which * rows, rows), rows)
            out[:rows, :] = (m[at, :].astype(wide) + g[at, :].astype(wide)).astype(low)
        if extra:
            total = (m[2 * rows :, :].astype(wide) + g[2 * rows :, :].astype(wide)).astype(low)
            send[rows:, :] = total
            keep[rows:, :] = total

    return whole_call(body, [mine, got], [struct((rows + extra, cols), low)] * 2, bits, after)


def add_up(mine, got, bits, after=()):
    def body(b, m, g, out):
        out[...] = (m[...].astype(wide) + g[...].astype(wide)).astype(low)

    return whole_call(body, [mine, got], [struct(mine.shape, low)], bits, after)


def add_last(mine, got, lengths, width, bits, after=()):
    rows = mine.shape[0] - SMALL

    def body(b, m, g, *refs):
        *vectors, out = refs
        out[...] = (m[:rows, :].astype(wide) + g[:rows, :].astype(wide)).astype(low)
        total = (m[rows:, :width].astype(wide) + g[rows:, :width].astype(wide)).astype(low).astype(wide)
        at = 0
        for vector in vectors:
            for c in range(0, vector.shape[0], width):
                vector[pl.ds(c, width)] = total[at : at + 1].reshape(-1)
                at += 1

    shapes = [struct((v,), wide) for v in lengths] + [struct((rows, mine.shape[1]), low)]
    return whole_call(body, [mine, got], shapes, bits, after, far_out=range(len(lengths)))


def join(mine, got, bit, bits, after=()):
    rows, cols = mine.shape

    def body(b, m, g, out):
        out[pl.ds(pl.multiple_of(b[bit] * rows, rows), rows), :] = m[...]
        out[pl.ds(pl.multiple_of((1 - b[bit]) * rows, rows), rows), :] = g[...]

    return whole_call(body, [mine, got], [struct((2 * rows, cols), low)], bits, after)


def widen(sources, targets, before, bits, after=()):
    half = sources[0][0].shape[0]
    parts = 4
    tile = half // parts
    total = parts * len(sources)
    old = [(i, a) for i, a in enumerate(before) if a is not None]

    def body(b, *refs):
        given = refs[: len(sources)]
        refs = refs[len(sources) + len(old) :]
        n = len(targets)
        outs, token, bufs, sems = refs[:n], refs[n], refs[n + 1 : -1], refs[-1]
        token[...] = jnp.zeros_like(token)
        copies = []
        for k, (src, (_, which)) in enumerate(zip(given, sources)):
            start = (1 - b[CORE] if which else b[CORE]) * half
            for t in range(parts):
                at = 0
                for out, buf, (_, first, size) in zip(outs, bufs, targets):
                    slot = k * parts + t
                    buf[slot] = src[t * tile : (t + 1) * tile, at : at + size].astype(wide)
                    rows = pl.ds(pl.multiple_of(start + t * tile, tile), tile)
                    to = out.at[rows, pl.ds(first, size)]
                    copies.append(pltpu.make_async_copy(buf.at[slot], to, sems.at[len(copies)]))
                    copies[-1].start()
                    at += size
        for copy in copies:
            copy.wait()

    return call(
        body,
        [a for a, _ in sources] + [a for _, a in old],
        [struct(shape, wide) for shape, _, _ in targets] + [struct((8, 128), wide)],
        bits=bits,
        scratch=[pltpu.VMEM((total, tile, size), wide) for _, _, size in targets]
        + [pltpu.SemaphoreType.DMA((total * len(targets),))],
        aliases={1 * len(sources) + k: i for k, (i, _) in enumerate(old)},
        after=after,
        far=range(len(sources), len(sources) + len(old)),
        hand_out=range(len(targets)),
        limit=12,
        cost=920,
    )


class Reduction:
    def __init__(self, src, order, targets, outs, bits, clock, tail, lengths=()):
        self.src, self.order, self.targets, self.outs = src, order, targets, outs
        self.bits, self.clock, self.tail, self.lengths = bits, clock, tail, lengths
        self.extra = SMALL if src.small else 0

    def step(self, fn, *args):
        out = fn(*args, self.bits, after=self.clock.now())
        self.clock.set(out[-1])
        return out

    def core_send(self):
        send, *self.kept = self.step(gradient_to_send, self.src)
        self.got = cross(send)

    def core_sum(self):
        out = gradient_sum(
            self.src, self.bits, self.got, self.kept[0] if self.kept else None, self.order[0], after=self.clock.now()
        )
        self.clock.set(out[-1])
        self.v = out[1]
        self.got = exchange(out[0], MASKS[self.order[0]])

    def halve(self, i):
        send, self.v = self.step(halve, self.v, self.got, self.order[i], self.extra)
        self.got = exchange(send, MASKS[self.order[i]])

    def first_sum(self):
        self.halve(1)

    def second_sum(self):
        self.halve(2)

    def third_sum(self):
        for mask in self.tail:
            (self.v,) = self.step(add_up, self.v, self.got)
            self.got = exchange(self.v, (mask, mask))

    def last_sum(self):
        if self.extra:
            *self.sums, self.v = self.step(add_last, self.v, self.got, self.lengths, self.src.small[0].shape[1])
        else:
            (self.v,) = self.step(add_up, self.v, self.got)
        self.got = exchange(self.v, MASKS[self.order[2]])

    def join(self, i):
        (self.v,) = self.step(join, self.v, self.got, self.order[i])
        self.got = exchange(self.v, MASKS[self.order[i - 1]]) if i else cross(self.v)

    def third_back(self):
        self.join(2)

    def second_back(self):
        self.join(1)

    def first_back(self):
        self.join(0)

    def write(self, *sources):
        before = [self.outs.get(name) for name, *_ in self.targets]
        *arrays, _ = self.step(widen, sources, [t[1:] for t in self.targets], before)
        for (name, *_), array in zip(self.targets, arrays):
            self.outs[name] = array

    def finish_own(self):
        self.write((self.v, 0))

    def finish(self):
        self.write((self.got, 1))

    def finish_both(self):
        self.write((self.v, 0), (self.got, 1))


class Clock:
    def __init__(self, start):
        self.last = start

    def now(self):
        return (self.last,)

    def set(self, value):
        self.last = value


def shards(
    embedded, seq_cotangent, pair_ids, w_qkv, b_qv, w_out, b_out, ln1_gain, ln1_bias, w_in, b_in, w_down, b_down,
    ln2_gain, ln2_bias, w_pool, b_pool,
):
    x = embedded[0]
    tokens, width = x.shape
    sents = tokens // SEQ
    ffn = w_in.shape[1]
    dp = lax.axis_size("dp")
    stream, place_dp = lax.axis_index("stream"), lax.axis_index("dp")
    first, second = (place_dp >> stream) & 1, (place_dp >> (1 - stream)) & 1
    bits = jnp.stack([stream, first, second, (place_dp >> 2) & 1, place_dp]).astype(jnp.int32)
    later = [
        w_in, w_down, seq_cotangent[0], w_pool, b_in, b_down, ln2_gain, ln2_bias, b_pool, pair_ids
    ]
    proj, probs, context, hidden, hidden_low, inv_one, *later = attention_forward(
        bits, x, w_qkv, b_qv, w_out, b_out, ln1_gain, ln1_bias, later
    )
    w_in, w_down, cotangent, w_pool, b_in, b_down, ln2_gain, ln2_bias, b_pool, ids = later
    hid3 = hidden.reshape(sents, SEQ, width)
    cot3 = cotangent.reshape(sents, SEQ, width)
    upper = (w_in, b_in, w_down, b_down, ln2_gain, ln2_bias)
    enc, act, gate_in, phi, normed_two, inv_two, first_low = ffn_group(0, hid3, cot3, upper, ())
    masks = [1 << i for i in range(dp.bit_length() - 1)]
    state = [enc, act]
    gathered = first_low
    group = 1
    order = [inv_two]
    for low_bit in range(0, len(masks), 2):
        span = 4 if low_bit + 1 < len(masks) else 2
        blocks = [gathered] + [exchange(gathered, (i << low_bit,) * 2) for i in range(1, span)]
        if group < SEQ // GROUP:
            state = ffn_group(group, hid3, cot3, upper, state, after=order)
            group += 1
            order = [state[-1]]
        gathered = put_in_order(blocks, bits, low_bit, order)
        order = [gathered]
    other = cross(gathered)
    while group < SEQ // GROUP:
        state = ffn_group(group, hid3, cot3, upper, state, after=order)
        group += 1
        order = [state[-1]]
    enc, act, gate, two, small_up, bin_sum = state
    grad_first, grad_w_pool, grad_b_pool = contrastive(
        gathered, other, bits, sents, ids, w_pool, b_pool, order
    )
    gate, two, small_up, bin_sum = ffn_first_back(
        cot3, grad_first, normed_two, inv_two, gate_in, phi, ln2_gain, w_down, gate, two, small_up, bin_sum
    )
    clock = Clock(small_up)
    act, gate, two = (v.reshape(tokens, -1) for v in (act, gate, two))
    tail = masks[3:]
    outs = {}
    shape_of = {"down": (ffn, width), "into": (width, ffn), "qkv": (width, 3 * width), "out": (width, width)}

    def target(name, first, size):
        return name, shape_of[name], first, size

    plain, third_first = (FIRST, SECOND, THIRD), (THIRD, FIRST, SECOND)
    rest = (outs, bits, clock, tail)
    down = Reduction(Sources([(act, two, 0, width)]), plain, [target("down", 0, width)], *rest)
    into = Reduction(Sources([(hidden_low, gate, 0, ffn)]), third_first, [target("into", 0, ffn)], *rest)
    lower = (two, gate, hidden, inv_one, proj, probs, w_in, w_out, ln1_gain, ln1_bias)

    def lower_reductions(grad_one, grad_proj, small_low, bqv):
        edge, end = 2 * width, 3 * width
        lengths = (width, width, width, ffn, width, width, width, 2 * width)
        part_a = Sources([(x, grad_proj, 0, edge)], [small_up, bin_sum, small_low, bqv])
        part_b = Sources([(x, grad_proj, edge, end), (context, grad_one, 0, width)])
        return (
            Reduction(part_a, plain, [target("qkv", 0, edge)], *rest, lengths),
            Reduction(part_b, plain, [target("qkv", edge, end - edge), target("out", 0, width)], *rest),
        )

    into.core_send()
    down.core_send()
    into.core_sum()
    down.core_sum()
    state = lower_backward(0, 2, *lower, after=clock.now())
    clock.set(state[-1])
    state = lower_backward(1, 2, *lower, before=state, after=clock.now())
    grad_one, grad_proj, small_low, bqv = state
    clock.set(bqv)
    lower_a, lower_b = lower_reductions(grad_one, grad_proj, small_low, bqv)
    lower_a.core_send()
    down.first_sum()
    lower_a.core_sum()
    down.second_sum()
    into.first_sum()
    lower_b.core_send()
    down.third_sum()
    lower_a.first_sum()
    into.second_sum()
    lower_b.core_sum()
    lower_a.second_sum()
    into.third_sum()
    grad_input, token = input_gradient(grad_proj, w_qkv, grad_one, after=clock.now())
    clock.set(token)
    lower_b.first_sum()
    down.last_sum()
    lower_b.second_sum()
    lower_a.third_sum()
    into.last_sum()
    down.third_back()
    into.third_back()
    lower_b.third_sum()
    down.second_back()
    lower_a.last_sum()
    lower_b.last_sum()
    into.second_back()
    lower_a.third_back()
    lower_b.third_back()
    down.first_back()
    lower_a.second_back()
    lower_b.second_back()
    down.finish_both()
    lower_a.first_back()
    lower_a.finish_own()
    lower_a.finish()
    lower_b.first_back()
    into.first_back()
    lower_b.finish_both()
    into.finish_both()
    g_ln2_gain, g_ln2_bias, g_b_down, g_b_in, g_ln1_gain, g_ln1_bias, g_b_out, g_b_qv = lower_a.sums
    return (
        enc.reshape(1, tokens, width),
        grad_input[None],
        outs["qkv"],
        g_b_qv,
        outs["out"],
        g_b_out,
        g_ln1_gain,
        g_ln1_bias,
        outs["into"],
        g_b_in,
        outs["down"],
        g_b_down,
        g_ln2_gain,
        g_ln2_bias,
        grad_w_pool,
        grad_b_pool,
    )


def solution(mesh):
    sharded = P("stream", "dp", None)
    return jax.shard_map(
        shards,
        mesh=mesh,
        in_specs=(sharded, sharded) + (P(),) * 15,
        out_specs=(sharded, sharded) + (P(),) * 14,
        check_vma=False,
    )
```

```python
import functools
import math

import jax
import jax.numpy as jnp
from jax import lax
from jax.experimental import pallas as pl
from jax.experimental.pallas import tpu as pltpu
from jax.sharding import PartitionSpec as P

HEAD_DIM = 64
SEQ = 64
GROUP = 16
CHUNK = 1536

epsilon = 1e-06
score_scale = 10.0
margin_shift = score_scale * 0.3
root_half = 0.7071067811865476
gauss_norm = 0.3989422804014327

low = jnp.bfloat16
wide = jnp.float32
ANY = pl.BlockSpec(memory_space=pl.ANY)
VMEM = pl.BlockSpec(memory_space=pltpu.VMEM)
SMEM = pl.BlockSpec(memory_space=pltpu.SMEM)
HBM = pl.BlockSpec(memory_space=pltpu.HBM)
MIB = 1 << 20


def struct(shape, dtype):
    return jax.ShapeDtypeStruct(shape, dtype)


def call(body, ins, outs, bits=None, scratch=(), aliases=None, after=(), limit=10, far=(), far_out=(), hand_out=(), cost=460):
    first = 0 if bits is None else 1
    ins = [pltpu.with_memory_space_constraint(a, pltpu.HBM) if i in far else a for i, a in enumerate(ins)]

    def wrapped(*refs):
        body(*refs[: first + len(ins)], *refs[first + len(ins) + len(after) :])

    return pl.pallas_call(
        wrapped,
        in_specs=[SMEM] * first + [HBM if i in far else VMEM for i in range(len(ins))] + [ANY] * len(after),
        out_specs=[HBM if i in hand_out else VMEM for i in range(len(outs))],
        out_shape=[(pltpu.HBM if i in far_out or i in hand_out else pltpu.VMEM)(o.shape, o.dtype) for i, o in enumerate(outs)],
        scratch_shapes=list(scratch),
        input_output_aliases={first + k: v for k, v in (aliases or {}).items()},
        cost_estimate=pl.CostEstimate(flops=int(cost * 1.5 * 10**7), bytes_accessed=0, transcendentals=0),
        compiler_params=pltpu.CompilerParams(vmem_limit_bytes=limit * MIB),
    )(*([] if bits is None else [bits]), *ins, *after)


def row_of(ref, start=0, size=None):
    return ref[pl.ds(start, ref.shape[0] if size is None else size)].reshape(1, -1)


def mat_mul(a, b):
    return jnp.dot(a, b, preferred_element_type=wide)


def trans_left(a, b):
    return lax.dot_general(a, b, (((0,), (0,)), ((), ())), preferred_element_type=wide)


def trans_right(a, b):
    return lax.dot_general(a, b, (((1,), (1,)), ((), ())), preferred_element_type=wide)


def normalize(h):
    center = h - jnp.mean(h, axis=-1, keepdims=True)
    inv = lax.rsqrt(jnp.mean(center * center, axis=-1, keepdims=True) + epsilon)
    return center * inv, inv


def norm_input_grad(grad, normed, inv):
    return inv * (
        grad
        - jnp.mean(grad, axis=-1, keepdims=True)
        - normed * jnp.mean(grad * normed, axis=-1, keepdims=True)
    )


def split_heads(pair, first):
    zero = jnp.zeros_like(pair)
    return jnp.concatenate([jnp.where(first, pair, zero), jnp.where(first, zero, pair)], axis=0)


def join_heads(rows, first):
    return jnp.where(first, rows[:SEQ], rows[SEQ:])


def heads_product(left, right, cols, first):
    zero = jnp.zeros_like(right[0][:, cols[0]])
    out = ([], [])
    for c in cols:
        both = jnp.concatenate([left[0][:, c], left[1][:, c]], axis=0)
        apart = jnp.concatenate(
            [jnp.concatenate([right[0][:, c], zero], axis=1), jnp.concatenate([zero, right[1][:, c]], axis=1)], axis=0
        )
        rows = trans_left(both, apart)
        for i in range(2):
            out[i].append(join_heads(rows[:, i * 128 : (i + 1) * 128], first))
    return [jnp.concatenate(o, axis=1) for o in out]


def attention_forward(bits, x, w_qkv, b_qv, w_out, b_out, gain, bias, later):
    tokens, width = x.shape
    rows = 4 * SEQ
    pairs = width // (2 * HEAD_DIM)
    scale = 1.0 / math.sqrt(HEAD_DIM)

    def body(_bits, *refs):
        n = len(later)
        far, far_later, outs, near_later, near, sems = (
            refs[:7], refs[7 : 7 + n], refs[7 + n : 13 + n], refs[13 + n : 13 + 2 * n], refs[13 + 2 * n : -1], refs[-1]
        )
        proj_ref, prob_ref, ctx_ref, hid_ref, low_ref, inv_ref = outs
        x_ref, wq_ref, bqv_ref, wo_ref, bo_ref, g_ref, b_ref = near
        pairs_of = zip(far + far_later, near + near_later)
        copies = [pltpu.make_async_copy(f, near_f, sems.at[i]) for i, (f, near_f) in enumerate(pairs_of)]
        for copy in copies[:3]:
            copy.start()
        for copy in copies[:3]:
            copy.wait()
        for copy in copies[3:]:
            copy.start()
        first = lax.broadcasted_iota(jnp.int32, (SEQ, 128), 1) < HEAD_DIM
        cols = [slice(p * 128, (p + 1) * 128) for p in range(pairs)]

        def project(block):
            for part in range(3):
                c = slice(part * width, (part + 1) * width)
                value = mat_mul(x_ref[block, :], wq_ref[:, c])
                if part != 1:
                    value = value + row_of(bqv_ref, (part // 2) * width, width)
                proj_ref[block, c] = value.astype(low)

        def attend(base):
            for two in range(2):
                at = [slice(base + (2 * two + i) * SEQ, base + (2 * two + i + 1) * SEQ) for i in range(2)]
                probs = []
                for r in at:
                    q = proj_ref[r, :width] * low(scale)
                    k = proj_ref[r, width : 2 * width]
                    scores = jnp.concatenate([trans_right(k[:, c], split_heads(q[:, c], first)) for c in cols], axis=1)
                    e = jnp.exp(scores - jnp.max(scores, axis=0, keepdims=True))
                    probs.append((e * (1.0 / jnp.sum(e, axis=0, keepdims=True))).astype(low))
                    prob_ref[r, :] = probs[-1]
                values = [proj_ref[r, 2 * width :] for r in at]
                for r, context in zip(at, heads_product(probs, values, cols, first)):
                    ctx_ref[r, :] = context.astype(low)

        def finish(block):
            h = x_ref[block, :].astype(wide) + mat_mul(ctx_ref[block, :], wo_ref[...]) + row_of(bo_ref)
            normed, inv = normalize(h)
            hidden = normed * row_of(g_ref) + row_of(b_ref)
            hid_ref[block, :] = hidden
            low_ref[block, :] = hidden.astype(low)
            inv_ref[block, :] = inv

        blocks = [slice(start, start + rows) for start in range(0, tokens, rows)]
        project(blocks[0])
        for copy in copies[3:7]:
            copy.wait()
        for i, block in enumerate(blocks):
            if i + 1 < len(blocks):
                project(blocks[i + 1])
            attend(block.start)
            if i:
                finish(blocks[i - 1])
        finish(blocks[-1])

        for copy in copies[7:]:
            copy.wait()

    return call(
        body,
        [x, w_qkv, b_qv, w_out, b_out, gain, bias] + later,
        [
            struct((tokens, 3 * width), low),
            struct((tokens, width), low),
            struct((tokens, width), low),
            struct((tokens, width), wide),
            struct((tokens, width), low),
            struct((tokens, 1), wide),
        ]
        + [struct(v.shape, v.dtype) for v in later],
        scratch=[pltpu.VMEM(v.shape, v.dtype) for v in (x, w_qkv, b_qv, w_out, b_out, gain, bias)]
        + [pltpu.SemaphoreType.DMA((7 + len(later),))],
        bits=bits,
        far=range(7 + len(later)),
        limit=14,
    )


def ffn_forward_rows(hidden, wi_ref, bi_ref, wd_ref, bd_ref, store_act, store_gate_in):
    h_low = hidden.astype(low)
    total = hidden + row_of(bd_ref)
    for c in range(0, wi_ref.shape[1], CHUNK):
        u = mat_mul(h_low, wi_ref[:, c : c + CHUNK]) + row_of(bi_ref, c, CHUNK)
        phi = 0.5 + 0.5 * lax.erf(u * root_half)
        act = (u * phi).astype(low)
        store_act(c, act)
        store_gate_in(c, u.astype(low), phi.astype(low))
        total = total + mat_mul(act, wd_ref[c : c + CHUNK, :])
    return normalize(total)


def ffn_backward_rows(grad_block, normed, inv, gain, wd_ref, gate_in, store_gate, small_ref, bin_ref):
    grad_two = norm_input_grad(grad_block * gain, normed, inv)
    small_ref[0:1, :] += jnp.sum(grad_block * normed, axis=0, keepdims=True)
    small_ref[1:2, :] += jnp.sum(grad_block, axis=0, keepdims=True)
    small_ref[2:3, :] += jnp.sum(grad_two, axis=0, keepdims=True)
    grad_low = grad_two.astype(low)
    for c in range(0, wd_ref.shape[0], CHUNK):
        u, phi = gate_in(c)
        slope = phi + u * jnp.exp(u * u * low(-0.5)) * low(gauss_norm)
        gate = trans_right(grad_low, wd_ref[c : c + CHUNK, :]) * slope.astype(wide)
        bin_ref[:, c : c + CHUNK] += jnp.sum(gate, axis=0, keepdims=True)
        store_gate(c, gate.astype(low))
    return grad_low


def ffn_group(index, hidden, cot, upper, state, after=()):
    w_in, b_in, w_down, b_down, gain, bias = upper
    sents, _, width = hidden.shape
    ffn = w_in.shape[1]
    rows = sents * GROUP
    at = slice(index * GROUP, (index + 1) * GROUP)
    first = index == 0
    second = index == 1

    def stores(act_ref, u_ref, phi_ref):
        def store_act(c, v):
            act_ref[:, at, c : c + CHUNK] = v.reshape(sents, GROUP, CHUNK)

        def store_gate_in(c, u, phi):
            u_ref[:, c : c + CHUNK] = u
            phi_ref[:, c : c + CHUNK] = phi

        return store_act, store_gate_in

    def forward(h_ref, wi_ref, bi_ref, wd_ref, bd_ref, act_ref, u_ref, phi_ref):
        return ffn_forward_rows(
            h_ref[:, at, :].reshape(rows, width), wi_ref, bi_ref, wd_ref, bd_ref, *stores(act_ref, u_ref, phi_ref)
        )

    def body_first(h_ref, wi_ref, bi_ref, wd_ref, bd_ref, g_ref, b_ref, enc_hbm, act_ref, u_ref, phi_ref, n_ref, inv_ref, first_ref, enc_ref, sem):
        normed, inv = forward(h_ref, wi_ref, bi_ref, wd_ref, bd_ref, act_ref, u_ref, phi_ref)
        n_ref[...] = normed
        inv_ref[...] = inv
        block = (normed * row_of(g_ref) + row_of(b_ref)).reshape(sents, GROUP, width)
        enc_ref[...] = block.astype(low)
        copy = pltpu.make_async_copy(enc_ref, enc_hbm.at[:, pl.ds(index * GROUP, GROUP), :], sem)
        copy.start()
        first_ref[...] = block[:, 0, :].astype(low)
        copy.wait()

    enc_shape = struct((sents, SEQ, width), low)
    enc_scratch = [pltpu.VMEM((sents, GROUP, width), low), pltpu.SemaphoreType.DMA]
    act_shape = struct((sents, SEQ, ffn), low)
    if first:
        return call(
            body_first,
            [hidden, w_in, b_in, w_down, b_down, gain, bias],
            [
                enc_shape,
                act_shape,
                struct((rows, ffn), low),
                struct((rows, ffn), low),
                struct((rows, width), wide),
                struct((rows, 1), wide),
                struct((sents, width), low),
            ],
            scratch=enc_scratch,
            hand_out=[0],
        )

    def body(h_ref, cot_ref, wi_ref, bi_ref, wd_ref, bd_ref, g_ref, b_ref, *refs):
        refs = refs[2 if second else 4 :]
        if not second:
            sin_ref, bin_in_ref = refs[:2]
            refs = refs[2:]
        enc_hbm, act_ref, gate_ref, two_ref, small_ref, bin_ref, u_ref, phi_ref, enc_ref, sem = refs
        small_ref[...] = jnp.zeros_like(small_ref) if second else sin_ref[...]
        bin_ref[...] = jnp.zeros_like(bin_ref) if second else bin_in_ref[...]

        def store_gate(c, v):
            gate_ref[:, at, c : c + CHUNK] = v.reshape(sents, GROUP, CHUNK)

        normed, inv = forward(h_ref, wi_ref, bi_ref, wd_ref, bd_ref, act_ref, u_ref, phi_ref)
        gain_row = row_of(g_ref)
        enc_ref[...] = (normed * gain_row + row_of(b_ref)).astype(low).reshape(sents, GROUP, width)
        copy = pltpu.make_async_copy(enc_ref, enc_hbm.at[:, pl.ds(index * GROUP, GROUP), :], sem)
        copy.start()
        grad_block = cot_ref[:, at, :].reshape(rows, width).astype(wide)
        got = ffn_backward_rows(
            grad_block, normed, inv, gain_row, wd_ref, lambda c: (u_ref[:, c : c + CHUNK], phi_ref[:, c : c + CHUNK]),
            store_gate, small_ref, bin_ref,
        )
        two_ref[:, at, :] = got.reshape(sents, GROUP, width)
        copy.wait()

    aliases = {8: 0, 9: 1}
    if not second:
        aliases.update({10: 2, 11: 3})
    return call(
        body,
        [hidden, cot, w_in, b_in, w_down, b_down, gain, bias] + list(state),
        [enc_shape, act_shape, act_shape, enc_shape, struct((8, width), wide), struct((1, ffn), wide)],
        scratch=[pltpu.VMEM((rows, ffn), low)] * 2 + enc_scratch,
        aliases=aliases,
        after=after,
        far=[8],
        hand_out=[0],
    )


def ffn_first_back(cot, grad_first, normed, inv, gate_in, phi, gain, w_down, gate, two, small, bin_sum):
    sents, _, width = cot.shape
    ffn = w_down.shape[0]
    rows = sents * GROUP
    at = slice(0, GROUP)

    def body(cot_ref, first_ref, n_ref, inv_ref, u_ref, phi_ref, g_ref, wd_ref, sin_ref, bin_in_ref, _g, _t, gate_ref, two_ref, small_ref, bin_ref):
        small_ref[...] = sin_ref[...]
        bin_ref[...] = bin_in_ref[...]
        position = lax.broadcasted_iota(jnp.int32, (sents, GROUP, width), 1)
        at_first = jnp.broadcast_to(first_ref[...][:, None, :], (sents, GROUP, width))
        grad_block = cot_ref[:, at, :].astype(wide) + jnp.where(position == 0, at_first, 0.0)

        def store_gate(c, v):
            gate_ref[:, at, c : c + CHUNK] = v.reshape(sents, GROUP, CHUNK)

        got = ffn_backward_rows(
            grad_block.reshape(rows, width), n_ref[...], inv_ref[...], row_of(g_ref), wd_ref,
            lambda c: (u_ref[:, c : c + CHUNK], phi_ref[:, c : c + CHUNK]), store_gate, small_ref, bin_ref,
        )
        two_ref[:, at, :] = got.reshape(sents, GROUP, width)

    return call(
        body,
        [cot, grad_first, normed, inv, gate_in, phi, gain, w_down, small, bin_sum, gate, two],
        [struct((sents, SEQ, ffn), low), struct((sents, SEQ, width), low), struct((8, width), wide), struct((1, ffn), wide)],
        aliases={10: 0, 11: 1},
    )


def lower_backward(part, parts, two, gate, hidden, inv, proj, probs, w_in, w_out, gain, bias, before=None, after=()):
    tokens, width = hidden.shape
    ffn = w_in.shape[1]
    rows = 4 * SEQ
    steps = tokens // rows // parts
    pairs = width // (2 * HEAD_DIM)
    scale = 1.0 / math.sqrt(HEAD_DIM)
    fresh = before is None

    def body(two_ref, gate_ref, hid_ref, inv_ref, proj_ref, prob_ref, wi_ref, wo_ref, g_ref, b_ref, *refs):
        if not fresh:
            sin_ref, bin_ref = refs[2:4]
            refs = refs[4:]
        one_ref, gp_ref, small_ref, bqv_ref, ctx_ref = refs
        small_ref[...] = jnp.zeros_like(small_ref) if fresh else sin_ref[...]
        bqv_ref[...] = jnp.zeros_like(bqv_ref) if fresh else bin_ref[...]
        first = lax.broadcasted_iota(jnp.int32, (SEQ, 128), 1) < HEAD_DIM
        cols = [slice(p * 128, (p + 1) * 128) for p in range(pairs)]

        gain_row = row_of(g_ref)

        def first_norm(block, at):
            grad_hidden = two_ref[block, :].astype(wide) + trans_right(gate_ref[block, :], wi_ref[...])
            normed = (hid_ref[block, :] - row_of(b_ref)) * (1.0 / gain_row)
            small_ref[0:1, :] += jnp.sum(grad_hidden * normed, axis=0, keepdims=True)
            small_ref[1:2, :] += jnp.sum(grad_hidden, axis=0, keepdims=True)
            grad_one = norm_input_grad(grad_hidden * gain_row, normed, inv_ref[block, :])
            small_ref[2:3, :] += jnp.sum(grad_one, axis=0, keepdims=True)
            one_ref[block, :] = grad_one.astype(low)
            ctx_ref[at : at + rows, :] = trans_right(grad_one.astype(low), wo_ref[...]).astype(low)

        def attention(base, from_ctx):
            sum_q = jnp.zeros((1, width), wide)
            sum_v = jnp.zeros((1, width), wide)
            for two in range(2):
                at = [slice(base + (2 * two + i) * SEQ, base + (2 * two + i + 1) * SEQ) for i in range(2)]
                grads = []
                for i, r in enumerate(at):
                    q_all = proj_ref[r, :width] * low(scale)
                    v = proj_ref[r, 2 * width :]
                    start = from_ctx + (2 * two + i) * SEQ
                    d_all = ctx_ref[start : start + SEQ, :]
                    p_low = prob_ref[r, :]
                    q = [split_heads(q_all[:, c], first) for c in cols]
                    d = [split_heads(d_all[:, c], first) for c in cols]
                    p = p_low.astype(wide)
                    grad_p = jnp.concatenate([trans_right(v[:, c], dd) for c, dd in zip(cols, d)], axis=1)
                    grad_v = jnp.concatenate([mat_mul(p_low[:, c], dd) for c, dd in zip(cols, d)], axis=1)
                    gp = grad_p * p
                    grad_s = (gp - p * jnp.sum(gp, axis=0, keepdims=True)).astype(low)
                    grad_k = jnp.concatenate([mat_mul(grad_s[:, c], qq) for c, qq in zip(cols, q)], axis=1)
                    sum_v += jnp.sum(grad_v, axis=0, keepdims=True)
                    gp_ref[r, width : 2 * width] = grad_k.astype(low)
                    gp_ref[r, 2 * width :] = grad_v.astype(low)
                    grads.append(grad_s)
                keys = [proj_ref[r, width : 2 * width] * low(scale) for r in at]
                for r, grad_q in zip(at, heads_product(grads, keys, cols, first)):
                    sum_q += jnp.sum(grad_q, axis=0, keepdims=True)
                    gp_ref[r, :width] = grad_q.astype(low)
            bqv_ref[0:1, :] += sum_q
            bqv_ref[1:2, :] += sum_v

        base = part * steps * rows
        first_norm(slice(base, base + rows), 0)
        for i in range(steps):
            if i + 1 < steps:
                start = base + (i + 1) * rows
                first_norm(slice(start, start + rows), ((i + 1) % 2) * rows)
            attention(base + i * rows, (i % 2) * rows)

    return call(
        body,
        [two, gate, hidden, inv, proj, probs, w_in, w_out, gain, bias] + ([] if fresh else list(before)),
        [struct((tokens, width), low), struct((tokens, 3 * width), low), struct((8, width), wide), struct((8, width), wide)],
        scratch=[pltpu.VMEM((2 * rows, width), low)],
        aliases=None if fresh else {10: 0, 11: 1},
        after=after,
    )


def input_gradient(grad_proj, w_qkv, grad_one, after=()):
    tokens, width = grad_one.shape
    rows = tokens // 2

    def body(gp_ref, w_ref, one_ref, out_ref, token):
        token[...] = jnp.zeros_like(token)

        for start in range(0, tokens, rows):
            block = slice(start, start + rows)
            out_ref[block, :] = (one_ref[block, :].astype(wide) + trans_right(gp_ref[block, :], w_ref[...])).astype(low)

    return call(
        body, [grad_proj, w_qkv, grad_one], [struct((tokens, width), low), struct((8, 128), wide)], after=after, far_out=[0]
    )


def pooler_gradients(flat, id_row, w_pool, b_pool):
    total = flat.shape[0] // 2
    pooled = jnp.tanh(mat_mul(flat, w_pool) + b_pool)
    inv_len = lax.rsqrt(jnp.sum(pooled * pooled, axis=-1, keepdims=True) + epsilon)
    unit = pooled * inv_len
    embed = unit.astype(low)
    zero, one = embed[:total], embed[total:]
    square = (total, total)
    eye = (lax.broadcasted_iota(jnp.int32, square, 0) == lax.broadcasted_iota(jnp.int32, square, 1)).astype(wide)
    logits = score_scale * trans_right(zero, one) - margin_shift * eye
    id_column = jnp.sum(jnp.where(eye > 0, id_row, 0), axis=1, keepdims=True)
    masked = jnp.where(id_column == id_row, logits, -jnp.inf)

    def soft(axis):
        e = jnp.exp(masked - jnp.max(masked, axis=axis, keepdims=True))
        return (score_scale * (e / jnp.sum(e, axis=axis, keepdims=True) - eye)).astype(low)

    both = (soft(1).astype(wide) + soft(0).astype(wide)).astype(low)
    grad_embed = jnp.concatenate([mat_mul(both, one), trans_left(both, zero)], axis=0)
    grad_pre = (
        inv_len * (grad_embed - unit * jnp.sum(unit * grad_embed, axis=-1, keepdims=True)) * (1.0 - pooled * pooled)
    )
    pre_low = grad_pre.astype(low)
    return pre_low, trans_left(flat, pre_low), jnp.sum(grad_pre, axis=0, keepdims=True)


def contrastive(own, got, bits, sents, ids, w_pool, b_pool, after):
    total, width = own.shape
    if total > 512:
        start = bits[CORE] * total + bits[PLACE] * sents
        flat = jnp.where(bits[CORE] == 0, jnp.concatenate([own, got]), jnp.concatenate([got, own]))
        pre_low, grad_w, grad_b = pooler_gradients(flat, ids.reshape(1, -1), w_pool, b_pool.reshape(1, -1))
        return trans_right(lax.dynamic_slice_in_dim(pre_low, start, sents), w_pool), grad_w, grad_b.reshape(-1)

    def body(b, own_ref, got_ref, ids_ref, w_ref, b_ref, first_ref, gw_ref, gb_ref, flat_ref, pre_ref):
        flat_ref[pl.ds(pl.multiple_of(b[CORE] * total, total), total), :] = own_ref[...]
        flat_ref[pl.ds(pl.multiple_of((1 - b[CORE]) * total, total), total), :] = got_ref[...]
        pre_low, grad_w, grad_b = pooler_gradients(flat_ref[...], row_of(ids_ref), w_ref[...], row_of(b_ref))
        pre_ref[...] = pre_low
        gw_ref[...] = grad_w
        gb_ref[...] = grad_b.reshape(-1)
        first_ref[...] = trans_right(pre_ref[pl.ds(pl.multiple_of(b[CORE] * total + b[PLACE] * sents, sents), sents), :], w_ref[...])

    return call(
        body,
        [own, got, ids, w_pool, b_pool],
        [struct((sents, width), wide), struct((width, width), wide), struct((width,), wide)],
        bits=bits,
        scratch=[pltpu.VMEM((2 * total, width), low)] * 2,
        after=after,
        far_out=[1, 2],
    )


def put_in_order(blocks, bits, low_bit, after):
    rows, width = blocks[0].shape

    def body(b, *refs):
        me = (b[PLACE] >> low_bit) & (len(blocks) - 1)
        for i, ref in enumerate(refs[:-1]):
            at = pl.multiple_of((me ^ i) * rows, rows)
            refs[-1][pl.ds(at, rows), :] = ref[...]

    return call(
        body, blocks, [struct((rows * len(blocks), width), low)], bits=bits, after=after, limit=8, cost=920
    )[0]


CORE, FIRST, SECOND, THIRD, PLACE = range(5)
SMALL = 16
MASKS = {FIRST: (1, 2), SECOND: (2, 1), THIRD: (4, 4)}


def exchange(a, masks):
    size = lax.axis_size("dp")
    pairs = [(core * size + i, core * size + (i ^ masks[core])) for core in range(2) for i in range(size)]
    return lax.ppermute(a, ("stream", "dp"), pairs)


def cross(a):
    return lax.ppermute(a, "stream", [(0, 1), (1, 0)])


class Sources:
    def __init__(self, products, small=()):
        self.products = products
        self.small = list(small)
        self.m = products[0][0].shape[1]
        self.n = sum(hi - lo for _, _, lo, hi in products)
        self.arrays = [a for left, right, _, _ in products for a in (left, right)]

    def pieces(self, refs):
        at = 0
        for i, (_, _, lo, hi) in enumerate(self.products):
            yield refs[2 * i], refs[2 * i + 1], lo, at, hi - lo
            at += hi - lo


def gradient_to_send(src, bits, after=()):
    m, n = src.m, src.n
    half = m // 2
    count = len(src.arrays)
    small = src.small

    def body(b, *refs):
        out = refs[count + len(small)]
        rows = pl.ds(pl.multiple_of((1 - b[CORE]) * half, 128), half)
        for a, g, lo, at, size in src.pieces(refs):
            out[:half, at : at + size] = trans_left(a[:, rows], g[:, lo : lo + size]).astype(low)
        if small:
            up, bin_sum, down, bqv = refs[count : count + 4]
            kept = refs[-1]
            width = up.shape[1]
            parts = [up[:3]] + [bin_sum[:, c : c + width] for c in range(0, bin_sum.shape[1], width)] + [down[:3], bqv[:2]]
            parts.append(jnp.zeros((SMALL - sum(p.shape[0] for p in parts), width), wide))
            kept[...] = jnp.concatenate(parts, axis=0).astype(low)
            out[half:, :] = jnp.zeros((SMALL, n), low)
            out[half:, :width] = kept[...]

    shapes = [struct((half + (SMALL if small else 0), n), low)]
    if small:
        shapes.append(struct((SMALL, small[0].shape[1]), low))
    return call(body, src.arrays + small, shapes, bits=bits, after=after)


def gradient_sum(src, bits, got, kept, bit, after=()):
    m, n = src.m, src.n
    half, quarter = m // 2, m // 4
    count = len(src.arrays)
    extra = SMALL if src.small else 0

    def body(b, *refs):
        got_ref, send, keep = refs[-3:]
        if extra:
            mine = refs[count]
            total = (mine[...].astype(wide) + got_ref[half:, : mine.shape[1]].astype(wide)).astype(low)
            for ref in (send, keep):
                ref[quarter:, :] = jnp.zeros((SMALL, n), low)
                ref[quarter:, : mine.shape[1]] = total
        rows = pl.ds(pl.multiple_of(b[CORE] * half, 128), half)
        for a, g, lo, at, size in src.pieces(refs):
            c = slice(at, at + size)
            value = (trans_left(a[:, rows], g[:, lo : lo + size]) + got_ref[:half, c].astype(wide)).astype(low)

            def put(kept_half, c=c, value=value):
                keep[:quarter, c] = value[kept_half * quarter : (kept_half + 1) * quarter]
                send[:quarter, c] = value[(1 - kept_half) * quarter : (2 - kept_half) * quarter]

            pl.when(b[bit] == 0)(functools.partial(put, 0))
            pl.when(b[bit] != 0)(functools.partial(put, 1))

    return call(
        body,
        src.arrays + ([kept] if extra else []) + [got],
        [struct((quarter + extra, n), low)] * 2,
        bits=bits,
        after=after,
    )


def whole_call(body, arrays, shapes, bits, after=(), **kwargs):
    return call(body, arrays, shapes, bits=bits, after=after, limit=8, cost=920, **kwargs)


def halve(mine, got, bit, extra, bits, after=()):
    rows, cols = (mine.shape[0] - extra) // 2, mine.shape[1]

    def body(b, m, g, send, keep):
        for which, out in ((1 - b[bit], send), (b[bit], keep)):
            at = pl.ds(pl.multiple_of(which * rows, rows), rows)
            out[:rows, :] = (m[at, :].astype(wide) + g[at, :].astype(wide)).astype(low)
        if extra:
            total = (m[2 * rows :, :].astype(wide) + g[2 * rows :, :].astype(wide)).astype(low)
            send[rows:, :] = total
            keep[rows:, :] = total

    return whole_call(body, [mine, got], [struct((rows + extra, cols), low)] * 2, bits, after)


def add_up(mine, got, bits, after=()):
    def body(b, m, g, out):
        out[...] = (m[...].astype(wide) + g[...].astype(wide)).astype(low)

    return whole_call(body, [mine, got], [struct(mine.shape, low)], bits, after)


def add_last(mine, got, lengths, width, bits, after=()):
    rows = mine.shape[0] - SMALL

    def body(b, m, g, *refs):
        *vectors, out = refs
        out[...] = (m[:rows, :].astype(wide) + g[:rows, :].astype(wide)).astype(low)
        total = (m[rows:, :width].astype(wide) + g[rows:, :width].astype(wide)).astype(low).astype(wide)
        at = 0
        for vector in vectors:
            for c in range(0, vector.shape[0], width):
                vector[pl.ds(c, width)] = total[at : at + 1].reshape(-1)
                at += 1

    shapes = [struct((v,), wide) for v in lengths] + [struct((rows, mine.shape[1]), low)]
    return whole_call(body, [mine, got], shapes, bits, after, far_out=range(len(lengths)))


def join(mine, got, bit, bits, after=()):
    rows, cols = mine.shape

    def body(b, m, g, out):
        out[pl.ds(pl.multiple_of(b[bit] * rows, rows), rows), :] = m[...]
        out[pl.ds(pl.multiple_of((1 - b[bit]) * rows, rows), rows), :] = g[...]

    return whole_call(body, [mine, got], [struct((2 * rows, cols), low)], bits, after)


def widen(sources, targets, before, bits, after=()):
    half = sources[0][0].shape[0]
    parts = 4
    tile = half // parts
    total = parts * len(sources)
    old = [(i, a) for i, a in enumerate(before) if a is not None]

    def body(b, *refs):
        given = refs[: len(sources)]
        refs = refs[len(sources) + len(old) :]
        n = len(targets)
        outs, token, bufs, sems = refs[:n], refs[n], refs[n + 1 : -1], refs[-1]
        token[...] = jnp.zeros_like(token)
        copies = []
        for k, (src, (_, which)) in enumerate(zip(given, sources)):
            start = (1 - b[CORE] if which else b[CORE]) * half
            for t in range(parts):
                at = 0
                for out, buf, (_, first, size) in zip(outs, bufs, targets):
                    slot = k * parts + t
                    buf[slot] = src[t * tile : (t + 1) * tile, at : at + size].astype(wide)
                    rows = pl.ds(pl.multiple_of(start + t * tile, tile), tile)
                    to = out.at[rows, pl.ds(first, size)]
                    copies.append(pltpu.make_async_copy(buf.at[slot], to, sems.at[len(copies)]))
                    copies[-1].start()
                    at += size
        for copy in copies:
            copy.wait()

    return call(
        body,
        [a for a, _ in sources] + [a for _, a in old],
        [struct(shape, wide) for shape, _, _ in targets] + [struct((8, 128), wide)],
        bits=bits,
        scratch=[pltpu.VMEM((total, tile, size), wide) for _, _, size in targets]
        + [pltpu.SemaphoreType.DMA((total * len(targets),))],
        aliases={1 * len(sources) + k: i for k, (i, _) in enumerate(old)},
        after=after,
        far=range(len(sources), len(sources) + len(old)),
        hand_out=range(len(targets)),
        limit=12,
        cost=920,
    )


class Reduction:
    def __init__(self, src, order, targets, outs, bits, clock, tail, lengths=()):
        self.src, self.order, self.targets, self.outs = src, order, targets, outs
        self.bits, self.clock, self.tail, self.lengths = bits, clock, tail, lengths
        self.extra = SMALL if src.small else 0

    def step(self, fn, *args):
        out = fn(*args, self.bits, after=self.clock.now())
        self.clock.set(out[-1])
        return out

    def core_send(self):
        send, *self.kept = self.step(gradient_to_send, self.src)
        self.got = cross(send)

    def core_sum(self):
        out = gradient_sum(
            self.src, self.bits, self.got, self.kept[0] if self.kept else None, self.order[0], after=self.clock.now()
        )
        self.clock.set(out[-1])
        self.v = out[1]
        self.got = exchange(out[0], MASKS[self.order[0]])

    def halve(self, i):
        send, self.v = self.step(halve, self.v, self.got, self.order[i], self.extra)
        self.got = exchange(send, MASKS[self.order[i]])

    def first_sum(self):
        self.halve(1)

    def second_sum(self):
        self.halve(2)

    def third_sum(self):
        for mask in self.tail:
            (self.v,) = self.step(add_up, self.v, self.got)
            self.got = exchange(self.v, (mask, mask))

    def last_sum(self):
        if self.extra:
            *self.sums, self.v = self.step(add_last, self.v, self.got, self.lengths, self.src.small[0].shape[1])
        else:
            (self.v,) = self.step(add_up, self.v, self.got)
        self.got = exchange(self.v, MASKS[self.order[2]])

    def join(self, i):
        (self.v,) = self.step(join, self.v, self.got, self.order[i])
        self.got = exchange(self.v, MASKS[self.order[i - 1]]) if i else cross(self.v)

    def third_back(self):
        self.join(2)

    def second_back(self):
        self.join(1)

    def first_back(self):
        self.join(0)

    def write(self, *sources):
        before = [self.outs.get(name) for name, *_ in self.targets]
        *arrays, _ = self.step(widen, sources, [t[1:] for t in self.targets], before)
        for (name, *_), array in zip(self.targets, arrays):
            self.outs[name] = array

    def finish_own(self):
        self.write((self.v, 0))

    def finish(self):
        self.write((self.got, 1))

    def finish_both(self):
        self.write((self.v, 0), (self.got, 1))


class Clock:
    def __init__(self, start):
        self.last = start

    def now(self):
        return (self.last,)

    def set(self, value):
        self.last = value


def shards(
    embedded, seq_cotangent, pair_ids, w_qkv, b_qv, w_out, b_out, ln1_gain, ln1_bias, w_in, b_in, w_down, b_down,
    ln2_gain, ln2_bias, w_pool, b_pool,
):
    x = embedded[0]
    tokens, width = x.shape
    sents = tokens // SEQ
    ffn = w_in.shape[1]
    dp = lax.axis_size("dp")
    stream, place_dp = lax.axis_index("stream"), lax.axis_index("dp")
    first, second = (place_dp >> stream) & 1, (place_dp >> (1 - stream)) & 1
    bits = jnp.stack([stream, first, second, (place_dp >> 2) & 1, place_dp]).astype(jnp.int32)
    later = [
        w_in, w_down, seq_cotangent[0], w_pool, b_in, b_down, ln2_gain, ln2_bias, b_pool, pair_ids
    ]
    proj, probs, context, hidden, hidden_low, inv_one, *later = attention_forward(
        bits, x, w_qkv, b_qv, w_out, b_out, ln1_gain, ln1_bias, later
    )
    w_in, w_down, cotangent, w_pool, b_in, b_down, ln2_gain, ln2_bias, b_pool, ids = later
    hid3 = hidden.reshape(sents, SEQ, width)
    cot3 = cotangent.reshape(sents, SEQ, width)
    upper = (w_in, b_in, w_down, b_down, ln2_gain, ln2_bias)
    enc, act, gate_in, phi, normed_two, inv_two, first_low = ffn_group(0, hid3, cot3, upper, ())
    masks = [1 << i for i in range(dp.bit_length() - 1)]
    state = [enc, act]
    gathered = first_low
    group = 1
    order = [inv_two]
    for low_bit in range(0, len(masks), 2):
        span = 4 if low_bit + 1 < len(masks) else 2
        blocks = [gathered] + [exchange(gathered, (i << low_bit,) * 2) for i in range(1, span)]
        if group < SEQ // GROUP:
            state = ffn_group(group, hid3, cot3, upper, state, after=order)
            group += 1
            order = [state[-1]]
        gathered = put_in_order(blocks, bits, low_bit, order)
        order = [gathered]
    other = cross(gathered)
    while group < SEQ // GROUP:
        state = ffn_group(group, hid3, cot3, upper, state, after=order)
        group += 1
        order = [state[-1]]
    enc, act, gate, two, small_up, bin_sum = state
    grad_first, grad_w_pool, grad_b_pool = contrastive(
        gathered, other, bits, sents, ids, w_pool, b_pool, order
    )
    gate, two, small_up, bin_sum = ffn_first_back(
        cot3, grad_first, normed_two, inv_two, gate_in, phi, ln2_gain, w_down, gate, two, small_up, bin_sum
    )
    clock = Clock(small_up)
    act, gate, two = (v.reshape(tokens, -1) for v in (act, gate, two))
    tail = masks[3:]
    outs = {}
    shape_of = {"down": (ffn, width), "into": (width, ffn), "qkv": (width, 3 * width), "out": (width, width)}

    def target(name, first, size):
        return name, shape_of[name], first, size

    plain, third_first = (FIRST, SECOND, THIRD), (THIRD, FIRST, SECOND)
    rest = (outs, bits, clock, tail)
    down = Reduction(Sources([(act, two, 0, width)]), plain, [target("down", 0, width)], *rest)
    into = Reduction(Sources([(hidden_low, gate, 0, ffn)]), third_first, [target("into", 0, ffn)], *rest)
    lower = (two, gate, hidden, inv_one, proj, probs, w_in, w_out, ln1_gain, ln1_bias)

    def lower_reductions(grad_one, grad_proj, small_low, bqv):
        edge, end = 2 * width, 3 * width
        lengths = (width, width, width, ffn, width, width, width, 2 * width)
        part_a = Sources([(x, grad_proj, 0, edge)], [small_up, bin_sum, small_low, bqv])
        part_b = Sources([(x, grad_proj, edge, end), (context, grad_one, 0, width)])
        return (
            Reduction(part_a, plain, [target("qkv", 0, edge)], *rest, lengths),
            Reduction(part_b, plain, [target("qkv", edge, end - edge), target("out", 0, width)], *rest),
        )

    into.core_send()
    down.core_send()
    into.core_sum()
    down.core_sum()
    state = lower_backward(0, 2, *lower, after=clock.now())
    clock.set(state[-1])
    state = lower_backward(1, 2, *lower, before=state, after=clock.now())
    grad_one, grad_proj, small_low, bqv = state
    clock.set(bqv)
    lower_a, lower_b = lower_reductions(grad_one, grad_proj, small_low, bqv)
    lower_a.core_send()
    down.first_sum()
    lower_a.core_sum()
    down.second_sum()
    into.first_sum()
    lower_b.core_send()
    down.third_sum()
    lower_a.first_sum()
    into.second_sum()
    lower_b.core_sum()
    lower_a.second_sum()
    into.third_sum()
    grad_input, token = input_gradient(grad_proj, w_qkv, grad_one, after=clock.now())
    clock.set(token)
    lower_b.first_sum()
    down.last_sum()
    lower_b.second_sum()
    lower_a.third_sum()
    into.last_sum()
    down.third_back()
    into.third_back()
    lower_b.third_sum()
    down.second_back()
    lower_a.last_sum()
    lower_b.last_sum()
    into.second_back()
    lower_a.third_back()
    lower_b.third_back()
    down.first_back()
    lower_a.second_back()
    lower_b.second_back()
    down.finish_both()
    lower_a.first_back()
    lower_a.finish_own()
    lower_a.finish()
    lower_b.first_back()
    into.first_back()
    lower_b.finish_both()
    into.finish_both()
    g_ln2_gain, g_ln2_bias, g_b_down, g_b_in, g_ln1_gain, g_ln1_bias, g_b_out, g_b_qv = lower_a.sums
    return (
        enc.reshape(1, tokens, width),
        grad_input[None],
        outs["qkv"],
        g_b_qv,
        outs["out"],
        g_b_out,
        g_ln1_gain,
        g_ln1_bias,
        outs["into"],
        g_b_in,
        outs["down"],
        g_b_down,
        g_ln2_gain,
        g_ln2_bias,
        grad_w_pool,
        grad_b_pool,
    )


def solution(mesh):
    sharded = P("stream", "dp", None)
    return jax.shard_map(
        shards,
        mesh=mesh,
        in_specs=(sharded, sharded) + (P(),) * 15,
        out_specs=(sharded, sharded) + (P(),) * 14,
        check_vma=False,
    )
```
